32 devices in a mesh: seq: 8 (over z, x), wt: 4 (over y, core).
Axes of the slice: x: 2, y: 2, z: 4, core: 2. Of those that a mesh axis runs over, the one named last changes fastest.
Arguments:
- block_in: bfloat16 [2, 4, 1024, 1536], P(None, 'wt', 'seq'), may hold values from -6 to 6
- start_flags: int32 [2, 4, 1024], P(None, 'wt', 'seq'), may hold values from 0 to 1, as said below
- out_grad: bfloat16 [2, 4, 1024, 1536], P(None, 'wt', 'seq'), may hold values from -6 to 6
- mix_gain: bfloat16 [2, 1536], P(None, ('seq', 'wt')), may hold values from 0.5 to 1.5
- proj_gelu: bfloat16 [2, 1536, 2048], P(None, ('seq', 'wt')), may hold values from -0.15625 to 0.15625
- proj_stream: bfloat16 [2, 1536, 2048], P(None, ('seq', 'wt')), may hold values from -0.15625 to 0.15625
- conv_taps: bfloat16 [2, 4, 2048], P(None, None, ('seq', 'wt')), may hold values from -3 to 3
- lru_gates: bfloat16 [2, 4096, 128], P(None, ('seq', 'wt')), may hold values from -0.5 to 0.5
- decay_param: bfloat16 [2, 2048], P(None, ('seq', 'wt')), may hold values from -11 to -5
- proj_out: bfloat16 [2, 2048, 1536], P(None, ('seq', 'wt')), may hold values from -0.25 to 0.25
- mlp_gain: bfloat16 [2, 1536], P(None, ('seq', 'wt')), may hold values from 0.5 to 1.5
- proj_gate: bfloat16 [2, 1536, 4608], P(None, ('seq', 'wt')), may hold values from -0.15625 to 0.15625
- proj_up: bfloat16 [2, 1536, 4608], P(None, ('seq', 'wt')), may hold values from -0.15625 to 0.15625
- proj_down: bfloat16 [2, 4608, 1536], P(None, ('seq', 'wt')), may hold values from -0.1875 to 0.1875
Outputs:
- block_out: bfloat16 [2, 4, 1024, 1536], P(None, 'wt', 'seq')
- grad_input: bfloat16 [2, 4, 1024, 1536], P(None, 'wt', 'seq')
- grad_mix_gain: float32 [2, 1536], P(None, ('seq', 'wt'))
- grad_proj_gelu: float32 [2, 1536, 2048], P(None, ('seq', 'wt'))
- grad_proj_stream: float32 [2, 1536, 2048], P(None, ('seq', 'wt'))
- grad_conv_taps: float32 [2, 4, 2048], P(None, None, ('seq', 'wt'))
- grad_lru_gates: float32 [2, 4096, 128], P(None, ('seq', 'wt'))
- grad_decay_param: float32 [2, 2048], P(None, ('seq', 'wt'))
- grad_proj_out: float32 [2, 2048, 1536], P(None, ('seq', 'wt'))
- grad_mlp_gain: float32 [2, 1536], P(None, ('seq', 'wt'))
- grad_proj_gate: float32 [2, 1536, 4608], P(None, ('seq', 'wt'))
- grad_proj_up: float32 [2, 1536, 4608], P(None, ('seq', 'wt'))
- grad_proj_down: float32 [2, 4608, 1536], P(None, ('seq', 'wt'))
The draws below stay inside these ranges and needn't reach their ends.
Inputs may be any that keep to these rules, and one draw needn't show every extreme that they name: `start_flags`: 1 where a sequence begins, 0 elsewhere; position 0 of every stream begins one.
All inputs are finite; a program needn't handle non-finite values.
Results may differ from the reference program's by a relative error of at most 0.033.
Values may be sent and summed in bfloat16 or wider, within the bound.
No kernel may reach another device: no remote copies, remote signals or barrier semaphores. Data moves between devices by JAX's collectives and lax.ppermute only.
A program may use at most 576 MiB of HBM per device.

```python
import jax
import jax.numpy as jnp
from jax import lax

D = 1536
R = 2048
HEAD_W = 128
FF = 4608
CONV = 4
LAYERS = 2
MB = 2
CH = 128
HEADS = 16
GROUPS = 4
STREAM = 1024


def draw_start_flags(key, part):
    key = jax.random.fold_in(key, 7)
    head_key, tail_key = jax.random.split(key)
    head_len = jax.random.randint(head_key, (MB, GROUPS, 1), 1, CH // 2 + 1)
    tail_len = jax.random.randint(tail_key, (MB, GROUPS, 1), 1, CH // 2 + 1)
    position = jnp.arange(STREAM, dtype=jnp.int32)[None, None, :]
    flags = (position == 0) | (position == head_len) | (position == STREAM - tail_len)
    return flags.astype(jnp.int32)


def shard_levels(own_key, extent, shards, smallest, high):
    level = 1.0
    for dim, blocks in shards:
        draws = jax.random.uniform(jax.random.fold_in(jax.random.fold_in(own_key, 6), dim), (blocks,), jnp.float32, smallest / len(shards), high / len(shards))
        level = level * jnp.repeat(jnp.exp(draws), extent[dim] // blocks).reshape((-1,) + (1,) * (len(extent) - 1 - dim))
    return level


def bell_draw(rng, shape, scale, most, cuts=(), held_as=jnp.bfloat16):
    entries = jax.random.normal(rng, shape, jnp.float32) * scale
    if len(cuts) > 0:
        entries = shard_levels(rng, shape, cuts, -0.22, 0.18) * entries
    return jnp.clip(entries, min=-most, max=most).astype(held_as)


def setup_inputs(seed: int = 0) -> dict:
    key_list = jax.random.split(jax.random.key(seed), 15)
    block_in = bell_draw(key_list[0], (MB, GROUPS, STREAM, D), 1.0, 6.0, ((1, 4), (2, 8)))
    start_flags = draw_start_flags(jax.random.fold_in(key_list[14], 71), 0)
    out_grad = bell_draw(key_list[2], (MB, GROUPS, STREAM, D), 1.0, 6.0, ((1, 4), (2, 8)))
    mix_gain = jnp.clip(1.0 + 0.1 * jax.random.normal(key_list[3], (LAYERS, D), jnp.float32), 0.5, 1.5).astype(jnp.bfloat16)
    proj_gelu = bell_draw(key_list[4], (LAYERS, D, R), D ** -0.5, 0.15625, ((1, 32),))
    proj_stream = bell_draw(key_list[5], (LAYERS, D, R), D ** -0.5, 0.15625, ((1, 32),))
    conv_taps = bell_draw(key_list[6], (LAYERS, CONV, R), CONV ** -0.5, 3.0, ((2, 32),))
    lru_gates = bell_draw(key_list[7], (LAYERS, 2 * R, HEAD_W), HEAD_W ** -0.5, 0.5, ((1, 32),))
    decay_param = jnp.clip(-11.0 + 6.0 * jax.random.uniform(key_list[8], (LAYERS, R), jnp.float32) ** shard_levels(key_list[8], (LAYERS, R), ((1, 32),), -0.2, 0.2), -11.0, -5.0).astype(jnp.bfloat16)
    proj_out = bell_draw(key_list[9], (LAYERS, R, D), (R // 4) ** -0.5, 0.25, ((1, 32),))
    mlp_gain = jnp.clip(1.0 + 0.1 * jax.random.normal(key_list[10], (LAYERS, D), jnp.float32), 0.5, 1.5).astype(jnp.bfloat16)
    proj_gate = bell_draw(key_list[11], (LAYERS, D, FF), D ** -0.5, 0.15625, ((1, 32),))
    proj_up = bell_draw(key_list[12], (LAYERS, D, FF), D ** -0.5, 0.15625, ((1, 32),))
    proj_down = bell_draw(key_list[13], (LAYERS, FF, D), (FF // 4) ** -0.5, 0.1875, ((1, 32),))
    return dict(block_in=block_in, start_flags=start_flags, out_grad=out_grad, mix_gain=mix_gain, proj_gelu=proj_gelu, proj_stream=proj_stream, conv_taps=conv_taps, lru_gates=lru_gates, decay_param=decay_param, proj_out=proj_out, mlp_gain=mlp_gain, proj_gate=proj_gate, proj_up=proj_up, proj_down=proj_down)


@jax.custom_vjp
def low(v):
    return lax.optimization_barrier(v.astype(jnp.bfloat16)).astype(jnp.float32)

@jax.custom_vjp
def low_back(v):
    return v

def low_keep(v):
    return (low(v), None)

def low_pass(kept, grad):
    return (grad,)

def back_keep(v):
    return (v, None)

def back_low(kept, grad):
    return (low(grad),)
low.defvjp(low_keep, low_pass)
low_back.defvjp(back_keep, back_low)
norm_eps = 1e-06
decay_scale = 8.0
highest = lax.Precision.HIGHEST

def matmul(left, right):
    return jnp.einsum('btk,kn->btn', left, right, precision=highest)

def rms_norm(values, gain_vec):
    return values * lax.rsqrt(lax.optimization_barrier(jnp.mean(values * values, axis=-1, keepdims=True)) + norm_eps) * gain_vec

def conv_mix(padded_rows, keep_rows, conv_weight):
    tap_count = conv_weight.shape[0]
    reach = tap_count - 1
    token_count = padded_rows.shape[1] - reach
    summed = conv_weight[0] * padded_rows[:, reach:reach + token_count]
    valid_mask = jnp.ones_like(keep_rows[:, reach:reach + token_count])
    for lag_index in range(1, tap_count):
        begin = reach - lag_index + 1
        valid_mask = valid_mask * keep_rows[:, begin:begin + token_count]
        lagged = padded_rows[:, reach - lag_index:reach - lag_index + token_count]
        summed = summed + conv_weight[lag_index] * lagged * valid_mask[..., None]
    return summed

def coefficients(conv_out, rate_pre, input_pre, decay_values, start_mask):
    keep_mask = (1.0 - start_mask)[..., None]
    log_decay = -decay_scale * jax.nn.softplus(decay_values) * jax.nn.sigmoid(rate_pre)
    decay_eff = jnp.exp(log_decay) * keep_mask
    scale_sq = keep_mask * -jnp.expm1(2.0 * log_decay) + start_mask[..., None]
    return (decay_eff, jnp.sqrt(scale_sq) * jax.nn.sigmoid(input_pre) * conv_out)

def layer_forward(values, start_mask, weights):
    mix_gain, proj_gelu, proj_stream, conv_taps, lru_gates, decay_param, proj_out, mlp_gain, proj_gate, proj_up, proj_down = weights
    normed = low(rms_norm(values, mix_gain))
    branch_pre = low_back(matmul(normed, proj_gelu))
    stream_in = low(low_back(matmul(normed, proj_stream)))
    reach = conv_taps.shape[0] - 1
    padded_rows = jnp.pad(stream_in, ((0, 0), (reach, 0), (0, 0)))
    keep_rows = jnp.pad(1.0 - start_mask, ((0, 0), (reach, 0)), constant_values=1.0)
    conv_out = low(conv_mix(padded_rows, keep_rows, conv_taps))
    batch_rows, token_count, lru_width = conv_out.shape
    gate_blocks = lru_gates.reshape(2, HEADS, HEAD_W, HEAD_W)
    pre_gates = jnp.einsum('btni,gnio->gbtno', conv_out.reshape(batch_rows, token_count, HEADS, HEAD_W), gate_blocks, precision=highest)
    rate_pre = low_back(pre_gates[0].reshape(batch_rows, token_count, lru_width))
    input_pre = low_back(pre_gates[1].reshape(batch_rows, token_count, lru_width))
    decay_eff, driven = coefficients(conv_out, rate_pre, input_pre, decay_param, start_mask)

    def advance(carried, step_in):
        carried = step_in[0] * carried + step_in[1]
        return (carried, carried)
    start_state = jnp.zeros((batch_rows, lru_width), jnp.float32)
    _, states = lax.scan(advance, start_state, (jnp.swapaxes(decay_eff, 0, 1), jnp.swapaxes(driven, 0, 1)))
    states = jnp.swapaxes(states, 0, 1)
    merged = low(states * jax.nn.gelu(branch_pre))
    hidden_res = values + low_back(matmul(merged, proj_out))
    mlp_in = low(rms_norm(hidden_res, mlp_gain))
    gate_pre = low_back(matmul(mlp_in, proj_gate))
    up_pre = low_back(matmul(mlp_in, proj_up))
    product = low(jax.nn.gelu(gate_pre) * up_pre)
    return hidden_res + low_back(matmul(product, proj_down))

def reference(block_in, start_flags, out_grad, mix_gain, proj_gelu, proj_stream, conv_taps, lru_gates, decay_param, proj_out, mlp_gain, proj_gate, proj_up, proj_down):
    batch_rows = MB * GROUPS
    inputs = block_in.astype(jnp.float32).reshape(batch_rows, STREAM, D)
    start_mask = start_flags.reshape(batch_rows, STREAM).astype(jnp.float32)
    params = (mix_gain.astype(jnp.float32), proj_gelu.astype(jnp.float32), proj_stream.astype(jnp.float32), conv_taps.astype(jnp.float32), lru_gates.astype(jnp.float32), decay_param.astype(jnp.float32), proj_out.astype(jnp.float32), mlp_gain.astype(jnp.float32), proj_gate.astype(jnp.float32), proj_up.astype(jnp.float32), proj_down.astype(jnp.float32))

    def forward(values, weights):
        for layer_index in range(LAYERS):
            values = layer_forward(values, start_mask, tuple((item[layer_index] for item in weights)))
        return values
    output, pullback = jax.vjp(forward, inputs, params)
    grad_values, grads = pullback(out_grad.astype(jnp.float32).reshape(batch_rows, STREAM, D))
    return (output.astype(jnp.bfloat16).reshape(block_in.shape), grad_values.astype(jnp.bfloat16).reshape(block_in.shape), grads[0], grads[1], grads[2], grads[3], grads[4], grads[5], grads[6], grads[7], grads[8], grads[9], grads[10])
```

```python
import functools

import jax
import jax.numpy as jnp
from jax import lax
from jax.experimental import pallas as pl
from jax.experimental.pallas import tpu as pltpu
from jax.sharding import PartitionSpec as P

f32 = jnp.float32
bf16 = jnp.bfloat16
HEAD_W = 128
CONV = 4
REACH = CONV - 1
TP = 4
EPS = 1e-06
DECAY = 8.0
GELU_C = 0.7978845608
GELU_K = 0.044715


def dot(left, right, out=f32):
    return lax.dot_general(left, right, (((1,), (0,)), ((), ())), preferred_element_type=f32).astype(out)


def dot_t(left, right, out=f32):
    return lax.dot_general(left, right, (((1,), (1,)), ((), ())), preferred_element_type=f32).astype(out)


def dot_tokens(left, right, out=bf16):
    return lax.dot_general(left, right, (((0,), (0,)), ((), ())), preferred_element_type=f32).astype(out)


def sigmoid(v):
    return 1.0 / (1.0 + jnp.exp(-v))


def gelu(v):
    return 0.5 * v * (1.0 + jnp.tanh(GELU_C * (v + GELU_K * v * v * v)))


def gelu_and_slope(v):
    square = v * v
    t = jnp.tanh(GELU_C * v * (1.0 + GELU_K * square))
    value = 0.5 * v * (1.0 + t)
    slope = 0.5 * (1.0 + t) + 0.5 * v * (1.0 - t * t) * GELU_C * (1.0 + 3.0 * GELU_K * square)
    return value, slope


def minus_expm1(y, e):
    series = -y * (1.0 + y * (1 / 2) * (1.0 + y * (1 / 3) * (1.0 + y * (1 / 4) * (1.0 + y * (1 / 5) * (1.0 + y * (1 / 6))))))
    return jnp.where(y > -0.25, series, 1.0 - e)


def rms_norm(v, gain):
    return v * lax.rsqrt(jnp.mean(v * v, axis=-1, keepdims=True) + EPS) * gain


def rms_norm_back(v, gain, dy):
    r = lax.rsqrt(jnp.mean(v * v, axis=-1, keepdims=True) + EPS)
    dgain = jnp.sum(dy * v * r, axis=0)
    dyg = dy * gain
    dv = r * dyg - v * (r * r * r) * jnp.mean(dyg * v, axis=-1, keepdims=True)
    return dv, dgain


def swap(x, k):
    return lax.ppermute(x, "wt", [(i, i ^ k) for i in range(TP)])


def tp_gather(x):
    far = swap(x, 2)
    near = swap(x, 1)
    diagonal = swap(far, 1)
    return jnp.concatenate([x, near, far, diagonal], axis=0)


def tp_scatter(part):
    far = (part[2].astype(f32) + swap(part[3], 1).astype(f32)).astype(bf16)
    across = swap(far, 2)
    near = swap(part[1], 1)
    return part[0].astype(f32) + near.astype(f32) + across.astype(f32)


def wt_exchange(pieces):
    w = lax.axis_index("wt")
    pick = lambda stack, j: lax.dynamic_index_in_dim(stack, j, 0, keepdims=False)
    got = [pick(pieces, w)] + [swap(pick(pieces, w ^ k), k) for k in range(1, TP)]
    stack = jnp.stack(got)
    return [pick(stack, w ^ j) for j in range(TP)]


def ring_tables():
    n = lax.axis_size("seq")
    order = [0, 1, 3, 5, 7, 6, 4, 2] if n == 8 else list(range(n))
    place = [0] * n
    for i, dev in enumerate(order):
        place[dev] = i
    right = [(order[i], order[(i + 1) % n]) for i in range(n)]
    left = [(b, a) for a, b in right]
    position = jnp.asarray(place, jnp.int32)[lax.axis_index("seq")]
    table = jnp.asarray(order, jnp.int32)
    device = lambda offset: table[lax.rem(position + offset + n, n)]
    return n, right, left, device


def ring_gather(block, flip, after=None):
    n, right, left, device = ring_tables()
    if flip:
        right, left = left, right
    sign = -1 if flip else 1
    if after is not None:
        block, _ = lax.optimization_barrier((block, after))
    out = jnp.zeros((n,) + block.shape, block.dtype)
    put = lambda o, b, k: lax.dynamic_update_index_in_dim(o, b, device(k), 0)
    out = put(out, block, 0)
    a = b = block
    marks = []
    for hop in range(1, n // 2 + 1):
        a = lax.ppermute(a, "seq", right)
        if hop <= n - 1 - n // 2:
            b = lax.ppermute(b, "seq", left)
            out = put(out, b, sign * hop)
        out = put(out, a, -sign * hop)
        marks.append(a)
    return out, marks


def ring_scatter(stack, flip):
    n, right, left, device = ring_tables()
    if flip:
        right, left = left, right
    sign = -1 if flip else 1
    chunk = lambda k: lax.dynamic_index_in_dim(stack, device(sign * k), 0, keepdims=False)
    add = lambda x, y: (x.astype(f32) + y.astype(f32)).astype(bf16)
    far, near = n // 2, n - 1 - n // 2
    a, b = chunk(far), chunk(-near)
    for hop in range(1, far + 1):
        a = lax.ppermute(a, "seq", right)
        if hop < far:
            a = add(a, chunk(far - hop))
        if hop <= near:
            b = lax.ppermute(b, "seq", left)
            if hop < near:
                b = add(b, chunk(hop - near))
    return chunk(0).astype(f32) + a.astype(f32) + b.astype(f32)


def shift_seq(x, distance):
    n = lax.axis_size("seq")
    return lax.ppermute(x, "seq", [(i, i + distance) for i in range(n) if 0 <= i + distance < n])


def carry_in(decay, state, direction):
    n = lax.axis_size("seq")
    width = decay.shape[-1]
    inclusive = jnp.concatenate([decay, state], axis=-1)

    def then(near, far):
        return jnp.concatenate(
            [near[:, :width] * far[:, :width], near[:, width:] + near[:, :width] * far[:, width:]], axis=-1
        )

    reach, covered, total = 1, 0, None
    while covered < n - 1:
        first = shift_seq(inclusive, direction * reach)
        second = shift_seq(inclusive, direction * 2 * reach) if covered + reach < n - 1 else None
        both = first if second is None else then(first, second)
        total = both if total is None else then(total, both)
        covered += 2 * reach if second is not None else reach
        inclusive = then(inclusive, both)
        reach *= 3
    return total[:, width:]


def head_route(rows):
    n = lax.axis_size("seq")
    per = HEAD_W // rows
    route = []
    for s in range(n):
        base = s // per * per
        for w in range(TP):
            b = TP * (s - base) + w
            route.append((s * TP + w, (base + b % per) * TP + b // per))
    return route


def to_heads(x):
    route = head_route(x.shape[0])
    return x if all(a == b for a, b in route) else lax.ppermute(x, ("seq", "wt"), route)


def from_heads(x):
    route = head_route(x.shape[0])
    return x if all(a == b for a, b in route) else lax.ppermute(x, ("seq", "wt"), [(b, a) for a, b in route])


def vector_scatter(v):
    w, s = lax.axis_index("wt"), lax.axis_index("seq")
    pick = lambda x, j, ax: lax.dynamic_index_in_dim(x, j, ax, keepdims=False)
    n, _, k = v.shape
    v = v.reshape(n, 2, 2, k)
    hi, lo = w >> 1, w & 1
    v = pick(v, hi, 1) + swap(pick(v, 1 - hi, 1), 2)
    v = pick(v, lo, 1) + swap(pick(v, 1 - lo, 1), 1)
    half = n // 2
    while half:
        v = v.reshape(2, half, k)
        bit = (s // half) % 2
        other = lax.ppermute(pick(v, 1 - bit, 0), "seq", [(i, i ^ half) for i in range(n)])
        v = pick(v, bit, 0) + other
        half //= 2
    return v.reshape(k)


def lay_stream(buf, src, streams, tokens, lead):
    for b in range(streams):
        buf[pl.ds(lead + b, tokens, stride=streams), :] = src[pl.ds(b * tokens, tokens), :].astype(f32)


def gate_values(pre_rows, decay_row, keep):
    sr = sigmoid(pre_rows[:, :HEAD_W])
    si = sigmoid(pre_rows[:, HEAD_W:])
    log_a = decay_row * sr
    raw = jnp.exp(log_a)
    e2 = raw * raw
    msq = keep * minus_expm1(2.0 * log_a, e2) + (1.0 - keep)
    return sr, si, raw, e2, jnp.sqrt(msq)


def mix_kernel(
    streams, tokens, stream_ref, halo_ref, keep_ref, taps_ref, decay_ref, gates_ref,
    a_ref, d_ref, conv_ref, ends_ref, buf, pre,
):
    lead = REACH * streams
    rows = streams * tokens
    step = 128
    buf[pl.ds(0, lead), :] = halo_ref[...]
    lay_stream(buf, stream_ref, streams, tokens, lead)
    taps = [taps_ref[pl.ds(k, 1), :] for k in range(CONV)]

    def conv_step(i, _):
        r = pl.multiple_of(i * step, step)
        total = taps[0] * buf[pl.ds(r + lead, step), :]
        valid = None
        for k in range(1, CONV):
            keep = keep_ref[pl.ds(r + lead - (k - 1) * streams, step), :]
            valid = keep if valid is None else valid * keep
            total = total + taps[k] * buf[pl.ds(r + lead - k * streams, step), :] * valid
        conv_ref[pl.ds(r, step), :] = total.astype(bf16)
        return 0

    lax.fori_loop(0, rows // step, conv_step, 0)
    pre[...] = jnp.dot(conv_ref[...], gates_ref[0], preferred_element_type=f32)

    def gate_step(i, _):
        r = pl.multiple_of(i * step, step)
        keep = keep_ref[pl.ds(r + lead, step), :]
        _, si, raw, _, m = gate_values(pre[pl.ds(r, step), :], decay_ref[...], keep)
        a_ref[pl.ds(r, step), :] = raw * keep
        d_ref[pl.ds(r, step), :] = m * si * conv_ref[pl.ds(r, step), :].astype(f32)
        return 0

    lax.fori_loop(0, rows // step, gate_step, 0)

    def scan_step(t, carry):
        total, h = carry
        r = pl.multiple_of(t * streams, streams)
        a = a_ref[pl.ds(r, streams), :]
        return total * a, a * h + d_ref[pl.ds(r, streams), :]

    total, h = lax.fori_loop(
        0, tokens, scan_step, (jnp.ones((streams, HEAD_W), f32), jnp.zeros((streams, HEAD_W), f32)), unroll=8
    )
    ends_ref[0] = total
    ends_ref[1] = h


def state_kernel(streams, tokens, a_ref, d_ref, start_ref, branch_ref, h_ref, merged_ref):
    def scan_step(t, h):
        r = pl.multiple_of(t * streams, streams)
        h = a_ref[pl.ds(r, streams), :] * h + d_ref[pl.ds(r, streams), :]
        h_ref[pl.ds(r, streams), :] = h
        return h

    lax.fori_loop(0, tokens, scan_step, start_ref[...], unroll=8)
    for b in range(streams):
        at = pl.ds(b * tokens, tokens)
        h = h_ref[pl.ds(b, tokens, stride=streams), :]
        merged_ref[at, :] = (h * gelu(branch_ref[at, :])).astype(bf16)


def state_back_kernel(streams, tokens, dm_ref, branch_ref, a_ref, h_ref, dh_ref, db_ref, ends_ref):
    for b in range(streams):
        at = pl.ds(b * tokens, tokens)
        dm = dm_ref[at, :]
        value, slope = gelu_and_slope(branch_ref[at, :])
        h = h_ref[pl.ds(b, tokens, stride=streams), :]
        dh_ref[pl.ds(b, tokens, stride=streams), :] = dm * value
        db_ref[at, :] = (dm * h * slope).astype(bf16)

    def scan_step(i, g):
        r = pl.multiple_of((tokens - 1 - i) * streams, streams)
        return a_ref[pl.ds(r, streams), :] * (dh_ref[pl.ds(r, streams), :] + g)

    ends_ref[...] = lax.fori_loop(0, tokens, scan_step, jnp.zeros((streams, HEAD_W), f32), unroll=8)


def mix_back_kernel(
    streams, tokens, dh_ref, a_ref, h_ref, start_ref, back_ref, conv_ref, stream_ref, halo_ref, keep_ref, taps_ref,
    decay_ref, slope_ref, gates_ref,
    ds_ref, tail_ref, head_ref, dgates_ref, dtaps_ref, ddecay_ref,
    buf, pre, back, dpre, dconv,
):
    lead = REACH * streams
    rows = streams * tokens
    step = 128
    buf[pl.ds(0, lead), :] = halo_ref[...]
    lay_stream(buf, stream_ref, streams, tokens, lead)
    pre[...] = jnp.dot(conv_ref[...], gates_ref[0], preferred_element_type=f32)

    def scan_step(i, g):
        r = pl.multiple_of((tokens - 1 - i) * streams, streams)
        total = dh_ref[pl.ds(r, streams), :] + g
        back[pl.ds(r, streams), :] = total
        return a_ref[pl.ds(r, streams), :] * total

    lax.fori_loop(0, tokens, scan_step, back_ref[...], unroll=8)
    dconv[pl.ds(rows, lead), :] = jnp.zeros((lead, HEAD_W), f32)

    def gate_step(i, acc):
        r = pl.multiple_of(i * step, step)
        keep = keep_ref[pl.ds(r + lead, step), :]
        decay = decay_ref[...]
        sr, si, raw, e2, m = gate_values(pre[pl.ds(r, step), :], decay, keep)
        g = back[pl.ds(r, step), :]
        conv = conv_ref[pl.ds(r, step), :].astype(f32)
        before = h_ref[pl.ds(jnp.maximum(r - streams, 0), step), :]
        shifted = jnp.concatenate([start_ref[...], before[: step - streams]], axis=0)
        previous = jnp.where(i == 0, shifted, before)
        gsi = g * si
        gm = gsi * m
        dconv[pl.ds(r, step), :] = gm
        d_input = gm * conv * (1.0 - si)
        d_log = g * previous * raw * keep - gsi * conv * keep * e2 / m
        by_rate = d_log * sr
        d_rate = by_rate * decay * (1.0 - sr)
        dpre[pl.ds(r, step), :] = jnp.concatenate([d_rate.astype(bf16), d_input.astype(bf16)], axis=1)
        return acc + jnp.sum(by_rate.reshape(step // 8, 8, HEAD_W), axis=0)

    acc = lax.fori_loop(0, rows // step, gate_step, jnp.zeros((8, HEAD_W), f32))
    ddecay_ref[...] = jnp.sum(acc, axis=0, keepdims=True) * slope_ref[...]
    dgates_ref[0] = lax.dot_general(conv_ref[...], dpre[...], (((0,), (0,)), ((), ())), preferred_element_type=f32)
    pre[:, :HEAD_W] = lax.dot_general(dpre[...], gates_ref[0], (((1,), (1,)), ((), ())), preferred_element_type=f32)
    taps = [taps_ref[pl.ds(k, 1), :] for k in range(CONV)]

    def add_step(i, accs):
        r = pl.multiple_of(i * step, step)
        dc = dconv[pl.ds(r, step), :] + pre[pl.ds(r, step), :HEAD_W]
        dconv[pl.ds(r, step), :] = dc
        out, valid = [], None
        for k in range(CONV):
            term = dc * buf[pl.ds(r + lead - k * streams, step), :]
            if k:
                keep = keep_ref[pl.ds(r + lead - (k - 1) * streams, step), :]
                valid = keep if valid is None else valid * keep
                term = term * valid
            out.append(accs[k] + jnp.sum(term.reshape(step // 8, 8, HEAD_W), axis=0))
        return tuple(out)

    accs = lax.fori_loop(0, rows // step, add_step, tuple(jnp.zeros((8, HEAD_W), f32) for _ in range(CONV)))
    for k in range(CONV):
        dtaps_ref[pl.ds(k, 1), :] = jnp.sum(accs[k], axis=0, keepdims=True)

    def stream_rows(r, count):
        total = taps[0] * dconv[pl.ds(r, count), :]
        valid = None
        for k in range(1, CONV):
            keep = keep_ref[pl.ds(r + lead + k * streams, count), :]
            valid = keep if valid is None else valid * keep
            total = total + taps[k] * dconv[pl.ds(r + k * streams, count), :] * valid
        return total

    def stream_step(i, _):
        r = pl.multiple_of(i * step, step)
        buf[pl.ds(r, step), :] = stream_rows(r, step)
        return 0

    lax.fori_loop(0, rows // step, stream_step, 0)
    tail_ref[...] = buf[pl.ds(rows - lead, lead), :]
    for b in range(streams):
        ds_ref[pl.ds(b * tokens, tokens), :] = buf[pl.ds(b, tokens, stride=streams), :].astype(bf16)
    for j in range(REACH):
        total = None
        valid = None
        for k in range(1, CONV):
            at = j + k - REACH
            keep = keep_ref[pl.ds((j + k) * streams, streams), :]
            valid = keep if valid is None else valid * keep
            if at >= 0:
                term = taps[k] * dconv[pl.ds(at * streams, streams), :] * valid
                total = term if total is None else total + term
        head_ref[pl.ds(j * streams, streams), :] = total


def by_head(rows):
    return pl.BlockSpec((rows, HEAD_W), lambda h: (0, h))


def whole(rows):
    return pl.BlockSpec((rows, HEAD_W), lambda h: (0, 0))


def params():
    return pltpu.CompilerParams(vmem_limit_bytes=40 * 2**20, dimension_semantics=("arbitrary",))


def mix(streams, stream, halo, keep, taps, decay, gates):
    rows, width = stream.shape
    tokens, heads, lead = rows // streams, width // HEAD_W, REACH * streams
    two = pl.BlockSpec((2, streams, HEAD_W), lambda h: (0, 0, h))
    shape = jax.ShapeDtypeStruct
    return pl.pallas_call(
        functools.partial(mix_kernel, streams, tokens),
        grid=(heads,),
        in_specs=[
            by_head(rows), by_head(lead), whole(keep.shape[0]), by_head(CONV), by_head(1),
            pl.BlockSpec((1, HEAD_W, 2 * HEAD_W), lambda h: (h, 0, 0)),
        ],
        out_specs=[by_head(rows), by_head(rows), by_head(rows), two],
        out_shape=[
            shape((rows, width), f32), shape((rows, width), f32), shape((rows, width), bf16), shape((2, streams, width), f32),
        ],
        scratch_shapes=[pltpu.VMEM((rows + lead, HEAD_W), f32), pltpu.VMEM((rows, 2 * HEAD_W), f32)],
        compiler_params=params(),
        cost_estimate=pl.CostEstimate(flops=rows * width * 600, bytes_accessed=rows * width * 12, transcendentals=rows * width * 6),
    )(stream, halo, keep, taps, decay, gates)


def states(streams, a, driven, start, branch):
    rows, width = a.shape
    tokens, heads = rows // streams, width // HEAD_W
    shape = jax.ShapeDtypeStruct
    return pl.pallas_call(
        functools.partial(state_kernel, streams, tokens),
        grid=(heads,),
        in_specs=[by_head(rows), by_head(rows), by_head(streams), by_head(rows)],
        out_specs=[by_head(rows), by_head(rows)],
        out_shape=[shape((rows, width), f32), shape((rows, width), bf16)],
        compiler_params=params(),
        cost_estimate=pl.CostEstimate(flops=rows * width * 30, bytes_accessed=rows * width * 18, transcendentals=rows * width),
    )(a, driven, start, branch)


def states_back(streams, d_merged, branch, a, h):
    rows, width = a.shape
    tokens, heads = rows // streams, width // HEAD_W
    shape = jax.ShapeDtypeStruct
    return pl.pallas_call(
        functools.partial(state_back_kernel, streams, tokens),
        grid=(heads,),
        in_specs=[by_head(rows)] * 4,
        out_specs=[by_head(rows), by_head(rows), by_head(streams)],
        out_shape=[shape((rows, width), f32), shape((rows, width), bf16), shape((streams, width), f32)],
        compiler_params=params(),
        cost_estimate=pl.CostEstimate(flops=rows * width * 40, bytes_accessed=rows * width * 22, transcendentals=rows * width),
    )(d_merged, branch, a, h)


def mix_back(streams, dh, a, h, start, back, conv, stream, halo, keep, taps, decay, slope, gates):
    rows, width = a.shape
    tokens, heads, lead = rows // streams, width // HEAD_W, REACH * streams
    shape = jax.ShapeDtypeStruct
    gate_spec = pl.BlockSpec((1, HEAD_W, 2 * HEAD_W), lambda h: (h, 0, 0))
    return pl.pallas_call(
        functools.partial(mix_back_kernel, streams, tokens),
        grid=(heads,),
        in_specs=[
            by_head(rows), by_head(rows), by_head(rows), by_head(streams), by_head(streams), by_head(rows), by_head(rows),
            by_head(lead), whole(keep.shape[0]), by_head(CONV), by_head(1), by_head(1), gate_spec,
        ],
        out_specs=[by_head(rows), by_head(lead), by_head(lead), gate_spec, by_head(CONV), by_head(1)],
        out_shape=[
            shape((rows, width), bf16), shape((lead, width), f32), shape((lead, width), f32),
            shape((heads, HEAD_W, 2 * HEAD_W), f32), shape((CONV, width), f32), shape((1, width), f32),
        ],
        scratch_shapes=[
            pltpu.VMEM((rows + lead, HEAD_W), f32), pltpu.VMEM((rows, 2 * HEAD_W), f32), pltpu.VMEM((rows, HEAD_W), f32),
            pltpu.VMEM((rows, 2 * HEAD_W), bf16), pltpu.VMEM((rows + lead, HEAD_W), f32),
        ],
        compiler_params=params(),
        cost_estimate=pl.CostEstimate(flops=rows * width * 1200, bytes_accessed=rows * width * 22, transcendentals=rows * width * 6),
    )(dh, a, h, start, back, conv, stream, halo, keep, taps, decay, slope, gates)


def head_columns(block):
    rows, width = block.shape
    groups = width // (TP * HEAD_W)
    return block.reshape(rows, groups, TP, HEAD_W).transpose(2, 0, 1, 3).reshape(TP, rows, width // TP)


def ff_columns(block):
    rows, width = block.shape
    n = lax.axis_size("seq")
    return block.reshape(rows, n, TP, width // (n * TP)).transpose(2, 0, 1, 3).reshape(TP, rows, width // TP)


def head_columns_back(pieces):
    groups = pieces[0].shape[1] // HEAD_W
    rows = pieces[0].shape[0]
    stack = jnp.stack([p.reshape(rows, groups, HEAD_W) for p in pieces], axis=2)
    return stack.reshape(rows, -1)


def ff_columns_back(pieces):
    n = lax.axis_size("seq")
    rows, width = pieces[0].shape
    stack = jnp.stack([p.reshape(rows, n, width // n) for p in pieces], axis=2)
    return stack.reshape(rows, -1)


def send_weights(shards, after):
    (mix_gain, proj_gelu, proj_stream, conv_taps, lru_gates, decay_param, proj_out, mlp_gain, proj_gate, proj_up, proj_down) = shards
    rp = proj_gelu.shape[0]
    gr = lru_gates.shape[0] // TP
    small = jnp.concatenate([mix_gain, mlp_gain, conv_taps.reshape(-1), decay_param])
    top = jnp.pad(small, (0, (rp - gr) * HEAD_W - small.shape[0])).reshape(rp - gr, HEAD_W)
    extra = jnp.concatenate([top, jnp.zeros((gr, HEAD_W), bf16)])
    pieces = jnp.concatenate(
        [head_columns(proj_gelu), head_columns(proj_stream), jnp.broadcast_to(extra, (TP, rp, HEAD_W))], axis=2
    )
    got = jnp.stack(wt_exchange(pieces))
    gates = to_heads(lru_gates).reshape(TP, gr, HEAD_W)
    width = got.shape[2] - HEAD_W
    got = lax.dynamic_update_slice(got, gates, (0, rp - gr, width))
    first, marks1 = ring_gather(got.reshape(TP * rp, width + HEAD_W), False, after)
    rows = jnp.concatenate([proj_down, to_heads(proj_out)])
    second, marks2 = ring_gather(rows, True, marks1[1])
    wide = jnp.concatenate([ff_columns(proj_gate), ff_columns(proj_up)], axis=2)
    wide = jnp.stack(wt_exchange(wide)).reshape(TP * rp, -1)
    third, marks3 = ring_gather(wide, False, marks2[1])
    return (first, second, third), marks3[1]


def open_weights(gathered, sizes):
    first, second, third = gathered
    rp, gr, cp, fb = sizes
    w = lax.axis_index("wt")
    n = first.shape[0]
    depth = n * TP * rp
    width = first.shape[2] - HEAD_W
    flat = first.reshape(depth, width + HEAD_W)
    extra = flat[:, width:].reshape(n * TP, rp, HEAD_W)
    small = extra[:, : rp - gr].reshape(n * TP, -1)
    mix_gain = small[:, :rp].reshape(-1).astype(f32)
    mlp_gain = small[:, rp : 2 * rp].reshape(-1).astype(f32)
    at = 2 * rp

    def own_heads(v):
        v = v.reshape(v.shape[0], -1, TP, HEAD_W)
        return lax.dynamic_index_in_dim(v, w, 2, keepdims=False).reshape(v.shape[0], -1).astype(f32)

    taps = own_heads(small[:, at : at + CONV * cp].reshape(n * TP, CONV, cp).transpose(1, 0, 2).reshape(CONV, -1))
    decay = own_heads(small[:, at + CONV * cp : at + (CONV + 1) * cp].reshape(1, -1))
    gates = extra[:, rp - gr :].reshape(2, -1, HEAD_W, HEAD_W).transpose(1, 2, 0, 3)
    gates = gates.reshape(-1, HEAD_W, 2 * HEAD_W)
    return dict(
        gelu=flat[:, : width // 2], stream=flat[:, width // 2 : width],
        mix_gain=mix_gain, mlp_gain=mlp_gain, taps=taps, gates=gates,
        decay=-DECAY * jax.nn.softplus(decay), slope=-DECAY * jax.nn.sigmoid(decay),
        down=second[:, :fb].reshape(n * fb, -1), out=second[:, fb:].reshape(-1, second.shape[2]),
        wide=third.reshape(depth, -1),
    )


def forward_block(x, keep, streams, wts):
    width = x.shape[1]
    normed = tp_gather(rms_norm(x, wts["mix_gain"]).astype(bf16))
    tokens = normed.shape[0] // streams
    last = normed.reshape(streams, tokens, width)[:, tokens - REACH :].transpose(1, 0, 2)
    halo_in = shift_seq(last.reshape(REACH * streams, width), 1)
    stream = dot(normed, wts["stream"], bf16)
    branch = dot(normed, wts["gelu"])
    halo = dot(halo_in, wts["stream"], bf16).astype(f32)
    a, driven, conv, ends = mix(streams, stream, halo, keep, wts["taps"], wts["decay"], wts["gates"])
    start = carry_in(ends[0], ends[1], 1)
    h, merged = states(streams, a, driven, start, branch)
    x1 = x + tp_scatter(dot(merged, wts["out"], bf16).reshape(TP, -1, width))
    mlp_in = tp_gather(rms_norm(x1, wts["mlp_gain"]).astype(bf16))
    wide = dot(mlp_in, wts["wide"])
    half = wide.shape[1] // 2
    product = (gelu(wide[:, :half]) * wide[:, half:]).astype(bf16)
    x2 = x1 + tp_scatter(dot(product, wts["down"], bf16).reshape(TP, -1, width))
    kept = dict(
        x=x, normed=normed, stream=stream, branch=branch, halo=halo, a=a, conv=conv, whole=ends[0], start=start, h=h,
        merged=merged, x1=x1, mlp_in=mlp_in, wide=wide, product=product,
    )
    return x2, kept


def mlp_back(gx, g_down, wts, kept):
    width = gx.shape[1]
    n = lax.axis_size("seq")
    grad_down = dot_tokens(kept["product"], g_down)
    d_product = dot_t(g_down, wts["down"])
    wide = kept["wide"]
    half = wide.shape[1] // 2
    value, slope = gelu_and_slope(wide[:, :half])
    d_wide = jnp.concatenate([(d_product * wide[:, half:] * slope).astype(bf16), (d_product * value).astype(bf16)], axis=1)
    grad_wide = dot_tokens(kept["mlp_in"], d_wide)
    d_mlp_in = tp_scatter(dot_t(d_wide, wts["wide"], bf16).reshape(TP, -1, width))
    dv, d_gain = rms_norm_back(kept["x1"], wts["mlp_gain"], d_mlp_in)
    down = ring_scatter(grad_down.reshape(n, -1, width), False)
    wide = ring_scatter(grad_wide.reshape(n, -1, grad_wide.shape[1]), True)
    return gx + dv, d_gain, down, wide


def mixer_back(d_x1, keep, streams, wts, kept, d_mlp_gain, d_mix_gain, sizes):
    rp, gr, cp, fb = sizes
    width = d_x1.shape[1]
    n, w = lax.axis_size("seq"), lax.axis_index("wt")
    g_branch = tp_gather(d_x1.astype(bf16))
    d_merged = dot_t(g_branch, wts["out"])
    grad_out = dot_tokens(kept["merged"], g_branch)
    dh, d_branch, ends = states_back(streams, d_merged, kept["branch"], kept["a"], kept["h"])
    back = carry_in(kept["whole"], ends, -1)
    d_stream, tail, head, d_gates, d_taps, d_decay = mix_back(
        streams, dh, kept["a"], kept["h"], kept["start"], back, kept["conv"], kept["stream"], kept["halo"], keep,
        wts["taps"], wts["decay"], wts["slope"], wts["gates"],
    )
    tail = (tail + shift_seq(head, -1)).astype(bf16)
    tokens = d_stream.shape[0] // streams
    d_stream = lax.dynamic_update_slice(
        d_stream.reshape(streams, tokens, -1), tail.reshape(REACH, streams, -1).transpose(1, 0, 2), (0, tokens - REACH, 0)
    ).reshape(d_stream.shape)
    both = jnp.concatenate([d_branch, d_stream], axis=1)
    grad_both = dot_tokens(kept["normed"], both)

    def full(v):
        lines = v.reshape(v.shape[0], -1, 1, HEAD_W)
        return jnp.where(lax.iota(jnp.int32, TP)[None, None, :, None] == w, lines, 0.0).reshape(v.shape[0], n * TP, -1)

    small = jnp.concatenate(
        [
            d_mix_gain.reshape(n * TP, rp), d_mlp_gain.reshape(n * TP, rp),
            full(d_taps).transpose(1, 0, 2).reshape(n * TP, -1), full(d_decay)[0],
        ],
        axis=1,
    ).astype(bf16)
    used = small.shape[1]
    small = jnp.pad(small, ((0, 0), (0, (rp - gr) * HEAD_W - used))).reshape(n * TP, rp - gr, HEAD_W)
    gates = d_gates.reshape(-1, HEAD_W, 2, HEAD_W).transpose(2, 0, 1, 3).reshape(n * TP, gr, HEAD_W).astype(bf16)
    extra = jnp.concatenate([small, gates], axis=1).reshape(n, TP * rp, HEAD_W)
    both_sum = ring_scatter(
        jnp.concatenate([grad_both.reshape(n, TP * rp, -1), extra], axis=2), False
    )
    out = from_heads(ring_scatter(grad_out.reshape(n, -1, width), True))
    d_normed = tp_scatter(
        (dot_t(d_branch, wts["gelu"]) + dot_t(d_stream, wts["stream"])).astype(bf16).reshape(TP, -1, width)
    )
    dv, d_gain = rms_norm_back(kept["x"], wts["mix_gain"], d_normed)
    return d_x1 + dv, d_gain, both_sum, out, used


def finish_wide(wide, rp):
    pieces = wt_exchange(wide.astype(bf16).reshape(TP, rp, -1))
    half = wide.shape[1] // 2
    return (
        ff_columns_back([p[:, :half] for p in pieces]).astype(f32),
        ff_columns_back([p[:, half:] for p in pieces]).astype(f32),
    )


def finish_both(both, sizes, used):
    rp, gr, cp, fb = sizes
    width = both.shape[1] - HEAD_W
    stack = both.reshape(TP, rp, -1)
    gates = from_heads(stack[:, rp - gr :, width:].reshape(TP * gr, HEAD_W))
    pieces = wt_exchange(both.astype(bf16).reshape(TP, rp, -1))
    half = width // 2
    gelu_part = head_columns_back([p[:, :half] for p in pieces]).astype(f32)
    stream_part = head_columns_back([p[:, half:width] for p in pieces]).astype(f32)
    small = sum(p[: rp - gr, width:].astype(f32) for p in pieces).reshape(-1)[:used]
    d_mix, d_mlp = small[:rp], small[rp : 2 * rp]
    d_taps = small[2 * rp : 2 * rp + CONV * cp].reshape(CONV, cp)
    d_decay = small[2 * rp + CONV * cp :]
    return gelu_part, stream_part, gates, d_mix, d_mlp, d_taps, d_decay


def per_device(block_in, start_flags, out_grad, *shards):
    layers = shards[0].shape[0]
    n = lax.axis_size("seq")
    micro, _, tokens, width = block_in.shape
    streams = micro * TP
    lead = REACH * streams
    sizes = (shards[1].shape[1], shards[4].shape[1] // TP, shards[5].shape[1], shards[10].shape[1])
    rp = sizes[0]

    gathered, mark = [], None
    for layer in range(layers):
        sent, mark = send_weights([s[layer] for s in shards], mark)
        gathered.append(sent)

    flags = tp_gather(start_flags[:, 0].astype(f32))
    keep = 1.0 - flags.T
    behind = 1.0 - shift_seq(flags[:, tokens - REACH :].T, 1)
    keep = jnp.concatenate([behind, keep, jnp.ones((REACH, streams), f32)]).reshape(-1, 1)
    keep = jnp.broadcast_to(keep, (keep.shape[0], HEAD_W))

    x = block_in[:, 0].astype(f32).reshape(micro * tokens, width)
    grad = out_grad[:, 0].reshape(micro * tokens, width)
    wts, kept = [], []
    for layer in range(layers):
        wts.append(open_weights(gathered[layer], sizes))
        x, saved = forward_block(x, keep, streams, wts[layer])
        kept.append(saved)

    gx = grad.astype(f32)
    d_mix = jnp.zeros((width,), f32)
    results = [None] * layers
    for layer in reversed(range(layers)):
        g_down = tp_gather(gx.astype(bf16))
        d_x1, d_mlp, down, wide = mlp_back(gx, g_down, wts[layer], kept[layer])
        gate_part, up_part = finish_wide(wide, rp)
        gx, d_mix_next, both, out, used = mixer_back(d_x1, keep, streams, wts[layer], kept[layer], d_mlp, d_mix, sizes)
        gelu_part, stream_part, gates, mix_part, mlp_part, taps, decay = finish_both(both, sizes, used)
        if layer != layers - 1:
            results[layer + 1][0] = mix_part
        results[layer] = [None, gelu_part, stream_part, taps, gates, decay, out, mlp_part, gate_part, up_part, down]
        d_mix = d_mix_next
    results[0][0] = vector_scatter(d_mix.reshape(n, TP, rp))
    shape = (micro, 1, tokens, width)
    stacked = [jnp.stack([results[layer][k] for layer in range(layers)]) for k in range(11)]
    return (x.astype(bf16).reshape(shape), gx.astype(bf16).reshape(shape), *stacked)


def solution(mesh):
    both = ("seq", "wt")
    tokens = P(None, "wt", "seq", None)
    vector, matrix = P(None, both), P(None, both, None)
    weights = (vector, matrix, matrix, P(None, None, both), matrix, vector, matrix, vector, matrix, matrix, matrix)
    return jax.shard_map(
        per_device,
        mesh=mesh,
        in_specs=(tokens, P(None, "wt", "seq"), tokens, *weights),
        out_specs=(tokens, tokens, *weights),
        check_vma=False,
    )
```

```python
import functools

import jax
import jax.numpy as jnp
from jax import lax
from jax.experimental import pallas as pl
from jax.experimental.pallas import tpu as pltpu
from jax.sharding import PartitionSpec as P

f32 = jnp.float32
bf16 = jnp.bfloat16
HEAD_W = 128
CONV = 4
REACH = CONV - 1
TP = 4
EPS = 1e-06
DECAY = 8.0
GELU_C = 0.7978845608
GELU_K = 0.044715


def dot(left, right, out=f32):
    return lax.dot_general(left, right, (((1,), (0,)), ((), ())), preferred_element_type=f32).astype(out)


def dot_t(left, right, out=f32):
    return lax.dot_general(left, right, (((1,), (1,)), ((), ())), preferred_element_type=f32).astype(out)


def dot_tokens(left, right, out=bf16):
    return lax.dot_general(left, right, (((0,), (0,)), ((), ())), preferred_element_type=f32).astype(out)


def sigmoid(v):
    return 1.0 / (1.0 + jnp.exp(-v))


def gelu(v):
    return 0.5 * v * (1.0 + jnp.tanh(GELU_C * (v + GELU_K * v * v * v)))


def gelu_and_slope(v):
    square = v * v
    t = jnp.tanh(GELU_C * v * (1.0 + GELU_K * square))
    value = 0.5 * v * (1.0 + t)
    slope = 0.5 * (1.0 + t) + 0.5 * v * (1.0 - t * t) * GELU_C * (1.0 + 3.0 * GELU_K * square)
    return value, slope


def minus_expm1(y, e):
    series = -y * (1.0 + y * (1 / 2) * (1.0 + y * (1 / 3) * (1.0 + y * (1 / 4) * (1.0 + y * (1 / 5) * (1.0 + y * (1 / 6))))))
    return jnp.where(y > -0.25, series, 1.0 - e)


def rms_norm(v, gain):
    return v * lax.rsqrt(jnp.mean(v * v, axis=-1, keepdims=True) + EPS) * gain


def rms_norm_back(v, gain, dy):
    r = lax.rsqrt(jnp.mean(v * v, axis=-1, keepdims=True) + EPS)
    dgain = jnp.sum(dy * v * r, axis=0)
    dyg = dy * gain
    dv = r * dyg - v * (r * r * r) * jnp.mean(dyg * v, axis=-1, keepdims=True)
    return dv, dgain


def swap(x, k):
    return lax.ppermute(x, "wt", [(i, i ^ k) for i in range(TP)])


def tp_gather(x):
    far = swap(x, 2)
    near = swap(x, 1)
    diagonal = swap(far, 1)
    return jnp.concatenate([x, near, far, diagonal], axis=0)


def tp_scatter(part):
    far = (part[2].astype(f32) + swap(part[3], 1).astype(f32)).astype(bf16)
    across = swap(far, 2)
    near = swap(part[1], 1)
    return part[0].astype(f32) + near.astype(f32) + across.astype(f32)


def wt_exchange(pieces):
    w = lax.axis_index("wt")
    pick = lambda stack, j: lax.dynamic_index_in_dim(stack, j, 0, keepdims=False)
    got = [pick(pieces, w)] + [swap(pick(pieces, w ^ k), k) for k in range(1, TP)]
    stack = jnp.stack(got)
    return [pick(stack, w ^ j) for j in range(TP)]


def ring_tables():
    n = lax.axis_size("seq")
    order = [0, 1, 3, 5, 7, 6, 4, 2] if n == 8 else list(range(n))
    right = [(order[i], order[(i + 1) % n]) for i in range(n)]
    left = [(b, a) for a, b in right]
    s = lax.axis_index("seq")
    if n == 8:
        position = jnp.where(s % 2 == 1, s // 2 + 1, (8 - s // 2) % 8)
        owner = lambda p: jnp.where(p == 0, 0, jnp.where(p <= 4, 2 * p - 1, 16 - 2 * p))
    else:
        position, owner = s, lambda p: p
    device = lambda offset: owner(lax.rem(position + offset + n, n))
    return n, right, left, device


class GatherJob:
    def __init__(self, block, flip, place):
        self.n, right, left, self.device = ring_tables()
        self.routes = (left, right) if flip else (right, left)
        self.sign = -1 if flip else 1
        self.a = self.b = block
        self.hop, self.place = 0, place
        self.place(block, self.device(0))
        self.done = False

    def start(self):
        self.hop += 1
        flight = [lax.ppermute(self.a, "seq", self.routes[0])]
        if self.hop <= self.n - 1 - self.n // 2:
            flight.append(lax.ppermute(self.b, "seq", self.routes[1]))
        return flight

    def bytes(self):
        return self.a.size * 2

    def receive(self, flight):
        self.a = flight[0]
        self.place(self.a, self.device(-self.sign * self.hop))
        if len(flight) > 1:
            self.b = flight[1]
            self.place(self.b, self.device(self.sign * self.hop))
        self.done = self.hop == self.n // 2


class ScatterJob:
    def __init__(self, stack, flip, finish):
        self.n, right, left, self.device = ring_tables()
        self.routes = (left, right) if flip else (right, left)
        self.sign = -1 if flip else 1
        self.stack, self.finish = stack, finish
        self.far, self.near = self.n // 2, self.n - 1 - self.n // 2
        self.a, self.b = self.chunk(self.far), self.chunk(-self.near)
        self.hop, self.done = 0, False

    def chunk(self, k):
        return lax.dynamic_index_in_dim(self.stack, self.device(self.sign * k), 0, keepdims=False)

    def bytes(self):
        return self.a.size * 2

    def start(self):
        self.hop += 1
        flight = [lax.ppermute(self.a, "seq", self.routes[0])]
        if self.hop <= self.near:
            flight.append(lax.ppermute(self.b, "seq", self.routes[1]))
        return flight

    def receive(self, flight):
        add = lambda x, y: (x.astype(f32) + y.astype(f32)).astype(bf16)
        self.a = flight[0]
        if self.hop < self.far:
            self.a = add(self.a, self.chunk(self.far - self.hop))
        if len(flight) > 1:
            self.b = flight[1]
            if self.hop < self.near:
                self.b = add(self.b, self.chunk(self.hop - self.near))
        if self.hop == self.far:
            self.done = True
            self.finish(self.chunk(0).astype(f32) + self.a.astype(f32) + self.b.astype(f32))


def tie(*values):
    return lax.optimization_barrier(values)


def run(job):
    while not job.done:
        job.receive(job.start())


class Pump:
    def __init__(self):
        self.waiting, self.active = [], []

    def add(self, *jobs):
        self.waiting += jobs

    def step(self, value):
        flights = [flight for _, flight in self.active]
        heads = [(job.a, job.b) for job in self.waiting]
        if flights or heads:
            value, flights, heads = lax.optimization_barrier((value, flights, heads))
        moved = []
        for (job, _), flight in zip(self.active, flights):
            job.receive(flight)
            if not job.done:
                moved.append(job)
        for job, (a, b) in zip(self.waiting, heads):
            job.a, job.b = a, b
            moved.append(job)
        self.waiting = []
        self.active = [(job, job.start()) for job in moved]
        return value

    def finish(self):
        for job, flight in self.active:
            job.receive(flight)
            run(job)
        for job in self.waiting:
            run(job)
        self.active, self.waiting = [], []


def shift_seq(x, distance):
    n = lax.axis_size("seq")
    return lax.ppermute(x, "seq", [(i, i + distance) for i in range(n) if 0 <= i + distance < n])


def carry_in(decay, state, direction):
    n = lax.axis_size("seq")
    width = decay.shape[-1]
    inclusive = jnp.concatenate([decay, state], axis=-1)

    def then(near, far):
        return jnp.concatenate(
            [near[:, :width] * far[:, :width], near[:, width:] + near[:, :width] * far[:, width:]], axis=-1
        )

    reach, covered, total = 1, 0, None
    while covered < n - 1:
        first = shift_seq(inclusive, direction * reach)
        second = shift_seq(inclusive, direction * 2 * reach) if covered + reach < n - 1 else None
        both = first if second is None else then(first, second)
        total = both if total is None else then(total, both)
        covered += 2 * reach if second is not None else reach
        inclusive = then(inclusive, both)
        reach *= 3
    return total[:, width:]


def head_route(rows):
    n = lax.axis_size("seq")
    per = HEAD_W // rows
    route = []
    for s in range(n):
        base = s // per * per
        for w in range(TP):
            b = TP * (s - base) + w
            route.append((s * TP + w, (base + b % per) * TP + b // per))
    return route


def to_heads(x):
    route = head_route(x.shape[0])
    return x if all(a == b for a, b in route) else lax.ppermute(x, ("seq", "wt"), route)


def from_heads(x):
    route = head_route(x.shape[0])
    return x if all(a == b for a, b in route) else lax.ppermute(x, ("seq", "wt"), [(b, a) for a, b in route])


def vector_scatter(v):
    w, s = lax.axis_index("wt"), lax.axis_index("seq")
    pick = lambda x, j, ax: lax.dynamic_index_in_dim(x, j, ax, keepdims=False)
    n, _, k = v.shape
    v = v.reshape(n, 2, 2, k)
    hi, lo = w >> 1, w & 1
    v = pick(v, hi, 1) + swap(pick(v, 1 - hi, 1), 2)
    v = pick(v, lo, 1) + swap(pick(v, 1 - lo, 1), 1)
    half = n // 2
    while half:
        v = v.reshape(2, half, k)
        bit = (s // half) % 2
        other = lax.ppermute(pick(v, 1 - bit, 0), "seq", [(i, i ^ half) for i in range(n)])
        v = pick(v, bit, 0) + other
        half //= 2
    return v.reshape(k)


def lay_stream(buf, src, streams, tokens, lead):
    for b in range(streams):
        buf[pl.ds(lead + b, tokens, stride=streams), :] = src[pl.ds(b * tokens, tokens), :].astype(f32)


def gate_values(pre_rows, decay_row, keep):
    sr = sigmoid(pre_rows[:, :HEAD_W])
    si = sigmoid(pre_rows[:, HEAD_W:])
    log_a = decay_row * sr
    raw = jnp.exp(log_a)
    e2 = raw * raw
    msq = keep * minus_expm1(2.0 * log_a, e2) + (1.0 - keep)
    return sr, si, raw, e2, jnp.sqrt(msq)


def mix_kernel(
    streams, tokens, stream_ref, halo_ref, keep_ref, taps_ref, decay_ref, gates_ref,
    a_ref, d_ref, conv_ref, ends_ref, buf, pre,
):
    lead = REACH * streams
    rows = streams * tokens
    step = 128
    buf[pl.ds(0, lead), :] = halo_ref[...]
    lay_stream(buf, stream_ref, streams, tokens, lead)
    taps = [taps_ref[pl.ds(k, 1), :] for k in range(CONV)]

    def conv_step(i, _):
        r = pl.multiple_of(i * step, step)
        total = taps[0] * buf[pl.ds(r + lead, step), :]
        valid = None
        for k in range(1, CONV):
            keep = keep_ref[pl.ds(r + lead - (k - 1) * streams, step), :]
            valid = keep if valid is None else valid * keep
            total = total + taps[k] * buf[pl.ds(r + lead - k * streams, step), :] * valid
        conv_ref[pl.ds(r, step), :] = total.astype(bf16)
        return 0

    lax.fori_loop(0, rows // step, conv_step, 0)
    pre[...] = jnp.dot(conv_ref[...], gates_ref[0], preferred_element_type=f32)

    def gate_step(i, _):
        r = pl.multiple_of(i * step, step)
        keep = keep_ref[pl.ds(r + lead, step), :]
        _, si, raw, _, m = gate_values(pre[pl.ds(r, step), :], decay_ref[...], keep)
        a_ref[pl.ds(r, step), :] = raw * keep
        d_ref[pl.ds(r, step), :] = m * si * conv_ref[pl.ds(r, step), :].astype(f32)
        return 0

    lax.fori_loop(0, rows // step, gate_step, 0)

    def scan_step(t, carry):
        total, h = carry
        r = pl.multiple_of(t * streams, streams)
        a = a_ref[pl.ds(r, streams), :]
        return total * a, a * h + d_ref[pl.ds(r, streams), :]

    total, h = lax.fori_loop(
        0, tokens, scan_step, (jnp.ones((streams, HEAD_W), f32), jnp.zeros((streams, HEAD_W), f32)), unroll=8
    )
    ends_ref[0] = total
    ends_ref[1] = h


def state_kernel(streams, tokens, a_ref, d_ref, start_ref, branch_ref, h_ref, merged_ref):
    def scan_step(t, h):
        r = pl.multiple_of(t * streams, streams)
        h = a_ref[pl.ds(r, streams), :] * h + d_ref[pl.ds(r, streams), :]
        h_ref[pl.ds(r, streams), :] = h
        return h

    lax.fori_loop(0, tokens, scan_step, start_ref[...], unroll=8)
    for b in range(streams):
        at = pl.ds(b * tokens, tokens)
        h = h_ref[pl.ds(b, tokens, stride=streams), :]
        merged_ref[at, :] = (h * gelu(branch_ref[at, :])).astype(bf16)


def state_back_kernel(streams, tokens, dm_ref, branch_ref, a_ref, h_ref, dh_ref, db_ref, ends_ref):
    for b in range(streams):
        at = pl.ds(b * tokens, tokens)
        dm = dm_ref[at, :]
        value, slope = gelu_and_slope(branch_ref[at, :])
        h = h_ref[pl.ds(b, tokens, stride=streams), :]
        dh_ref[pl.ds(b, tokens, stride=streams), :] = dm * value
        db_ref[at, :] = (dm * h * slope).astype(bf16)

    def scan_step(i, g):
        r = pl.multiple_of((tokens - 1 - i) * streams, streams)
        return a_ref[pl.ds(r, streams), :] * (dh_ref[pl.ds(r, streams), :] + g)

    ends_ref[...] = lax.fori_loop(0, tokens, scan_step, jnp.zeros((streams, HEAD_W), f32), unroll=8)


def mix_back_kernel(
    streams, tokens, dh_ref, a_ref, h_ref, start_ref, back_ref, conv_ref, stream_ref, halo_ref, keep_ref, taps_ref,
    decay_ref, slope_ref, gates_ref,
    ds_ref, tail_ref, head_ref, dgates_ref, dtaps_ref, ddecay_ref,
    buf, pre, back, dpre, dconv,
):
    lead = REACH * streams
    rows = streams * tokens
    step = 128
    buf[pl.ds(0, lead), :] = halo_ref[...]
    lay_stream(buf, stream_ref, streams, tokens, lead)
    pre[...] = jnp.dot(conv_ref[...], gates_ref[0], preferred_element_type=f32)

    def scan_step(i, g):
        r = pl.multiple_of((tokens - 1 - i) * streams, streams)
        total = dh_ref[pl.ds(r, streams), :] + g
        back[pl.ds(r, streams), :] = total
        return a_ref[pl.ds(r, streams), :] * total

    lax.fori_loop(0, tokens, scan_step, back_ref[...], unroll=8)
    dconv[pl.ds(rows, lead), :] = jnp.zeros((lead, HEAD_W), f32)

    def gate_step(i, acc):
        r = pl.multiple_of(i * step, step)
        keep = keep_ref[pl.ds(r + lead, step), :]
        decay = decay_ref[...]
        sr, si, raw, e2, m = gate_values(pre[pl.ds(r, step), :], decay, keep)
        g = back[pl.ds(r, step), :]
        conv = conv_ref[pl.ds(r, step), :].astype(f32)
        before = h_ref[pl.ds(jnp.maximum(r - streams, 0), step), :]
        shifted = jnp.concatenate([start_ref[...], before[: step - streams]], axis=0)
        previous = jnp.where(i == 0, shifted, before)
        gsi = g * si
        gm = gsi * m
        dconv[pl.ds(r, step), :] = gm
        d_input = gm * conv * (1.0 - si)
        d_log = g * previous * raw * keep - gsi * conv * keep * e2 / m
        by_rate = d_log * sr
        d_rate = by_rate * decay * (1.0 - sr)
        dpre[pl.ds(r, step), :] = jnp.concatenate([d_rate.astype(bf16), d_input.astype(bf16)], axis=1)
        return acc + jnp.sum(by_rate.reshape(step // 8, 8, HEAD_W), axis=0)

    acc = lax.fori_loop(0, rows // step, gate_step, jnp.zeros((8, HEAD_W), f32))
    ddecay_ref[...] = jnp.sum(acc, axis=0, keepdims=True) * slope_ref[...]
    dgates_ref[0] = lax.dot_general(conv_ref[...], dpre[...], (((0,), (0,)), ((), ())), preferred_element_type=f32)
    pre[:, :HEAD_W] = lax.dot_general(dpre[...], gates_ref[0], (((1,), (1,)), ((), ())), preferred_element_type=f32)
    taps = [taps_ref[pl.ds(k, 1), :] for k in range(CONV)]

    def add_step(i, accs):
        r = pl.multiple_of(i * step, step)
        dc = dconv[pl.ds(r, step), :] + pre[pl.ds(r, step), :HEAD_W]
        dconv[pl.ds(r, step), :] = dc
        out, valid = [], None
        for k in range(CONV):
            term = dc * buf[pl.ds(r + lead - k * streams, step), :]
            if k:
                keep = keep_ref[pl.ds(r + lead - (k - 1) * streams, step), :]
                valid = keep if valid is None else valid * keep
                term = term * valid
            out.append(accs[k] + jnp.sum(term.reshape(step // 8, 8, HEAD_W), axis=0))
        return tuple(out)

    accs = lax.fori_loop(0, rows // step, add_step, tuple(jnp.zeros((8, HEAD_W), f32) for _ in range(CONV)))
    for k in range(CONV):
        dtaps_ref[pl.ds(k, 1), :] = jnp.sum(accs[k], axis=0, keepdims=True)

    def stream_rows(r, count):
        total = taps[0] * dconv[pl.ds(r, count), :]
        valid = None
        for k in range(1, CONV):
            keep = keep_ref[pl.ds(r + lead + k * streams, count), :]
            valid = keep if valid is None else valid * keep
            total = total + taps[k] * dconv[pl.ds(r + k * streams, count), :] * valid
        return total

    def stream_step(i, _):
        r = pl.multiple_of(i * step, step)
        buf[pl.ds(r, step), :] = stream_rows(r, step)
        return 0

    lax.fori_loop(0, rows // step, stream_step, 0)
    tail_ref[...] = buf[pl.ds(rows - lead, lead), :]
    for b in range(streams):
        ds_ref[pl.ds(b * tokens, tokens), :] = buf[pl.ds(b, tokens, stride=streams), :].astype(bf16)
    for j in range(REACH):
        total = None
        valid = None
        for k in range(1, CONV):
            at = j + k - REACH
            keep = keep_ref[pl.ds((j + k) * streams, streams), :]
            valid = keep if valid is None else valid * keep
            if at >= 0:
                term = taps[k] * dconv[pl.ds(at * streams, streams), :] * valid
                total = term if total is None else total + term
        head_ref[pl.ds(j * streams, streams), :] = total


def by_head(rows):
    return pl.BlockSpec((rows, HEAD_W), lambda h: (0, h))


def whole(rows):
    return pl.BlockSpec((rows, HEAD_W), lambda h: (0, 0))


def params():
    return pltpu.CompilerParams(vmem_limit_bytes=40 * 2**20, dimension_semantics=("arbitrary",))


def mix(streams, stream, halo, keep, taps, decay, gates):
    rows, width = stream.shape
    tokens, heads, lead = rows // streams, width // HEAD_W, REACH * streams
    two = pl.BlockSpec((2, streams, HEAD_W), lambda h: (0, 0, h))
    shape = jax.ShapeDtypeStruct
    return pl.pallas_call(
        functools.partial(mix_kernel, streams, tokens),
        grid=(heads,),
        in_specs=[
            by_head(rows), by_head(lead), whole(keep.shape[0]), by_head(CONV), by_head(1),
            pl.BlockSpec((1, HEAD_W, 2 * HEAD_W), lambda h: (h, 0, 0)),
        ],
        out_specs=[by_head(rows), by_head(rows), by_head(rows), two],
        out_shape=[
            shape((rows, width), f32), shape((rows, width), f32), shape((rows, width), bf16), shape((2, streams, width), f32),
        ],
        scratch_shapes=[pltpu.VMEM((rows + lead, HEAD_W), f32), pltpu.VMEM((rows, 2 * HEAD_W), f32)],
        compiler_params=params(),
        cost_estimate=pl.CostEstimate(flops=rows * width * 600, bytes_accessed=rows * width * 12, transcendentals=rows * width * 6),
    )(stream, halo, keep, taps, decay, gates)


def states(streams, a, driven, start, branch):
    rows, width = a.shape
    tokens, heads = rows // streams, width // HEAD_W
    shape = jax.ShapeDtypeStruct
    return pl.pallas_call(
        functools.partial(state_kernel, streams, tokens),
        grid=(heads,),
        in_specs=[by_head(rows), by_head(rows), by_head(streams), by_head(rows)],
        out_specs=[by_head(rows), by_head(rows)],
        out_shape=[shape((rows, width), f32), shape((rows, width), bf16)],
        compiler_params=params(),
        cost_estimate=pl.CostEstimate(flops=rows * width * 30, bytes_accessed=rows * width * 18, transcendentals=rows * width),
    )(a, driven, start, branch)


def states_back(streams, d_merged, branch, a, h):
    rows, width = a.shape
    tokens, heads = rows // streams, width // HEAD_W
    shape = jax.ShapeDtypeStruct
    return pl.pallas_call(
        functools.partial(state_back_kernel, streams, tokens),
        grid=(heads,),
        in_specs=[by_head(rows)] * 4,
        out_specs=[by_head(rows), by_head(rows), by_head(streams)],
        out_shape=[shape((rows, width), f32), shape((rows, width), bf16), shape((streams, width), f32)],
        compiler_params=params(),
        cost_estimate=pl.CostEstimate(flops=rows * width * 40, bytes_accessed=rows * width * 22, transcendentals=rows * width),
    )(d_merged, branch, a, h)


def mix_back(streams, dh, a, h, start, back, conv, stream, halo, keep, taps, decay, slope, gates):
    rows, width = a.shape
    tokens, heads, lead = rows // streams, width // HEAD_W, REACH * streams
    shape = jax.ShapeDtypeStruct
    gate_spec = pl.BlockSpec((1, HEAD_W, 2 * HEAD_W), lambda h: (h, 0, 0))
    return pl.pallas_call(
        functools.partial(mix_back_kernel, streams, tokens),
        grid=(heads,),
        in_specs=[
            by_head(rows), by_head(rows), by_head(rows), by_head(streams), by_head(streams), by_head(rows), by_head(rows),
            by_head(lead), whole(keep.shape[0]), by_head(CONV), by_head(1), by_head(1), gate_spec,
        ],
        out_specs=[by_head(rows), by_head(lead), by_head(lead), gate_spec, by_head(CONV), by_head(1)],
        out_shape=[
            shape((rows, width), bf16), shape((lead, width), f32), shape((lead, width), f32),
            shape((heads, HEAD_W, 2 * HEAD_W), f32), shape((CONV, width), f32), shape((1, width), f32),
        ],
        scratch_shapes=[
            pltpu.VMEM((rows + lead, HEAD_W), f32), pltpu.VMEM((rows, 2 * HEAD_W), f32), pltpu.VMEM((rows, HEAD_W), f32),
            pltpu.VMEM((rows, 2 * HEAD_W), bf16), pltpu.VMEM((rows + lead, HEAD_W), f32),
        ],
        compiler_params=params(),
        cost_estimate=pl.CostEstimate(flops=rows * width * 1200, bytes_accessed=rows * width * 22, transcendentals=rows * width * 6),
    )(dh, a, h, start, back, conv, stream, halo, keep, taps, decay, slope, gates)


def head_columns(block):
    rows, width = block.shape
    groups = width // (TP * HEAD_W)
    return block.reshape(rows, groups, TP, HEAD_W).transpose(2, 0, 1, 3).reshape(TP, rows, width // TP)


def head_columns_back(pieces):
    groups = pieces[0].shape[1] // HEAD_W
    rows = pieces[0].shape[0]
    stack = jnp.stack([p.reshape(rows, groups, HEAD_W) for p in pieces], axis=2)
    return stack.reshape(rows, -1)


def ff_back_kernel(n, pieces_ref, gate_ref, up_ref):
    part = gate_ref.shape[1] // (n * TP)
    half = n * part
    for w in range(TP):
        for s in range(n):
            to = (s * TP + w) * part
            gate_ref[:, to : to + part] = pieces_ref[w, :, s * part : (s + 1) * part].astype(f32)
            up_ref[:, to : to + part] = pieces_ref[w, :, half + s * part : half + (s + 1) * part].astype(f32)


def ff_columns_back(pieces):
    n = lax.axis_size("seq")
    _, rows, width = pieces.shape
    out = jax.ShapeDtypeStruct((rows, TP * width // 2), f32)
    return pl.pallas_call(
        functools.partial(ff_back_kernel, n), out_shape=[out, out],
        compiler_params=pltpu.CompilerParams(vmem_limit_bytes=24 * 2**20),
        cost_estimate=pl.CostEstimate(flops=rows * width * 8, bytes_accessed=rows * width * 40, transcendentals=0),
    )(pieces)


def ff_kernel(n, gate_ref, up_ref, out_ref):
    part = gate_ref.shape[1] // (n * TP)
    half = n * part
    for w in range(TP):
        for s in range(n):
            at = (s * TP + w) * part
            out_ref[w, :, s * part : (s + 1) * part] = gate_ref[:, at : at + part]
            out_ref[w, :, half + s * part : half + (s + 1) * part] = up_ref[:, at : at + part]


def ff_columns(gate, up):
    rows, width = gate.shape
    return pl.pallas_call(
        functools.partial(ff_kernel, lax.axis_size("seq")),
        out_shape=jax.ShapeDtypeStruct((TP, rows, 2 * width // TP), bf16),
        compiler_params=pltpu.CompilerParams(vmem_limit_bytes=24 * 2**20),
        cost_estimate=pl.CostEstimate(flops=rows * width * 8, bytes_accessed=rows * width * 8, transcendentals=0),
    )(gate, up)


class Weights:
    def __init__(self, shards, layer):
        self.shards = [s[layer] for s in shards]
        self.buffers = {}
        self.flip = bool(layer % 2)

    def slot(self, name, shape):
        n = lax.axis_size("seq")
        if name not in self.buffers:
            self.buffers[name] = jnp.zeros((n,) + shape, bf16)

    def put(self, name, block, at, column=0):
        self.buffers[name] = lax.dynamic_update_slice(self.buffers[name], block[None], (at, 0, column))

    def prepare_first(self):
        (mix_gain, proj_gelu, proj_stream, conv_taps, lru_gates, decay_param, _, mlp_gain, _, _, _) = self.shards
        rp = proj_gelu.shape[0]
        gr = lru_gates.shape[0] // TP
        small = jnp.concatenate([mix_gain, mlp_gain, conv_taps.reshape(-1), decay_param])
        top = jnp.pad(small, (0, (rp - gr) * HEAD_W - small.shape[0])).reshape(rp - gr, HEAD_W)
        extra = jnp.concatenate([top, jnp.zeros((gr, HEAD_W), bf16)])
        pieces = jnp.concatenate(
            [head_columns(proj_gelu), head_columns(proj_stream), jnp.broadcast_to(extra, (TP, rp, HEAD_W))], axis=2
        )
        got = jnp.stack(wt_exchange(pieces))
        gates = to_heads(lru_gates).reshape(TP, gr, HEAD_W)
        width = got.shape[2] - HEAD_W
        self.first_block = lax.dynamic_update_slice(got, gates, (0, rp - gr, width)).reshape(TP * rp, width + HEAD_W)
        return self.first_block

    def prepare_out(self):
        self.out_block = to_heads(self.shards[6])

    def prepare_wide(self):
        proj_gate, proj_up = self.shards[8], self.shards[9]
        wide = jnp.stack(wt_exchange(ff_columns(proj_gate, proj_up)))
        self.wide_block = wide.reshape(TP * proj_gate.shape[0], -1)

    def first_job(self):
        self.slot("first", self.first_block.shape)
        return GatherJob(self.first_block, self.flip, lambda block, at: self.put("first", block, at))

    def out_job(self):
        self.slot("out", self.out_block.shape)
        return GatherJob(self.out_block, not self.flip, lambda block, at: self.put("out", block, at))

    def gather_down(self):
        self.down = lax.all_gather(self.shards[10], "seq", tiled=True)

    def gather_wide(self):
        self.wide = lax.all_gather(self.wide_block, "seq", tiled=True)

    def open_first(self, sizes):
        rp, gr, cp, fb = sizes
        first = self.buffers["first"]
        w = lax.axis_index("wt")
        n = first.shape[0]
        depth = n * TP * rp
        width = first.shape[2] - HEAD_W
        flat = first.reshape(depth, width + HEAD_W)
        extra = flat[:, width:].reshape(n * TP, rp, HEAD_W)
        small = extra[:, : rp - gr].reshape(n * TP, -1)
        at = 2 * rp

        def own_heads(v):
            v = v.reshape(v.shape[0], -1, TP, HEAD_W)
            return lax.dynamic_index_in_dim(v, w, 2, keepdims=False).reshape(v.shape[0], -1).astype(f32)

        self.taps = own_heads(small[:, at : at + CONV * cp].reshape(n * TP, CONV, cp).transpose(1, 0, 2).reshape(CONV, -1))
        decay = own_heads(small[:, at + CONV * cp : at + (CONV + 1) * cp].reshape(1, -1))
        gates = extra[:, rp - gr :].reshape(2, -1, HEAD_W, HEAD_W).transpose(1, 2, 0, 3)
        self.gates = gates.reshape(-1, HEAD_W, 2 * HEAD_W)
        self.mix_gain = small[:, :rp].reshape(-1).astype(f32)
        self.mlp_gain = small[:, rp : 2 * rp].reshape(-1).astype(f32)
        self.decay, self.slope = -DECAY * jax.nn.softplus(decay), -DECAY * jax.nn.sigmoid(decay)
        self.gelu, self.stream = flat[:, : width // 2], flat[:, width // 2 : width]


def forward_block(x, normed, keep, streams, wts, pump, following):
    width = x.shape[1]
    if normed is None:
        normed = tp_gather(rms_norm(x, wts.mix_gain).astype(bf16))
    tokens = normed.shape[0] // streams
    last = normed.reshape(streams, tokens, width)[:, tokens - REACH :].transpose(1, 0, 2)
    halo_in = shift_seq(last.reshape(REACH * streams, width), 1)
    stream = dot(normed, wts.stream, bf16)
    halo = dot(halo_in, wts.stream, bf16).astype(f32)
    a, driven, conv, ends = mix(streams, stream, halo, keep, wts.taps, wts.decay, wts.gates)
    branch = dot(normed, wts.gelu)
    start = carry_in(ends[0], ends[1], 1)
    h, merged = states(streams, a, driven, start, branch)
    wts.out = wts.buffers["out"].reshape(-1, width)
    if following is not None:
        pump.add(following.first_job(), following.out_job())
        merged = pump.step(merged)
    mixed = tp_scatter(dot(merged, wts.out, bf16).reshape(TP, -1, width))
    mixed, wts.wide = tie(mixed, wts.wide)
    mixed = pump.step(mixed)
    x1 = x + mixed
    mlp_in = tp_gather(rms_norm(x1, wts.mlp_gain).astype(bf16))
    mlp_in = pump.step(mlp_in)
    wide = pump.step(dot(mlp_in, wts.wide))
    half = wide.shape[1] // 2
    product = (gelu(wide[:, :half]) * wide[:, half:]).astype(bf16)
    kept = dict(
        x=x, normed=normed, stream=stream, branch=branch, halo=halo, a=a, conv=conv, whole=ends[0], start=start, h=h,
        merged=merged, x1=x1, mlp_in=mlp_in, wide=wide, product=product,
    )
    return kept


def block_end(kept, wts):
    product = kept["product"]
    width = kept["x1"].shape[1]
    return kept["x1"] + tp_scatter(dot(product, wts.down, bf16).reshape(TP, -1, width))


def mlp_back(gx, g_down, wts, kept, results, rp, pump, above):
    width = gx.shape[1]
    n = lax.axis_size("seq")
    grad_down = dot_tokens(kept["product"], g_down)
    g_down, grad_down = tie(g_down, grad_down)
    d_product = dot_t(g_down, wts.down)
    wide = kept["wide"]
    half = wide.shape[1] // 2
    value, slope = gelu_and_slope(wide[:, :half])
    d_wide = jnp.concatenate([(d_product * wide[:, half:] * slope).astype(bf16), (d_product * value).astype(bf16)], axis=1)
    grad_wide = dot_tokens(kept["mlp_in"], d_wide).reshape(n, -1, 2 * half)
    d_wide, grad_wide, grad_down = tie(d_wide, grad_wide, grad_down)
    if above is not None:
        d_wide, above["wide"] = tie(d_wide, above["wide"])
    part = dot_t(d_wide, wts.wide, bf16).reshape(TP, -1, width)
    d_mlp_in = tp_scatter(pump.step(part))
    d_mlp_in = pump.step(d_mlp_in)
    results["wide"] = lax.psum_scatter(grad_wide, "seq", scatter_dimension=0)
    if above is not None:
        d_mlp_in, grad_down = tie(d_mlp_in, grad_down)
    results["down"] = lax.psum_scatter(grad_down.reshape(n, -1, width), "seq", scatter_dimension=0).astype(f32)
    dv, d_gain = rms_norm_back(kept["x1"], wts.mlp_gain, d_mlp_in)
    return gx + dv, d_gain


def mixer_back(d_x1, keep, streams, wts, kept, d_mlp_gain, d_mix_gain, sizes, results, above, pump, end=None):
    rp, gr, cp, fb = sizes
    width = d_x1.shape[1]
    n, w = lax.axis_size("seq"), lax.axis_index("wt")
    g_branch = pump.step(tp_gather(d_x1.astype(bf16)))
    d_merged = dot_t(g_branch, wts.out)
    grad_out = dot_tokens(kept["merged"], g_branch)
    if end is not None:
        pump.add(ScatterJob(grad_out.reshape(n, -1, width), True, lambda total: results.update(out=from_heads(total))))
    dh, d_branch, ends = states_back(streams, d_merged, kept["branch"], kept["a"], kept["h"])
    if end is not None:
        ends = end(ends)
    ends = pump.step(ends)
    back = carry_in(kept["whole"], ends, -1)
    back = pump.step(back)
    d_stream, tail, head, d_gates, d_taps, d_decay = mix_back(
        streams, dh, kept["a"], kept["h"], kept["start"], back, kept["conv"], kept["stream"], kept["halo"], keep,
        wts.taps, wts.decay, wts.slope, wts.gates,
    )
    d_stream, head = pump.step((d_stream, head))
    tail = (tail + shift_seq(head, -1)).astype(bf16)
    tokens = d_stream.shape[0] // streams
    d_stream = lax.dynamic_update_slice(
        d_stream.reshape(streams, tokens, -1), tail.reshape(REACH, streams, -1).transpose(1, 0, 2), (0, tokens - REACH, 0)
    ).reshape(d_stream.shape)
    part = (dot_t(d_branch, wts.gelu) + dot_t(d_stream, wts.stream)).astype(bf16).reshape(TP, -1, width)

    def full(v):
        lines = v.reshape(v.shape[0], -1, 1, HEAD_W)
        return jnp.where(lax.iota(jnp.int32, TP)[None, None, :, None] == w, lines, 0.0).reshape(v.shape[0], n * TP, -1)

    small = jnp.concatenate(
        [
            d_mix_gain.reshape(n * TP, rp), d_mlp_gain.reshape(n * TP, rp),
            full(d_taps).transpose(1, 0, 2).reshape(n * TP, -1), full(d_decay)[0],
        ],
        axis=1,
    ).astype(bf16)
    used = small.shape[1]
    small = jnp.pad(small, ((0, 0), (0, (rp - gr) * HEAD_W - used))).reshape(n * TP, rp - gr, HEAD_W)
    gates = d_gates.reshape(-1, HEAD_W, 2, HEAD_W).transpose(2, 0, 1, 3).reshape(n * TP, gr, HEAD_W).astype(bf16)
    extra = jnp.concatenate([small, gates], axis=1).reshape(n, TP * rp, HEAD_W)
    grad_gelu = dot_tokens(kept["normed"], d_branch).reshape(n, TP * rp, -1)
    grad_stream = dot_tokens(kept["normed"], d_stream).reshape(n, TP * rp, -1)
    half = grad_gelu.shape[2]

    def finish(both):
        stack = both.reshape(TP, rp, -1)
        results["gates"] = from_heads(stack[:, rp - gr :, 2 * half :].reshape(TP * gr, HEAD_W))
        pieces = wt_exchange(both.astype(bf16).reshape(TP, rp, -1))
        results["gelu"] = head_columns_back([p[:, :half] for p in pieces]).astype(f32)
        results["stream"] = head_columns_back([p[:, half : 2 * half] for p in pieces]).astype(f32)
        sums = sum(p[: rp - gr, 2 * half :].astype(f32) for p in pieces).reshape(-1)[:used]
        above["mix_gain"], results["mlp_gain"] = sums[:rp], sums[rp : 2 * rp]
        results["taps"] = sums[2 * rp : 2 * rp + CONV * cp].reshape(CONV, cp)
        results["decay"] = sums[2 * rp + CONV * cp :]

    if end is None:
        part, grad_out, results["wide"] = tie(part, grad_out, results["wide"])
        run(ScatterJob(grad_out.reshape(n, -1, width), True, lambda total: results.update(out=from_heads(total))))
    run(ScatterJob(jnp.concatenate([grad_gelu, grad_stream, extra], axis=2), False, finish))
    d_normed = pump.step(tp_scatter(part))
    dv, d_gain = rms_norm_back(kept["x"], wts.mix_gain, d_normed)
    return d_x1 + dv, d_gain


def per_device(block_in, start_flags, out_grad, *shards):
    layers = shards[0].shape[0]
    micro, _, tokens, width = block_in.shape
    streams = micro * TP
    sizes = (shards[1].shape[1], shards[4].shape[1] // TP, shards[5].shape[1], shards[10].shape[1])
    rp = sizes[0]

    weights = [Weights(shards, layer) for layer in range(layers)]
    zero, pump = weights[0], Pump()
    zero.prepare_first()
    zero.prepare_out()
    pump.add(zero.first_job(), zero.out_job())
    rest = [w.shards for w in weights]
    block_in, start_flags, out_grad, rest = pump.step((block_in, start_flags, out_grad, rest))
    for w, shards_then in zip(weights, rest):
        w.shards = shards_then
    flags = tp_gather(start_flags[:, 0].astype(f32))
    x_in = block_in[:, 0].reshape(micro * tokens, width)
    grad = out_grad[:, 0].reshape(micro * tokens, width)
    x_all = tp_gather(x_in)
    keep = 1.0 - flags.T
    behind = 1.0 - shift_seq(flags[:, tokens - REACH :].T, 1)
    keep = jnp.concatenate([behind, keep, jnp.ones((REACH, streams), f32)]).reshape(-1, 1)
    keep = jnp.broadcast_to(keep, (keep.shape[0], HEAD_W))

    x = x_in.astype(f32)
    kept = []
    zero.prepare_wide()
    for _ in range(3):
        zero.wide_block = pump.step(zero.wide_block)
    zero.wide_block, x_all, rest = pump.step((zero.wide_block, x_all, [w.shards for w in weights]))
    pump.finish()
    zero.gather_wide()
    for w, shards_then in zip(weights, rest):
        w.shards = shards_then
    zero.gather_down()
    for wts in weights[1:]:
        wts.prepare_first()
        wts.prepare_out()
        wts.prepare_wide()
        wts.gather_wide()
        wts.gather_down()
    for layer in range(layers):
        wts = weights[layer]
        wts.open_first(sizes)
        normed = rms_norm(x_all.astype(f32), wts.mix_gain).astype(bf16) if layer == 0 else None
        following = weights[layer + 1] if layer < layers - 1 else None
        saved = forward_block(x, normed, keep, streams, wts, pump, following)
        if layer < layers - 1:
            x = pump.step(block_end(saved, wts))
            pump.finish()
        kept.append(saved)
        if layer == 0:
            grad_then, saved["wide"] = tie(grad, saved["wide"])
            g_down = tp_gather(grad_then)

    gx = grad.astype(f32)
    d_mix = jnp.zeros((width,), f32)
    results = [dict() for _ in range(layers)]
    spare, outcome = {}, []

    def last(ends):
        ends, kept[-1]["product"] = tie(ends, kept[-1]["product"])
        outcome.append(block_end(kept[-1], weights[-1]))
        return ends

    for layer in reversed(range(layers)):
        if layer != layers - 1:
            g_down = pump.step(tp_gather(gx.astype(bf16)))
            g_down, results[layer + 1]["down"] = tie(g_down, results[layer + 1]["down"])
        d_x1, d_mlp = mlp_back(
            gx, g_down, weights[layer], kept[layer], results[layer], rp, pump, results[layer + 1] if layer < layers - 1 else None
        )
        above = spare if layer == layers - 1 else results[layer + 1]
        gx, d_mix = mixer_back(
            d_x1, keep, streams, weights[layer], kept[layer], d_mlp, d_mix, sizes, results[layer], above, pump, last if layer == layers - 1 else None
        )
    pump.finish()
    for found in results:
        pieces = wt_exchange(found.pop("wide").reshape(TP, rp, -1))
        found["gate"], found["up"] = ff_columns_back(jnp.stack(pieces))
    results[0]["mix_gain"] = vector_scatter(d_mix.reshape(-1, TP, rp))
    shape = (micro, 1, tokens, width)
    names = ("mix_gain", "gelu", "stream", "taps", "gates", "decay", "out", "mlp_gain", "gate", "up", "down")
    stacked = [jnp.stack([results[layer][k] for layer in range(layers)]) for k in names]
    return (outcome[0].astype(bf16).reshape(shape), gx.astype(bf16).reshape(shape), *stacked)


def solution(mesh):
    both = ("seq", "wt")
    tokens = P(None, "wt", "seq", None)
    vector, matrix = P(None, both), P(None, both, None)
    weights = (vector, matrix, matrix, P(None, None, both), matrix, vector, matrix, vector, matrix, matrix, matrix)
    return jax.shard_map(
        per_device,
        mesh=mesh,
        in_specs=(tokens, P(None, "wt", "seq"), tokens, *weights),
        out_specs=(tokens, tokens, *weights),
        check_vma=False,
    )
```

```python
import functools

import jax
import jax.numpy as jnp
from jax import lax
from jax.experimental import pallas as pl
from jax.experimental.pallas import tpu as pltpu
from jax.sharding import PartitionSpec as P

f32 = jnp.float32
bf16 = jnp.bfloat16
HEAD_W = 128
CONV = 4
REACH = CONV - 1
TP = 4
EPS = 1e-06
DECAY = 8.0
GELU_C = 0.7978845608
GELU_K = 0.044715


def dot(left, right, out=f32):
    return lax.dot_general(left, right, (((1,), (0,)), ((), ())), preferred_element_type=f32).astype(out)


def dot_t(left, right, out=f32):
    return lax.dot_general(left, right, (((1,), (1,)), ((), ())), preferred_element_type=f32).astype(out)


def dot_tokens(left, right, out=bf16):
    return lax.dot_general(left, right, (((0,), (0,)), ((), ())), preferred_element_type=f32).astype(out)


def sigmoid(v):
    return 1.0 / (1.0 + jnp.exp(-v))


def gelu(v):
    return 0.5 * v * (1.0 + jnp.tanh(GELU_C * (v + GELU_K * v * v * v)))


def gelu_and_slope(v):
    square = v * v
    t = jnp.tanh(GELU_C * v * (1.0 + GELU_K * square))
    value = 0.5 * v * (1.0 + t)
    slope = 0.5 * (1.0 + t) + 0.5 * v * (1.0 - t * t) * GELU_C * (1.0 + 3.0 * GELU_K * square)
    return value, slope


def minus_expm1(y, e):
    series = -y * (1.0 + y * (1 / 2) * (1.0 + y * (1 / 3) * (1.0 + y * (1 / 4) * (1.0 + y * (1 / 5) * (1.0 + y * (1 / 6))))))
    return jnp.where(y > -0.25, series, 1.0 - e)


def rms_norm(v, gain):
    return v * lax.rsqrt(jnp.mean(v * v, axis=-1, keepdims=True) + EPS) * gain


def rms_norm_back(v, gain, dy):
    r = lax.rsqrt(jnp.mean(v * v, axis=-1, keepdims=True) + EPS)
    dgain = jnp.sum(dy * v * r, axis=0)
    dyg = dy * gain
    dv = r * dyg - v * (r * r * r) * jnp.mean(dyg * v, axis=-1, keepdims=True)
    return dv, dgain


def swap(x, k):
    return lax.ppermute(x, "wt", [(i, i ^ k) for i in range(TP)])


def tp_gather(x):
    far = swap(x, 2)
    near = swap(x, 1)
    diagonal = swap(far, 1)
    return jnp.concatenate([x, near, far, diagonal], axis=0)


def tp_scatter(part):
    far = (part[2].astype(f32) + swap(part[3], 1).astype(f32)).astype(bf16)
    across = swap(far, 2)
    near = swap(part[1], 1)
    return part[0].astype(f32) + near.astype(f32) + across.astype(f32)


def wt_exchange(pieces):
    w = lax.axis_index("wt")
    pick = lambda stack, j: lax.dynamic_index_in_dim(stack, j, 0, keepdims=False)
    got = [pick(pieces, w)] + [swap(pick(pieces, w ^ k), k) for k in range(1, TP)]
    stack = jnp.stack(got)
    return [pick(stack, w ^ j) for j in range(TP)]


def ring_tables():
    n = lax.axis_size("seq")
    order = [0, 1, 3, 5, 7, 6, 4, 2] if n == 8 else list(range(n))
    right = [(order[i], order[(i + 1) % n]) for i in range(n)]
    left = [(b, a) for a, b in right]
    s = lax.axis_index("seq")
    if n == 8:
        position = jnp.where(s % 2 == 1, s // 2 + 1, (8 - s // 2) % 8)
        owner = lambda p: jnp.where(p == 0, 0, jnp.where(p <= 4, 2 * p - 1, 16 - 2 * p))
    else:
        position, owner = s, lambda p: p
    device = lambda offset: owner(lax.rem(position + offset + n, n))
    return n, right, left, device


class GatherJob:
    def __init__(self, block, flip, place):
        self.n, right, left, self.device = ring_tables()
        self.routes = (left, right) if flip else (right, left)
        self.sign = -1 if flip else 1
        self.a = self.b = block
        self.hop, self.place = 0, place
        self.place(block, self.device(0))
        self.done = False

    def start(self):
        self.hop += 1
        flight = [lax.ppermute(self.a, "seq", self.routes[0])]
        if self.hop <= self.n - 1 - self.n // 2:
            flight.append(lax.ppermute(self.b, "seq", self.routes[1]))
        return flight

    def bytes(self):
        return self.a.size * 2

    def receive(self, flight):
        self.a = flight[0]
        self.place(self.a, self.device(-self.sign * self.hop))
        if len(flight) > 1:
            self.b = flight[1]
            self.place(self.b, self.device(self.sign * self.hop))
        self.done = self.hop == self.n // 2


class ScatterJob:
    def __init__(self, stack, flip, finish):
        self.n, right, left, self.device = ring_tables()
        self.routes = (left, right) if flip else (right, left)
        self.sign = -1 if flip else 1
        self.stack, self.finish = stack, finish
        self.far, self.near = self.n // 2, self.n - 1 - self.n // 2
        self.a, self.b = self.chunk(self.far), self.chunk(-self.near)
        self.hop, self.done = 0, False

    def chunk(self, k):
        return lax.dynamic_index_in_dim(self.stack, self.device(self.sign * k), 0, keepdims=False)

    def bytes(self):
        return self.a.size * 2

    def start(self):
        self.hop += 1
        flight = [lax.ppermute(self.a, "seq", self.routes[0])]
        if self.hop <= self.near:
            flight.append(lax.ppermute(self.b, "seq", self.routes[1]))
        return flight

    def receive(self, flight):
        add = lambda x, y: (x.astype(f32) + y.astype(f32)).astype(bf16)
        self.a = flight[0]
        if self.hop < self.far:
            self.a = add(self.a, self.chunk(self.far - self.hop))
        if len(flight) > 1:
            self.b = flight[1]
            if self.hop < self.near:
                self.b = add(self.b, self.chunk(self.hop - self.near))
        if self.hop == self.far:
            self.done = True
            self.finish(self.chunk(0).astype(f32) + self.a.astype(f32) + self.b.astype(f32))


def tie(*values):
    return lax.optimization_barrier(values)


def run(job):
    while not job.done:
        job.receive(job.start())


class Pump:
    def __init__(self):
        self.waiting, self.active = [], []

    def add(self, *jobs):
        self.waiting += jobs

    def hold(self, value):
        flights = [flight for _, flight in self.active]
        if flights:
            value, flights = lax.optimization_barrier((value, flights))
        for (job, _), flight in zip(self.active, flights):
            job.receive(flight)
            if not job.done:
                self.waiting.append(job)
        self.active = []
        return value

    def step(self, value):
        flights = [flight for _, flight in self.active]
        heads = [(job.a, job.b) for job in self.waiting]
        if flights or heads:
            value, flights, heads = lax.optimization_barrier((value, flights, heads))
        moved = []
        for (job, _), flight in zip(self.active, flights):
            job.receive(flight)
            if not job.done:
                moved.append(job)
        for job, (a, b) in zip(self.waiting, heads):
            job.a, job.b = a, b
            moved.append(job)
        self.waiting = []
        self.active = [(job, job.start()) for job in moved]
        return value

    def complete(self, jobs):
        for job, flight in self.active:
            if job in jobs:
                job.receive(flight)
        self.active = [(job, flight) for job, flight in self.active if job not in jobs]
        self.waiting = [job for job in self.waiting if job not in jobs]
        for job in jobs:
            run(job)

    def finish(self):
        for job, flight in self.active:
            job.receive(flight)
            run(job)
        for job in self.waiting:
            run(job)
        self.active, self.waiting = [], []


def shift_seq(x, distance):
    n = lax.axis_size("seq")
    return lax.ppermute(x, "seq", [(i, i + distance) for i in range(n) if 0 <= i + distance < n])


def carry_in(decay, state, direction):
    n = lax.axis_size("seq")
    width = decay.shape[-1]
    inclusive = jnp.concatenate([decay, state], axis=-1)

    def then(near, far):
        return jnp.concatenate(
            [near[:, :width] * far[:, :width], near[:, width:] + near[:, :width] * far[:, width:]], axis=-1
        )

    reach, covered, total = 1, 0, None
    while covered < n - 1:
        first = shift_seq(inclusive, direction * reach)
        second = shift_seq(inclusive, direction * 2 * reach) if covered + reach < n - 1 else None
        both = first if second is None else then(first, second)
        total = both if total is None else then(total, both)
        covered += 2 * reach if second is not None else reach
        inclusive = then(inclusive, both)
        reach *= 3
    return total[:, width:]


def head_route(rows):
    n = lax.axis_size("seq")
    per = HEAD_W // rows
    route = []
    for s in range(n):
        base = s // per * per
        for w in range(TP):
            b = TP * (s - base) + w
            route.append((s * TP + w, (base + b % per) * TP + b // per))
    return route


def to_heads(x):
    route = head_route(x.shape[0])
    return x if all(a == b for a, b in route) else lax.ppermute(x, ("seq", "wt"), route)


def from_heads(x):
    route = head_route(x.shape[0])
    return x if all(a == b for a, b in route) else lax.ppermute(x, ("seq", "wt"), [(b, a) for a, b in route])


def vector_scatter(v):
    w, s = lax.axis_index("wt"), lax.axis_index("seq")
    pick = lambda x, j, ax: lax.dynamic_index_in_dim(x, j, ax, keepdims=False)
    n, _, k = v.shape
    v = v.reshape(n, 2, 2, k)
    hi, lo = w >> 1, w & 1
    v = pick(v, hi, 1) + swap(pick(v, 1 - hi, 1), 2)
    v = pick(v, lo, 1) + swap(pick(v, 1 - lo, 1), 1)
    half = n // 2
    while half:
        v = v.reshape(2, half, k)
        bit = (s // half) % 2
        other = lax.ppermute(pick(v, 1 - bit, 0), "seq", [(i, i ^ half) for i in range(n)])
        v = pick(v, bit, 0) + other
        half //= 2
    return v.reshape(k)


def lay_stream(buf, src, streams, tokens, lead):
    for b in range(streams):
        buf[pl.ds(lead + b, tokens, stride=streams), :] = src[pl.ds(b * tokens, tokens), :].astype(f32)


def gate_values(pre_rows, decay_row, keep):
    sr = sigmoid(pre_rows[:, :HEAD_W])
    si = sigmoid(pre_rows[:, HEAD_W:])
    log_a = decay_row * sr
    raw = jnp.exp(log_a)
    e2 = raw * raw
    msq = keep * minus_expm1(2.0 * log_a, e2) + (1.0 - keep)
    return sr, si, raw, e2, jnp.sqrt(msq)


def mix_kernel(
    streams, tokens, stream_ref, halo_ref, keep_ref, taps_ref, decay_ref, gates_ref,
    a_ref, d_ref, conv_ref, ends_ref, buf, pre,
):
    lead = REACH * streams
    rows = streams * tokens
    step = 128
    buf[pl.ds(0, lead), :] = halo_ref[...]
    lay_stream(buf, stream_ref, streams, tokens, lead)
    taps = [taps_ref[pl.ds(k, 1), :] for k in range(CONV)]

    def conv_step(i, _):
        r = pl.multiple_of(i * step, step)
        total = taps[0] * buf[pl.ds(r + lead, step), :]
        valid = None
        for k in range(1, CONV):
            keep = keep_ref[pl.ds(r + lead - (k - 1) * streams, step), :]
            valid = keep if valid is None else valid * keep
            total = total + taps[k] * buf[pl.ds(r + lead - k * streams, step), :] * valid
        conv_ref[pl.ds(r, step), :] = total.astype(bf16)
        return 0

    lax.fori_loop(0, rows // step, conv_step, 0)
    pre[...] = jnp.dot(conv_ref[...], gates_ref[0], preferred_element_type=f32)

    def gate_step(i, _):
        r = pl.multiple_of(i * step, step)
        keep = keep_ref[pl.ds(r + lead, step), :]
        _, si, raw, _, m = gate_values(pre[pl.ds(r, step), :], decay_ref[...], keep)
        a_ref[pl.ds(r, step), :] = raw * keep
        d_ref[pl.ds(r, step), :] = m * si * conv_ref[pl.ds(r, step), :].astype(f32)
        return 0

    lax.fori_loop(0, rows // step, gate_step, 0)

    def scan_step(t, carry):
        total, h = carry
        r = pl.multiple_of(t * streams, streams)
        a = a_ref[pl.ds(r, streams), :]
        return total * a, a * h + d_ref[pl.ds(r, streams), :]

    total, h = lax.fori_loop(
        0, tokens, scan_step, (jnp.ones((streams, HEAD_W), f32), jnp.zeros((streams, HEAD_W), f32)), unroll=8
    )
    ends_ref[0] = total
    ends_ref[1] = h


def state_kernel(streams, tokens, a_ref, d_ref, start_ref, branch_ref, h_ref, merged_ref):
    def scan_step(t, h):
        r = pl.multiple_of(t * streams, streams)
        h = a_ref[pl.ds(r, streams), :] * h + d_ref[pl.ds(r, streams), :]
        h_ref[pl.ds(r, streams), :] = h
        return h

    lax.fori_loop(0, tokens, scan_step, start_ref[...], unroll=8)
    for b in range(streams):
        at = pl.ds(b * tokens, tokens)
        h = h_ref[pl.ds(b, tokens, stride=streams), :]
        merged_ref[at, :] = (h * gelu(branch_ref[at, :])).astype(bf16)


def state_back_kernel(streams, tokens, dm_ref, branch_ref, a_ref, h_ref, dh_ref, db_ref, ends_ref):
    for b in range(streams):
        at = pl.ds(b * tokens, tokens)
        dm = dm_ref[at, :]
        value, slope = gelu_and_slope(branch_ref[at, :])
        h = h_ref[pl.ds(b, tokens, stride=streams), :]
        dh_ref[pl.ds(b, tokens, stride=streams), :] = dm * value
        db_ref[at, :] = (dm * h * slope).astype(bf16)

    def scan_step(i, g):
        r = pl.multiple_of((tokens - 1 - i) * streams, streams)
        return a_ref[pl.ds(r, streams), :] * (dh_ref[pl.ds(r, streams), :] + g)

    ends_ref[...] = lax.fori_loop(0, tokens, scan_step, jnp.zeros((streams, HEAD_W), f32), unroll=8)


def mix_back_kernel(
    streams, tokens, dh_ref, a_ref, h_ref, start_ref, back_ref, conv_ref, stream_ref, halo_ref, keep_ref, taps_ref,
    decay_ref, slope_ref, gates_ref,
    ds_ref, tail_ref, head_ref, dgates_ref, dtaps_ref, ddecay_ref,
    buf, pre, back, dpre, dconv,
):
    lead = REACH * streams
    rows = streams * tokens
    step = 128
    buf[pl.ds(0, lead), :] = halo_ref[...]
    lay_stream(buf, stream_ref, streams, tokens, lead)
    pre[...] = jnp.dot(conv_ref[...], gates_ref[0], preferred_element_type=f32)

    def scan_step(i, g):
        r = pl.multiple_of((tokens - 1 - i) * streams, streams)
        total = dh_ref[pl.ds(r, streams), :] + g
        back[pl.ds(r, streams), :] = total
        return a_ref[pl.ds(r, streams), :] * total

    lax.fori_loop(0, tokens, scan_step, back_ref[...], unroll=8)
    dconv[pl.ds(rows, lead), :] = jnp.zeros((lead, HEAD_W), f32)

    def gate_step(i, acc):
        r = pl.multiple_of(i * step, step)
        keep = keep_ref[pl.ds(r + lead, step), :]
        decay = decay_ref[...]
        sr, si, raw, e2, m = gate_values(pre[pl.ds(r, step), :], decay, keep)
        g = back[pl.ds(r, step), :]
        conv = conv_ref[pl.ds(r, step), :].astype(f32)
        before = h_ref[pl.ds(jnp.maximum(r - streams, 0), step), :]
        shifted = jnp.concatenate([start_ref[...], before[: step - streams]], axis=0)
        previous = jnp.where(i == 0, shifted, before)
        gsi = g * si
        gm = gsi * m
        dconv[pl.ds(r, step), :] = gm
        d_input = gm * conv * (1.0 - si)
        d_log = g * previous * raw * keep - gsi * conv * keep * e2 / m
        by_rate = d_log * sr
        d_rate = by_rate * decay * (1.0 - sr)
        dpre[pl.ds(r, step), :] = jnp.concatenate([d_rate.astype(bf16), d_input.astype(bf16)], axis=1)
        return acc + jnp.sum(by_rate.reshape(step // 8, 8, HEAD_W), axis=0)

    acc = lax.fori_loop(0, rows // step, gate_step, jnp.zeros((8, HEAD_W), f32))
    ddecay_ref[...] = jnp.sum(acc, axis=0, keepdims=True) * slope_ref[...]
    dgates_ref[0] = lax.dot_general(conv_ref[...], dpre[...], (((0,), (0,)), ((), ())), preferred_element_type=f32)
    pre[:, :HEAD_W] = lax.dot_general(dpre[...], gates_ref[0], (((1,), (1,)), ((), ())), preferred_element_type=f32)
    taps = [taps_ref[pl.ds(k, 1), :] for k in range(CONV)]

    def add_step(i, accs):
        r = pl.multiple_of(i * step, step)
        dc = dconv[pl.ds(r, step), :] + pre[pl.ds(r, step), :HEAD_W]
        dconv[pl.ds(r, step), :] = dc
        out, valid = [], None
        for k in range(CONV):
            term = dc * buf[pl.ds(r + lead - k * streams, step), :]
            if k:
                keep = keep_ref[pl.ds(r + lead - (k - 1) * streams, step), :]
                valid = keep if valid is None else valid * keep
                term = term * valid
            out.append(accs[k] + jnp.sum(term.reshape(step // 8, 8, HEAD_W), axis=0))
        return tuple(out)

    accs = lax.fori_loop(0, rows // step, add_step, tuple(jnp.zeros((8, HEAD_W), f32) for _ in range(CONV)))
    for k in range(CONV):
        dtaps_ref[pl.ds(k, 1), :] = jnp.sum(accs[k], axis=0, keepdims=True)

    def stream_rows(r, count):
        total = taps[0] * dconv[pl.ds(r, count), :]
        valid = None
        for k in range(1, CONV):
            keep = keep_ref[pl.ds(r + lead + k * streams, count), :]
            valid = keep if valid is None else valid * keep
            total = total + taps[k] * dconv[pl.ds(r + k * streams, count), :] * valid
        return total

    def stream_step(i, _):
        r = pl.multiple_of(i * step, step)
        buf[pl.ds(r, step), :] = stream_rows(r, step)
        return 0

    lax.fori_loop(0, rows // step, stream_step, 0)
    tail_ref[...] = buf[pl.ds(rows - lead, lead), :]
    for b in range(streams):
        ds_ref[pl.ds(b * tokens, tokens), :] = buf[pl.ds(b, tokens, stride=streams), :].astype(bf16)
    for j in range(REACH):
        total = None
        valid = None
        for k in range(1, CONV):
            at = j + k - REACH
            keep = keep_ref[pl.ds((j + k) * streams, streams), :]
            valid = keep if valid is None else valid * keep
            if at >= 0:
                term = taps[k] * dconv[pl.ds(at * streams, streams), :] * valid
                total = term if total is None else total + term
        head_ref[pl.ds(j * streams, streams), :] = total


def by_head(rows):
    return pl.BlockSpec((rows, HEAD_W), lambda h: (0, h))


def whole(rows):
    return pl.BlockSpec((rows, HEAD_W), lambda h: (0, 0))


def params():
    return pltpu.CompilerParams(vmem_limit_bytes=40 * 2**20, dimension_semantics=("arbitrary",))


def mix(streams, stream, halo, keep, taps, decay, gates):
    rows, width = stream.shape
    tokens, heads, lead = rows // streams, width // HEAD_W, REACH * streams
    two = pl.BlockSpec((2, streams, HEAD_W), lambda h: (0, 0, h))
    shape = jax.ShapeDtypeStruct
    return pl.pallas_call(
        functools.partial(mix_kernel, streams, tokens),
        grid=(heads,),
        in_specs=[
            by_head(rows), by_head(lead), whole(keep.shape[0]), by_head(CONV), by_head(1),
            pl.BlockSpec((1, HEAD_W, 2 * HEAD_W), lambda h: (h, 0, 0)),
        ],
        out_specs=[by_head(rows), by_head(rows), by_head(rows), two],
        out_shape=[
            shape((rows, width), f32), shape((rows, width), f32), shape((rows, width), bf16), shape((2, streams, width), f32),
        ],
        scratch_shapes=[pltpu.VMEM((rows + lead, HEAD_W), f32), pltpu.VMEM((rows, 2 * HEAD_W), f32)],
        compiler_params=params(),
        cost_estimate=pl.CostEstimate(flops=rows * width * 600, bytes_accessed=rows * width * 12, transcendentals=rows * width * 6),
    )(stream, halo, keep, taps, decay, gates)


def states(streams, a, driven, start, branch):
    rows, width = a.shape
    tokens, heads = rows // streams, width // HEAD_W
    shape = jax.ShapeDtypeStruct
    return pl.pallas_call(
        functools.partial(state_kernel, streams, tokens),
        grid=(heads,),
        in_specs=[by_head(rows), by_head(rows), by_head(streams), by_head(rows)],
        out_specs=[by_head(rows), by_head(rows)],
        out_shape=[shape((rows, width), f32), shape((rows, width), bf16)],
        compiler_params=params(),
        cost_estimate=pl.CostEstimate(flops=rows * width * 30, bytes_accessed=rows * width * 18, transcendentals=rows * width),
    )(a, driven, start, branch)


def states_back(streams, d_merged, branch, a, h):
    rows, width = a.shape
    tokens, heads = rows // streams, width // HEAD_W
    shape = jax.ShapeDtypeStruct
    return pl.pallas_call(
        functools.partial(state_back_kernel, streams, tokens),
        grid=(heads,),
        in_specs=[by_head(rows)] * 4,
        out_specs=[by_head(rows), by_head(rows), by_head(streams)],
        out_shape=[shape((rows, width), f32), shape((rows, width), bf16), shape((streams, width), f32)],
        compiler_params=params(),
        cost_estimate=pl.CostEstimate(flops=rows * width * 40, bytes_accessed=rows * width * 22, transcendentals=rows * width),
    )(d_merged, branch, a, h)


def mix_back(streams, dh, a, h, start, back, conv, stream, halo, keep, taps, decay, slope, gates):
    rows, width = a.shape
    tokens, heads, lead = rows // streams, width // HEAD_W, REACH * streams
    shape = jax.ShapeDtypeStruct
    gate_spec = pl.BlockSpec((1, HEAD_W, 2 * HEAD_W), lambda h: (h, 0, 0))
    return pl.pallas_call(
        functools.partial(mix_back_kernel, streams, tokens),
        grid=(heads,),
        in_specs=[
            by_head(rows), by_head(rows), by_head(rows), by_head(streams), by_head(streams), by_head(rows), by_head(rows),
            by_head(lead), whole(keep.shape[0]), by_head(CONV), by_head(1), by_head(1), gate_spec,
        ],
        out_specs=[by_head(rows), by_head(lead), by_head(lead), gate_spec, by_head(CONV), by_head(1)],
        out_shape=[
            shape((rows, width), bf16), shape((lead, width), f32), shape((lead, width), f32),
            shape((heads, HEAD_W, 2 * HEAD_W), f32), shape((CONV, width), f32), shape((1, width), f32),
        ],
        scratch_shapes=[
            pltpu.VMEM((rows + lead, HEAD_W), f32), pltpu.VMEM((rows, 2 * HEAD_W), f32), pltpu.VMEM((rows, HEAD_W), f32),
            pltpu.VMEM((rows, 2 * HEAD_W), bf16), pltpu.VMEM((rows + lead, HEAD_W), f32),
        ],
        compiler_params=params(),
        cost_estimate=pl.CostEstimate(flops=rows * width * 1200, bytes_accessed=rows * width * 22, transcendentals=rows * width * 6),
    )(dh, a, h, start, back, conv, stream, halo, keep, taps, decay, slope, gates)


def head_columns(block):
    rows, width = block.shape
    groups = width // (TP * HEAD_W)
    return block.reshape(rows, groups, TP, HEAD_W).transpose(2, 0, 1, 3).reshape(TP, rows, width // TP)


def head_back_kernel(groups, pieces_ref, gelu_ref, stream_ref):
    half = groups * HEAD_W
    for w in range(TP):
        for g in range(groups):
            to = (g * TP + w) * HEAD_W
            gelu_ref[:, to : to + HEAD_W] = pieces_ref[w, :, g * HEAD_W : (g + 1) * HEAD_W].astype(f32)
            stream_ref[:, to : to + HEAD_W] = pieces_ref[w, :, half + g * HEAD_W : half + (g + 1) * HEAD_W].astype(f32)


def head_columns_back(pieces):
    _, rows, width = pieces.shape
    groups = (width - HEAD_W) // (2 * HEAD_W)
    out = jax.ShapeDtypeStruct((rows, TP * groups * HEAD_W), f32)
    return pl.pallas_call(
        functools.partial(head_back_kernel, groups), out_shape=[out, out],
        compiler_params=pltpu.CompilerParams(vmem_limit_bytes=24 * 2**20),
        cost_estimate=pl.CostEstimate(flops=rows * width * 8, bytes_accessed=rows * width * 40, transcendentals=0),
    )(pieces)


def ff_back_kernel(n, pieces_ref, gate_ref, up_ref):
    part = gate_ref.shape[1] // (n * TP)
    half = n * part
    for w in range(TP):
        for s in range(n):
            to = (s * TP + w) * part
            gate_ref[:, to : to + part] = pieces_ref[w, :, s * part : (s + 1) * part].astype(f32)
            up_ref[:, to : to + part] = pieces_ref[w, :, half + s * part : half + (s + 1) * part].astype(f32)


def ff_columns_back(pieces):
    n = lax.axis_size("seq")
    _, rows, width = pieces.shape
    out = jax.ShapeDtypeStruct((rows, TP * width // 2), f32)
    return pl.pallas_call(
        functools.partial(ff_back_kernel, n), out_shape=[out, out],
        compiler_params=pltpu.CompilerParams(vmem_limit_bytes=24 * 2**20),
        cost_estimate=pl.CostEstimate(flops=rows * width * 8, bytes_accessed=rows * width * 40, transcendentals=0),
    )(pieces)


def ff_kernel(n, gate_ref, up_ref, out_ref):
    part = gate_ref.shape[1] // (n * TP)
    half = n * part
    for w in range(TP):
        for s in range(n):
            at = (s * TP + w) * part
            out_ref[w, :, s * part : (s + 1) * part] = gate_ref[:, at : at + part]
            out_ref[w, :, half + s * part : half + (s + 1) * part] = up_ref[:, at : at + part]


def ff_columns(gate, up):
    rows, width = gate.shape
    return pl.pallas_call(
        functools.partial(ff_kernel, lax.axis_size("seq")),
        out_shape=jax.ShapeDtypeStruct((TP, rows, 2 * width // TP), bf16),
        compiler_params=pltpu.CompilerParams(vmem_limit_bytes=24 * 2**20),
        cost_estimate=pl.CostEstimate(flops=rows * width * 8, bytes_accessed=rows * width * 8, transcendentals=0),
    )(gate, up)


class Weights:
    def __init__(self, shards, layer):
        self.shards = [s[layer] for s in shards]
        self.buffers = {}
        self.flip = bool(layer % 2)

    def slot(self, name, shape):
        n = lax.axis_size("seq")
        if name not in self.buffers:
            self.buffers[name] = jnp.zeros((n,) + shape, bf16)

    def put(self, name, block, at, column=0):
        self.buffers[name] = lax.dynamic_update_slice(self.buffers[name], block[None], (at, 0, column))

    def prepare_first(self):
        (mix_gain, proj_gelu, proj_stream, conv_taps, lru_gates, decay_param, _, mlp_gain, _, _, _) = self.shards
        rp = proj_gelu.shape[0]
        gr = lru_gates.shape[0] // TP
        small = jnp.concatenate([mix_gain, mlp_gain, conv_taps.reshape(-1), decay_param])
        top = jnp.pad(small, (0, (rp - gr) * HEAD_W - small.shape[0])).reshape(rp - gr, HEAD_W)
        extra = jnp.concatenate([top, jnp.zeros((gr, HEAD_W), bf16)])
        pieces = jnp.concatenate(
            [head_columns(proj_gelu), head_columns(proj_stream), jnp.broadcast_to(extra, (TP, rp, HEAD_W))], axis=2
        )
        got = jnp.stack(wt_exchange(pieces))
        gates = to_heads(lru_gates).reshape(TP, gr, HEAD_W)
        width = got.shape[2] - HEAD_W
        self.first_block = lax.dynamic_update_slice(got, gates, (0, rp - gr, width)).reshape(TP * rp, width + HEAD_W)
        return self.first_block

    def prepare_out(self):
        self.out_block = to_heads(self.shards[6])

    def prepare_wide(self):
        proj_gate, proj_up = self.shards[8], self.shards[9]
        wide = jnp.stack(wt_exchange(ff_columns(proj_gate, proj_up)))
        self.wide_block = wide.reshape(TP * proj_gate.shape[0], -1)

    def first_job(self):
        self.slot("first", self.first_block.shape)
        return GatherJob(self.first_block, self.flip, lambda block, at: self.put("first", block, at))

    def out_job(self):
        self.slot("out", self.out_block.shape)
        return GatherJob(self.out_block, not self.flip, lambda block, at: self.put("out", block, at))

    def gather_down(self):
        self.down = lax.all_gather(self.shards[10], "seq", tiled=True)

    def gather_wide(self):
        self.wide = lax.all_gather(self.wide_block, "seq", tiled=True)

    def open_first(self, sizes):
        rp, gr, cp, fb = sizes
        first = self.buffers["first"]
        w = lax.axis_index("wt")
        n = first.shape[0]
        depth = n * TP * rp
        width = first.shape[2] - HEAD_W
        flat = first.reshape(depth, width + HEAD_W)
        extra = flat[:, width:].reshape(n * TP, rp, HEAD_W)
        small = extra[:, : rp - gr].reshape(n * TP, -1)
        at = 2 * rp

        def own_heads(v):
            v = v.reshape(v.shape[0], -1, TP, HEAD_W)
            return lax.dynamic_index_in_dim(v, w, 2, keepdims=False).reshape(v.shape[0], -1).astype(f32)

        self.taps = own_heads(small[:, at : at + CONV * cp].reshape(n * TP, CONV, cp).transpose(1, 0, 2).reshape(CONV, -1))
        decay = own_heads(small[:, at + CONV * cp : at + (CONV + 1) * cp].reshape(1, -1))
        gates = extra[:, rp - gr :].reshape(2, -1, HEAD_W, HEAD_W).transpose(1, 2, 0, 3)
        self.gates = gates.reshape(-1, HEAD_W, 2 * HEAD_W)
        self.mix_gain = small[:, :rp].reshape(-1).astype(f32)
        self.mlp_gain = small[:, rp : 2 * rp].reshape(-1).astype(f32)
        self.decay, self.slope = -DECAY * jax.nn.softplus(decay), -DECAY * jax.nn.sigmoid(decay)
        self.gelu, self.stream = flat[:, : width // 2], flat[:, width // 2 : width]


def forward_block(x, normed, keep, streams, wts, pump, following):
    width = x.shape[1]
    if normed is None:
        normed = tp_gather(rms_norm(x, wts.mix_gain).astype(bf16))
    tokens = normed.shape[0] // streams
    last = normed.reshape(streams, tokens, width)[:, tokens - REACH :].transpose(1, 0, 2)
    halo_in = shift_seq(last.reshape(REACH * streams, width), 1)
    stream = dot(normed, wts.stream, bf16)
    halo = dot(halo_in, wts.stream, bf16).astype(f32)
    a, driven, conv, ends = mix(streams, stream, halo, keep, wts.taps, wts.decay, wts.gates)
    branch = dot(normed, wts.gelu)
    start = carry_in(ends[0], ends[1], 1)
    h, merged = states(streams, a, driven, start, branch)
    wts.out = wts.buffers["out"].reshape(-1, width)
    if following is not None:
        pump.add(following.first_job(), following.out_job())
        merged = pump.step(merged)
    mixed = tp_scatter(dot(merged, wts.out, bf16).reshape(TP, -1, width))
    mixed, wts.wide = tie(mixed, wts.wide)
    mixed = pump.step(mixed)
    x1 = x + mixed
    mlp_in = tp_gather(rms_norm(x1, wts.mlp_gain).astype(bf16))
    mlp_in = pump.step(mlp_in)
    wide = pump.step(dot(mlp_in, wts.wide))
    half = wide.shape[1] // 2
    product = (gelu(wide[:, :half]) * wide[:, half:]).astype(bf16)
    kept = dict(
        x=x, normed=normed, stream=stream, branch=branch, halo=halo, a=a, conv=conv, whole=ends[0], start=start, h=h,
        merged=merged, x1=x1, mlp_in=mlp_in, wide=wide, product=product,
    )
    return kept


def block_end(kept, wts):
    product = kept["product"]
    width = kept["x1"].shape[1]
    return kept["x1"] + tp_scatter(dot(product, wts.down, bf16).reshape(TP, -1, width))


def mlp_back(gx, g_down, wts, kept, results, rp, pump, above):
    width = gx.shape[1]
    n = lax.axis_size("seq")
    grad_down = dot_tokens(kept["product"], g_down)
    g_down, grad_down = tie(g_down, grad_down)
    d_product = dot_t(g_down, wts.down)
    wide = kept["wide"]
    half = wide.shape[1] // 2
    value, slope = gelu_and_slope(wide[:, :half])
    d_wide = jnp.concatenate([(d_product * wide[:, half:] * slope).astype(bf16), (d_product * value).astype(bf16)], axis=1)
    grad_wide = dot_tokens(kept["mlp_in"], d_wide).reshape(n, -1, 2 * half)
    d_wide, grad_wide, grad_down = tie(d_wide, grad_wide, grad_down)
    if above is not None:
        d_wide, above["wide"] = tie(d_wide, above["wide"])
    part = dot_t(d_wide, wts.wide, bf16).reshape(TP, -1, width)
    d_mlp_in = tp_scatter(pump.step(part))
    results["wide"] = lax.psum_scatter(grad_wide, "seq", scatter_dimension=0)
    if above is not None:
        d_mlp_in, grad_down = tie(d_mlp_in, grad_down)
    results["down"] = lax.psum_scatter(grad_down.reshape(n, -1, width), "seq", scatter_dimension=0).astype(f32)
    dv, d_gain = rms_norm_back(kept["x1"], wts.mlp_gain, d_mlp_in)
    return gx + dv, d_gain


def mixer_back(d_x1, keep, streams, wts, kept, d_mlp_gain, d_mix_gain, sizes, results, pump, end=None):
    rp, gr, cp, fb = sizes
    width = d_x1.shape[1]
    n, w = lax.axis_size("seq"), lax.axis_index("wt")
    g_branch = tp_gather(d_x1.astype(bf16))
    d_merged = dot_t(g_branch, wts.out)
    grad_out = dot_tokens(kept["merged"], g_branch)
    dh, d_branch, ends = states_back(streams, d_merged, kept["branch"], kept["a"], kept["h"])
    if end is not None:
        ends = end(ends)
    ends = pump.hold(ends)
    back = carry_in(kept["whole"], ends, -1)
    back = pump.step(back)
    d_stream, tail, head, d_gates, d_taps, d_decay = mix_back(
        streams, dh, kept["a"], kept["h"], kept["start"], back, kept["conv"], kept["stream"], kept["halo"], keep,
        wts.taps, wts.decay, wts.slope, wts.gates,
    )
    tail = (tail + shift_seq(head, -1)).astype(bf16)
    tokens = d_stream.shape[0] // streams
    d_stream = lax.dynamic_update_slice(
        d_stream.reshape(streams, tokens, -1), tail.reshape(REACH, streams, -1).transpose(1, 0, 2), (0, tokens - REACH, 0)
    ).reshape(d_stream.shape)
    part = (dot_t(d_branch, wts.gelu) + dot_t(d_stream, wts.stream)).astype(bf16).reshape(TP, -1, width)

    def full(v):
        lines = v.reshape(v.shape[0], -1, 1, HEAD_W)
        return jnp.where(lax.iota(jnp.int32, TP)[None, None, :, None] == w, lines, 0.0).reshape(v.shape[0], n * TP, -1)

    small = jnp.concatenate(
        [
            d_mix_gain.reshape(n * TP, rp), d_mlp_gain.reshape(n * TP, rp),
            full(d_taps).transpose(1, 0, 2).reshape(n * TP, -1), full(d_decay)[0],
        ],
        axis=1,
    ).astype(bf16)
    small = jnp.pad(small, ((0, 0), (0, (rp - gr) * HEAD_W - small.shape[1]))).reshape(n * TP, rp - gr, HEAD_W)
    gates = d_gates.reshape(-1, HEAD_W, 2, HEAD_W).transpose(2, 0, 1, 3).reshape(n * TP, gr, HEAD_W).astype(bf16)
    extra = jnp.concatenate([small, gates], axis=1).reshape(n, TP * rp, HEAD_W)
    grad_gelu = dot_tokens(kept["normed"], d_branch).reshape(n, TP * rp, -1)
    grad_stream = dot_tokens(kept["normed"], d_stream).reshape(n, TP * rp, -1)

    both = ScatterJob(
        jnp.concatenate([grad_gelu, grad_stream, extra], axis=2), False, lambda total: results.update(raw=total)
    )
    if end is None:
        part, results["wide"] = tie(part, results["wide"])
    pump.add(
        both,
        ScatterJob(grad_out.reshape(n, -1, width), True, lambda total: results.update(out=from_heads(total))),
    )
    d_normed = tp_scatter(pump.step(part))
    if end is None:
        d_normed = pump.step(d_normed)
    dv, d_gain = rms_norm_back(kept["x"], wts.mix_gain, d_normed)
    return d_x1 + dv, d_gain, both


def finish_both(raw, results, above, sizes):
    rp, gr, cp, fb = sizes
    width = raw.shape[1] - HEAD_W
    results["gates"] = from_heads(raw.reshape(TP, rp, -1)[:, rp - gr :, width:].reshape(TP * gr, HEAD_W))
    pieces = jnp.stack(wt_exchange(raw.astype(bf16).reshape(TP, rp, -1)))
    results["gelu"], results["stream"] = head_columns_back(pieces)
    sums = jnp.sum(pieces[:, : rp - gr, width:].astype(f32), axis=0).reshape(-1)
    above["mix_gain"], results["mlp_gain"] = sums[:rp], sums[rp : 2 * rp]
    results["taps"] = sums[2 * rp : 2 * rp + CONV * cp].reshape(CONV, cp)
    results["decay"] = sums[2 * rp + CONV * cp : 2 * rp + (CONV + 1) * cp]


def per_device(block_in, start_flags, out_grad, *shards):
    layers = shards[0].shape[0]
    micro, _, tokens, width = block_in.shape
    streams = micro * TP
    sizes = (shards[1].shape[1], shards[4].shape[1] // TP, shards[5].shape[1], shards[10].shape[1])
    rp = sizes[0]

    weights = [Weights(shards, layer) for layer in range(layers)]
    zero, pump = weights[0], Pump()
    zero.prepare_first()
    zero.prepare_out()
    pump.add(zero.first_job(), zero.out_job())
    rest = [w.shards for w in weights]
    block_in, start_flags, out_grad, rest = pump.step((block_in, start_flags, out_grad, rest))
    for w, shards_then in zip(weights, rest):
        w.shards = shards_then
    flags = tp_gather(start_flags[:, 0].astype(f32))
    x_in = block_in[:, 0].reshape(micro * tokens, width)
    grad = out_grad[:, 0].reshape(micro * tokens, width)
    x_all = tp_gather(x_in)
    keep = 1.0 - flags.T
    behind = 1.0 - shift_seq(flags[:, tokens - REACH :].T, 1)
    keep = jnp.concatenate([behind, keep, jnp.ones((REACH, streams), f32)]).reshape(-1, 1)
    keep = jnp.broadcast_to(keep, (keep.shape[0], HEAD_W))

    x = x_in.astype(f32)
    kept = []
    zero.prepare_wide()
    for _ in range(3):
        zero.wide_block = pump.step(zero.wide_block)
    zero.wide_block, x_all, rest = pump.step((zero.wide_block, x_all, [w.shards for w in weights]))
    pump.finish()
    zero.gather_wide()
    for w, shards_then in zip(weights, rest):
        w.shards = shards_then
    zero.gather_down()
    for wts in weights[1:]:
        wts.prepare_first()
        wts.prepare_out()
        wts.prepare_wide()
        wts.gather_wide()
        wts.gather_down()
    for layer in range(layers):
        wts = weights[layer]
        wts.open_first(sizes)
        normed = rms_norm(x_all.astype(f32), wts.mix_gain).astype(bf16) if layer == 0 else None
        following = weights[layer + 1] if layer < layers - 1 else None
        saved = forward_block(x, normed, keep, streams, wts, pump, following)
        if layer < layers - 1:
            x = pump.step(block_end(saved, wts))
            pump.finish()
        kept.append(saved)
        if layer == 0:
            grad_then, saved["wide"] = tie(grad, saved["wide"])
            g_down = tp_gather(grad_then)

    gx = grad.astype(f32)
    d_mix = jnp.zeros((width,), f32)
    results = [dict() for _ in range(layers)]
    spare, outcome, jobs = {}, [], []

    def last(ends):
        ends, kept[-1]["product"] = tie(ends, kept[-1]["product"])
        outcome.append(block_end(kept[-1], weights[-1]))
        return ends

    for layer in reversed(range(layers)):
        if layer != layers - 1:
            g_down = tp_gather(gx.astype(bf16))
            g_down, results[layer + 1]["down"] = tie(g_down, results[layer + 1]["down"])
        d_x1, d_mlp = mlp_back(
            gx, g_down, weights[layer], kept[layer], results[layer], rp, pump, results[layer + 1] if layer < layers - 1 else None
        )
        gx, d_mix, both = mixer_back(
            d_x1, keep, streams, weights[layer], kept[layer], d_mlp, d_mix, sizes, results[layer], pump, last if layer == layers - 1 else None
        )
        jobs.append(both)
    pump.complete(jobs[:-1])
    held = [found.pop("raw") for found in results[1:]]
    wide = [found["wide"] for found in results[1:]]
    held, wide = pump.step(pump.step((held, wide)))
    for layer in range(1, layers):
        results[layer]["wide"] = wide[layer - 1]
    pump.finish()
    for layer in reversed(range(layers)):
        raw = held[layer - 1] if layer else results[0].pop("raw")
        finish_both(raw, results[layer], results[layer + 1] if layer < layers - 1 else spare, sizes)
    for found in results:
        pieces = wt_exchange(found.pop("wide").reshape(TP, rp, -1))
        found["gate"], found["up"] = ff_columns_back(jnp.stack(pieces))
    results[0]["mix_gain"] = vector_scatter(d_mix.reshape(-1, TP, rp))
    shape = (micro, 1, tokens, width)
    names = ("mix_gain", "gelu", "stream", "taps", "gates", "decay", "out", "mlp_gain", "gate", "up", "down")
    stacked = [jnp.stack([results[layer][k] for layer in range(layers)]) for k in names]
    return (outcome[0].astype(bf16).reshape(shape), gx.astype(bf16).reshape(shape), *stacked)


def solution(mesh):
    both = ("seq", "wt")
    tokens = P(None, "wt", "seq", None)
    vector, matrix = P(None, both), P(None, both, None)
    weights = (vector, matrix, matrix, P(None, None, both), matrix, vector, matrix, vector, matrix, matrix, matrix)
    return jax.shard_map(
        per_device,
        mesh=mesh,
        in_specs=(tokens, P(None, "wt", "seq"), tokens, *weights),
        out_specs=(tokens, tokens, *weights),
        check_vma=False,
    )
```

```python
import functools

import jax
import jax.numpy as jnp
from jax import lax
from jax.experimental import pallas as pl
from jax.experimental.pallas import tpu as pltpu
from jax.sharding import PartitionSpec as P

f32 = jnp.float32
bf16 = jnp.bfloat16
HEAD_W = 128
CONV = 4
REACH = CONV - 1
TP = 4
EPS = 1e-06
DECAY = 8.0
GELU_C = 0.7978845608
GELU_K = 0.044715


def dot(left, right, out=f32):
    return lax.dot_general(left, right, (((1,), (0,)), ((), ())), preferred_element_type=f32).astype(out)


def dot_t(left, right, out=f32):
    return lax.dot_general(left, right, (((1,), (1,)), ((), ())), preferred_element_type=f32).astype(out)


def dot_tokens(left, right, out=bf16):
    return lax.dot_general(left, right, (((0,), (0,)), ((), ())), preferred_element_type=f32).astype(out)


def sigmoid(v):
    return 1.0 / (1.0 + jnp.exp(-v))


def gelu(v):
    return 0.5 * v * (1.0 + jnp.tanh(GELU_C * (v + GELU_K * v * v * v)))


def gelu_and_slope(v):
    square = v * v
    t = jnp.tanh(GELU_C * v * (1.0 + GELU_K * square))
    value = 0.5 * v * (1.0 + t)
    slope = 0.5 * (1.0 + t) + 0.5 * v * (1.0 - t * t) * GELU_C * (1.0 + 3.0 * GELU_K * square)
    return value, slope


def minus_expm1(y, e):
    series = -y * (1.0 + y * (1 / 2) * (1.0 + y * (1 / 3) * (1.0 + y * (1 / 4) * (1.0 + y * (1 / 5) * (1.0 + y * (1 / 6))))))
    return jnp.where(y > -0.25, series, 1.0 - e)


def rms_norm(v, gain):
    return v * lax.rsqrt(jnp.mean(v * v, axis=-1, keepdims=True) + EPS) * gain


def rms_norm_back(v, gain, dy):
    r = lax.rsqrt(jnp.mean(v * v, axis=-1, keepdims=True) + EPS)
    dgain = jnp.sum(dy * v * r, axis=0)
    dyg = dy * gain
    dv = r * dyg - v * (r * r * r) * jnp.mean(dyg * v, axis=-1, keepdims=True)
    return dv, dgain


def swap(x, k):
    return lax.ppermute(x, "wt", [(i, i ^ k) for i in range(TP)])


def tp_gather(x):
    far = swap(x, 2)
    near = swap(x, 1)
    diagonal = swap(far, 1)
    return jnp.concatenate([x, near, far, diagonal], axis=0)


def tp_scatter(term, *rows):
    half = rows[0].shape[0] // 2
    part = term(*[r[half:] for r in rows])
    part = part.reshape(2, half // 2, -1)
    far = (part[0].astype(f32) + swap(part[1], 1).astype(f32)).astype(bf16)
    across = swap(far, 2)
    close = term(*[r[:half] for r in rows])
    close = close.reshape(2, half // 2, -1)
    near = swap(close[1], 1)
    return close[0].astype(f32) + near.astype(f32) + across.astype(f32)


def wt_exchange(pieces):
    w = lax.axis_index("wt")
    pick = lambda stack, j: lax.dynamic_index_in_dim(stack, j, 0, keepdims=False)
    got = [pick(pieces, w)] + [swap(pick(pieces, w ^ k), k) for k in range(1, TP)]
    stack = jnp.stack(got)
    return [pick(stack, w ^ j) for j in range(TP)]


def ring_tables():
    n = lax.axis_size("seq")
    order = [0, 1, 3, 5, 7, 6, 4, 2] if n == 8 else list(range(n))
    right = [(order[i], order[(i + 1) % n]) for i in range(n)]
    left = [(b, a) for a, b in right]
    s = lax.axis_index("seq")
    if n == 8:
        position = jnp.where(s % 2 == 1, s // 2 + 1, (8 - s // 2) % 8)
        owner = lambda p: jnp.where(p == 0, 0, jnp.where(p <= 4, 2 * p - 1, 16 - 2 * p))
    else:
        position, owner = s, lambda p: p
    device = lambda offset: owner(lax.rem(position + offset + n, n))
    return n, right, left, device


class GatherJob:
    def __init__(self, block, flip, place):
        self.n, right, left, self.device = ring_tables()
        self.routes = (left, right) if flip else (right, left)
        self.sign = -1 if flip else 1
        self.a = self.b = block
        self.hop, self.place = 0, place
        self.place(block, self.device(0))
        self.done = False

    def start(self):
        self.hop += 1
        flight = [lax.ppermute(self.a, "seq", self.routes[0])]
        if self.hop <= self.n - 1 - self.n // 2:
            flight.append(lax.ppermute(self.b, "seq", self.routes[1]))
        return flight

    def bytes(self):
        return self.a.size * 2

    def receive(self, flight):
        self.a = flight[0]
        self.place(self.a, self.device(-self.sign * self.hop))
        if len(flight) > 1:
            self.b = flight[1]
            self.place(self.b, self.device(self.sign * self.hop))
        self.done = self.hop == self.n // 2


class ScatterJob:
    def __init__(self, stack, flip, finish):
        self.n, right, left, self.device = ring_tables()
        self.routes = (left, right) if flip else (right, left)
        self.sign = -1 if flip else 1
        self.stack, self.finish = stack, finish
        self.far, self.near = self.n // 2, self.n - 1 - self.n // 2
        self.a, self.b = self.chunk(self.far), self.chunk(-self.near)
        self.hop, self.done = 0, False

    def chunk(self, k):
        return lax.dynamic_index_in_dim(self.stack, self.device(self.sign * k), 0, keepdims=False)

    def bytes(self):
        return self.a.size * 2

    def start(self):
        self.hop += 1
        flight = [lax.ppermute(self.a, "seq", self.routes[0])]
        if self.hop <= self.near:
            flight.append(lax.ppermute(self.b, "seq", self.routes[1]))
        return flight

    def receive(self, flight):
        add = lambda x, y: (x.astype(f32) + y.astype(f32)).astype(bf16)
        self.a = flight[0]
        if self.hop < self.far:
            self.a = add(self.a, self.chunk(self.far - self.hop))
        if len(flight) > 1:
            self.b = flight[1]
            if self.hop < self.near:
                self.b = add(self.b, self.chunk(self.hop - self.near))
        if self.hop == self.far:
            self.done = True
            self.finish(self.chunk(0).astype(f32) + self.a.astype(f32) + self.b.astype(f32))


def tie(*values):
    return lax.optimization_barrier(values)


def run(job):
    while not job.done:
        job.receive(job.start())


class Pump:
    def __init__(self):
        self.waiting, self.active = [], []

    def add(self, *jobs):
        self.waiting += jobs

    def hold(self, value):
        flights = [flight for _, flight in self.active]
        if flights:
            value, flights = lax.optimization_barrier((value, flights))
        for (job, _), flight in zip(self.active, flights):
            job.receive(flight)
            if not job.done:
                self.waiting.append(job)
        self.active = []
        return value

    def step(self, value):
        flights = [flight for _, flight in self.active]
        heads = [(job.a, job.b) for job in self.waiting]
        if flights or heads:
            value, flights, heads = lax.optimization_barrier((value, flights, heads))
        moved = []
        for (job, _), flight in zip(self.active, flights):
            job.receive(flight)
            if not job.done:
                moved.append(job)
        for job, (a, b) in zip(self.waiting, heads):
            job.a, job.b = a, b
            moved.append(job)
        self.waiting = []
        self.active = [(job, job.start()) for job in moved]
        return value

    def complete(self, jobs):
        for job, flight in self.active:
            if job in jobs:
                job.receive(flight)
        self.active = [(job, flight) for job, flight in self.active if job not in jobs]
        self.waiting = [job for job in self.waiting if job not in jobs]
        for job in jobs:
            run(job)

    def finish(self):
        for job, flight in self.active:
            job.receive(flight)
            run(job)
        for job in self.waiting:
            run(job)
        self.active, self.waiting = [], []


def shift_seq(x, distance):
    n = lax.axis_size("seq")
    return lax.ppermute(x, "seq", [(i, i + distance) for i in range(n) if 0 <= i + distance < n])


def carry_in(decay, state, direction):
    n = lax.axis_size("seq")
    width = decay.shape[-1]
    inclusive = jnp.concatenate([decay, state], axis=-1)

    def then(near, far):
        return jnp.concatenate(
            [near[:, :width] * far[:, :width], near[:, width:] + near[:, :width] * far[:, width:]], axis=-1
        )

    reach, covered, total = 1, 0, None
    while covered < n - 1:
        first = shift_seq(inclusive, direction * reach)
        second = shift_seq(inclusive, direction * 2 * reach) if covered + reach < n - 1 else None
        both = first if second is None else then(first, second)
        total = both if total is None else then(total, both)
        covered += 2 * reach if second is not None else reach
        inclusive = then(inclusive, both)
        reach *= 3
    return total[:, width:]


def head_route(rows):
    n = lax.axis_size("seq")
    per = HEAD_W // rows
    route = []
    for s in range(n):
        base = s // per * per
        for w in range(TP):
            b = TP * (s - base) + w
            route.append((s * TP + w, (base + b % per) * TP + b // per))
    return route


def to_heads(x):
    route = head_route(x.shape[0])
    return x if all(a == b for a, b in route) else lax.ppermute(x, ("seq", "wt"), route)


def from_heads(x):
    route = head_route(x.shape[0])
    return x if all(a == b for a, b in route) else lax.ppermute(x, ("seq", "wt"), [(b, a) for a, b in route])


def vector_scatter(v):
    w, s = lax.axis_index("wt"), lax.axis_index("seq")
    pick = lambda x, j, ax: lax.dynamic_index_in_dim(x, j, ax, keepdims=False)
    n, _, k = v.shape
    v = v.reshape(n, 2, 2, k)
    hi, lo = w >> 1, w & 1
    v = pick(v, hi, 1) + swap(pick(v, 1 - hi, 1), 2)
    v = pick(v, lo, 1) + swap(pick(v, 1 - lo, 1), 1)
    half = n // 2
    while half:
        v = v.reshape(2, half, k)
        bit = (s // half) % 2
        other = lax.ppermute(pick(v, 1 - bit, 0), "seq", [(i, i ^ half) for i in range(n)])
        v = pick(v, bit, 0) + other
        half //= 2
    return v.reshape(k)


def lay_stream(buf, src, streams, tokens, lead):
    for b in range(streams):
        buf[pl.ds(lead + b, tokens, stride=streams), :] = src[pl.ds(b * tokens, tokens), :].astype(f32)


def gate_values(pre_rows, decay_row, keep):
    sr = sigmoid(pre_rows[:, :HEAD_W])
    si = sigmoid(pre_rows[:, HEAD_W:])
    log_a = decay_row * sr
    raw = jnp.exp(log_a)
    e2 = raw * raw
    msq = keep * minus_expm1(2.0 * log_a, e2) + (1.0 - keep)
    return sr, si, raw, e2, jnp.sqrt(msq)


def mix_kernel(
    streams, tokens, stream_ref, halo_ref, keep_ref, taps_ref, decay_ref, gates_ref,
    a_ref, d_ref, conv_ref, ends_ref, buf, pre,
):
    lead = REACH * streams
    rows = streams * tokens
    step = 128
    buf[pl.ds(0, lead), :] = halo_ref[...]
    lay_stream(buf, stream_ref, streams, tokens, lead)
    taps = [taps_ref[pl.ds(k, 1), :] for k in range(CONV)]

    def conv_step(i, _):
        r = pl.multiple_of(i * step, step)
        total = taps[0] * buf[pl.ds(r + lead, step), :]
        valid = None
        for k in range(1, CONV):
            keep = keep_ref[pl.ds(r + lead - (k - 1) * streams, step), :]
            valid = keep if valid is None else valid * keep
            total = total + taps[k] * buf[pl.ds(r + lead - k * streams, step), :] * valid
        conv_ref[pl.ds(r, step), :] = total.astype(bf16)
        return 0

    lax.fori_loop(0, rows // step, conv_step, 0)
    pre[...] = jnp.dot(conv_ref[...], gates_ref[0], preferred_element_type=f32)

    def gate_step(i, _):
        r = pl.multiple_of(i * step, step)
        keep = keep_ref[pl.ds(r + lead, step), :]
        _, si, raw, _, m = gate_values(pre[pl.ds(r, step), :], decay_ref[...], keep)
        a_ref[pl.ds(r, step), :] = raw * keep
        d_ref[pl.ds(r, step), :] = m * si * conv_ref[pl.ds(r, step), :].astype(f32)
        return 0

    lax.fori_loop(0, rows // step, gate_step, 0)

    def scan_step(t, carry):
        total, h = carry
        r = pl.multiple_of(t * streams, streams)
        a = a_ref[pl.ds(r, streams), :]
        return total * a, a * h + d_ref[pl.ds(r, streams), :]

    total, h = lax.fori_loop(
        0, tokens, scan_step, (jnp.ones((streams, HEAD_W), f32), jnp.zeros((streams, HEAD_W), f32)), unroll=8
    )
    ends_ref[0] = total
    ends_ref[1] = h


def state_kernel(streams, tokens, a_ref, d_ref, start_ref, branch_ref, h_ref, merged_ref):
    def scan_step(t, h):
        r = pl.multiple_of(t * streams, streams)
        h = a_ref[pl.ds(r, streams), :] * h + d_ref[pl.ds(r, streams), :]
        h_ref[pl.ds(r, streams), :] = h
        return h

    lax.fori_loop(0, tokens, scan_step, start_ref[...], unroll=8)
    for b in range(streams):
        at = pl.ds(b * tokens, tokens)
        h = h_ref[pl.ds(b, tokens, stride=streams), :]
        merged_ref[at, :] = (h * gelu(branch_ref[at, :])).astype(bf16)


def state_back_kernel(streams, tokens, dm_ref, branch_ref, a_ref, h_ref, dh_ref, db_ref, ends_ref):
    for b in range(streams):
        at = pl.ds(b * tokens, tokens)
        dm = dm_ref[at, :]
        value, slope = gelu_and_slope(branch_ref[at, :])
        h = h_ref[pl.ds(b, tokens, stride=streams), :]
        dh_ref[pl.ds(b, tokens, stride=streams), :] = dm * value
        db_ref[at, :] = (dm * h * slope).astype(bf16)

    def scan_step(i, g):
        r = pl.multiple_of((tokens - 1 - i) * streams, streams)
        return a_ref[pl.ds(r, streams), :] * (dh_ref[pl.ds(r, streams), :] + g)

    ends_ref[...] = lax.fori_loop(0, tokens, scan_step, jnp.zeros((streams, HEAD_W), f32), unroll=8)


def mix_back_kernel(
    streams, tokens, dh_ref, a_ref, h_ref, start_ref, back_ref, conv_ref, stream_ref, halo_ref, keep_ref, taps_ref,
    decay_ref, slope_ref, gates_ref,
    ds_ref, tail_ref, head_ref, dgates_ref, dtaps_ref, ddecay_ref,
    buf, pre, back, dpre, dconv,
):
    lead = REACH * streams
    rows = streams * tokens
    step = 128
    buf[pl.ds(0, lead), :] = halo_ref[...]
    lay_stream(buf, stream_ref, streams, tokens, lead)
    pre[...] = jnp.dot(conv_ref[...], gates_ref[0], preferred_element_type=f32)

    def scan_step(i, g):
        r = pl.multiple_of((tokens - 1 - i) * streams, streams)
        total = dh_ref[pl.ds(r, streams), :] + g
        back[pl.ds(r, streams), :] = total
        return a_ref[pl.ds(r, streams), :] * total

    lax.fori_loop(0, tokens, scan_step, back_ref[...], unroll=8)
    dconv[pl.ds(rows, lead), :] = jnp.zeros((lead, HEAD_W), f32)

    def gate_step(i, acc):
        r = pl.multiple_of(i * step, step)
        keep = keep_ref[pl.ds(r + lead, step), :]
        decay = decay_ref[...]
        sr, si, raw, e2, m = gate_values(pre[pl.ds(r, step), :], decay, keep)
        g = back[pl.ds(r, step), :]
        conv = conv_ref[pl.ds(r, step), :].astype(f32)
        before = h_ref[pl.ds(jnp.maximum(r - streams, 0), step), :]
        shifted = jnp.concatenate([start_ref[...], before[: step - streams]], axis=0)
        previous = jnp.where(i == 0, shifted, before)
        gsi = g * si
        gm = gsi * m
        dconv[pl.ds(r, step), :] = gm
        d_input = gm * conv * (1.0 - si)
        d_log = g * previous * raw * keep - gsi * conv * keep * e2 / m
        by_rate = d_log * sr
        d_rate = by_rate * decay * (1.0 - sr)
        dpre[pl.ds(r, step), :] = jnp.concatenate([d_rate.astype(bf16), d_input.astype(bf16)], axis=1)
        return acc + jnp.sum(by_rate.reshape(step // 8, 8, HEAD_W), axis=0)

    acc = lax.fori_loop(0, rows // step, gate_step, jnp.zeros((8, HEAD_W), f32))
    ddecay_ref[...] = jnp.sum(acc, axis=0, keepdims=True) * slope_ref[...]
    dgates_ref[0] = lax.dot_general(conv_ref[...], dpre[...], (((0,), (0,)), ((), ())), preferred_element_type=f32)
    pre[:, :HEAD_W] = lax.dot_general(dpre[...], gates_ref[0], (((1,), (1,)), ((), ())), preferred_element_type=f32)
    taps = [taps_ref[pl.ds(k, 1), :] for k in range(CONV)]

    def add_step(i, accs):
        r = pl.multiple_of(i * step, step)
        dc = dconv[pl.ds(r, step), :] + pre[pl.ds(r, step), :HEAD_W]
        dconv[pl.ds(r, step), :] = dc
        out, valid = [], None
        for k in range(CONV):
            term = dc * buf[pl.ds(r + lead - k * streams, step), :]
            if k:
                keep = keep_ref[pl.ds(r + lead - (k - 1) * streams, step), :]
                valid = keep if valid is None else valid * keep
                term = term * valid
            out.append(accs[k] + jnp.sum(term.reshape(step // 8, 8, HEAD_W), axis=0))
        return tuple(out)

    accs = lax.fori_loop(0, rows // step, add_step, tuple(jnp.zeros((8, HEAD_W), f32) for _ in range(CONV)))
    for k in range(CONV):
        dtaps_ref[pl.ds(k, 1), :] = jnp.sum(accs[k], axis=0, keepdims=True)

    def stream_rows(r, count):
        total = taps[0] * dconv[pl.ds(r, count), :]
        valid = None
        for k in range(1, CONV):
            keep = keep_ref[pl.ds(r + lead + k * streams, count), :]
            valid = keep if valid is None else valid * keep
            total = total + taps[k] * dconv[pl.ds(r + k * streams, count), :] * valid
        return total

    def stream_step(i, _):
        r = pl.multiple_of(i * step, step)
        buf[pl.ds(r, step), :] = stream_rows(r, step)
        return 0

    lax.fori_loop(0, rows // step, stream_step, 0)
    tail_ref[...] = buf[pl.ds(rows - lead, lead), :]
    for b in range(streams):
        ds_ref[pl.ds(b * tokens, tokens), :] = buf[pl.ds(b, tokens, stride=streams), :].astype(bf16)
    for j in range(REACH):
        total = None
        valid = None
        for k in range(1, CONV):
            at = j + k - REACH
            keep = keep_ref[pl.ds((j + k) * streams, streams), :]
            valid = keep if valid is None else valid * keep
            if at >= 0:
                term = taps[k] * dconv[pl.ds(at * streams, streams), :] * valid
                total = term if total is None else total + term
        head_ref[pl.ds(j * streams, streams), :] = total


def by_head(rows):
    return pl.BlockSpec((rows, HEAD_W), lambda h: (0, h))


def whole(rows):
    return pl.BlockSpec((rows, HEAD_W), lambda h: (0, 0))


def params():
    return pltpu.CompilerParams(vmem_limit_bytes=40 * 2**20, dimension_semantics=("arbitrary",))


def mix(streams, stream, halo, keep, taps, decay, gates):
    rows, width = stream.shape
    tokens, heads, lead = rows // streams, width // HEAD_W, REACH * streams
    two = pl.BlockSpec((2, streams, HEAD_W), lambda h: (0, 0, h))
    shape = jax.ShapeDtypeStruct
    return pl.pallas_call(
        functools.partial(mix_kernel, streams, tokens),
        grid=(heads,),
        in_specs=[
            by_head(rows), by_head(lead), whole(keep.shape[0]), by_head(CONV), by_head(1),
            pl.BlockSpec((1, HEAD_W, 2 * HEAD_W), lambda h: (h, 0, 0)),
        ],
        out_specs=[by_head(rows), by_head(rows), by_head(rows), two],
        out_shape=[
            shape((rows, width), f32), shape((rows, width), f32), shape((rows, width), bf16), shape((2, streams, width), f32),
        ],
        scratch_shapes=[pltpu.VMEM((rows + lead, HEAD_W), f32), pltpu.VMEM((rows, 2 * HEAD_W), f32)],
        compiler_params=params(),
        cost_estimate=pl.CostEstimate(flops=rows * width * 600, bytes_accessed=rows * width * 12, transcendentals=rows * width * 6),
    )(stream, halo, keep, taps, decay, gates)


def states(streams, a, driven, start, branch):
    rows, width = a.shape
    tokens, heads = rows // streams, width // HEAD_W
    shape = jax.ShapeDtypeStruct
    return pl.pallas_call(
        functools.partial(state_kernel, streams, tokens),
        grid=(heads,),
        in_specs=[by_head(rows), by_head(rows), by_head(streams), by_head(rows)],
        out_specs=[by_head(rows), by_head(rows)],
        out_shape=[shape((rows, width), f32), shape((rows, width), bf16)],
        compiler_params=params(),
        cost_estimate=pl.CostEstimate(flops=rows * width * 30, bytes_accessed=rows * width * 18, transcendentals=rows * width),
    )(a, driven, start, branch)


def states_back(streams, d_merged, branch, a, h):
    rows, width = a.shape
    tokens, heads = rows // streams, width // HEAD_W
    shape = jax.ShapeDtypeStruct
    return pl.pallas_call(
        functools.partial(state_back_kernel, streams, tokens),
        grid=(heads,),
        in_specs=[by_head(rows)] * 4,
        out_specs=[by_head(rows), by_head(rows), by_head(streams)],
        out_shape=[shape((rows, width), f32), shape((rows, width), bf16), shape((streams, width), f32)],
        compiler_params=params(),
        cost_estimate=pl.CostEstimate(flops=rows * width * 40, bytes_accessed=rows * width * 22, transcendentals=rows * width),
    )(d_merged, branch, a, h)


def mix_back(streams, dh, a, h, start, back, conv, stream, halo, keep, taps, decay, slope, gates):
    rows, width = a.shape
    tokens, heads, lead = rows // streams, width // HEAD_W, REACH * streams
    shape = jax.ShapeDtypeStruct
    gate_spec = pl.BlockSpec((1, HEAD_W, 2 * HEAD_W), lambda h: (h, 0, 0))
    return pl.pallas_call(
        functools.partial(mix_back_kernel, streams, tokens),
        grid=(heads,),
        in_specs=[
            by_head(rows), by_head(rows), by_head(rows), by_head(streams), by_head(streams), by_head(rows), by_head(rows),
            by_head(lead), whole(keep.shape[0]), by_head(CONV), by_head(1), by_head(1), gate_spec,
        ],
        out_specs=[by_head(rows), by_head(lead), by_head(lead), gate_spec, by_head(CONV), by_head(1)],
        out_shape=[
            shape((rows, width), bf16), shape((lead, width), f32), shape((lead, width), f32),
            shape((heads, HEAD_W, 2 * HEAD_W), f32), shape((CONV, width), f32), shape((1, width), f32),
        ],
        scratch_shapes=[
            pltpu.VMEM((rows + lead, HEAD_W), f32), pltpu.VMEM((rows, 2 * HEAD_W), f32), pltpu.VMEM((rows, HEAD_W), f32),
            pltpu.VMEM((rows, 2 * HEAD_W), bf16), pltpu.VMEM((rows + lead, HEAD_W), f32),
        ],
        compiler_params=params(),
        cost_estimate=pl.CostEstimate(flops=rows * width * 1200, bytes_accessed=rows * width * 22, transcendentals=rows * width * 6),
    )(dh, a, h, start, back, conv, stream, halo, keep, taps, decay, slope, gates)


def head_columns(block):
    rows, width = block.shape
    groups = width // (TP * HEAD_W)
    return block.reshape(rows, groups, TP, HEAD_W).transpose(2, 0, 1, 3).reshape(TP, rows, width // TP)


def head_back_kernel(groups, pieces_ref, gelu_ref, stream_ref):
    half = groups * HEAD_W
    for w in range(TP):
        for g in range(groups):
            to = (g * TP + w) * HEAD_W
            gelu_ref[:, to : to + HEAD_W] = pieces_ref[w, :, g * HEAD_W : (g + 1) * HEAD_W].astype(f32)
            stream_ref[:, to : to + HEAD_W] = pieces_ref[w, :, half + g * HEAD_W : half + (g + 1) * HEAD_W].astype(f32)


def head_columns_back(pieces):
    _, rows, width = pieces.shape
    groups = (width - HEAD_W) // (2 * HEAD_W)
    out = jax.ShapeDtypeStruct((rows, TP * groups * HEAD_W), f32)
    return pl.pallas_call(
        functools.partial(head_back_kernel, groups), out_shape=[out, out],
        compiler_params=pltpu.CompilerParams(vmem_limit_bytes=24 * 2**20),
        cost_estimate=pl.CostEstimate(flops=rows * width * 8, bytes_accessed=rows * width * 40, transcendentals=0),
    )(pieces)


def ff_back_kernel(n, pieces_ref, gate_ref, up_ref):
    part = gate_ref.shape[1] // (n * TP)
    half = n * part
    for w in range(TP):
        for s in range(n):
            to = (s * TP + w) * part
            gate_ref[:, to : to + part] = pieces_ref[w, :, s * part : (s + 1) * part].astype(f32)
            up_ref[:, to : to + part] = pieces_ref[w, :, half + s * part : half + (s + 1) * part].astype(f32)


def ff_columns_back(pieces):
    n = lax.axis_size("seq")
    _, rows, width = pieces.shape
    out = jax.ShapeDtypeStruct((rows, TP * width // 2), f32)
    return pl.pallas_call(
        functools.partial(ff_back_kernel, n), out_shape=[out, out],
        compiler_params=pltpu.CompilerParams(vmem_limit_bytes=24 * 2**20),
        cost_estimate=pl.CostEstimate(flops=rows * width * 8, bytes_accessed=rows * width * 40, transcendentals=0),
    )(pieces)


def ff_kernel(n, gate_ref, up_ref, out_ref):
    part = gate_ref.shape[1] // (n * TP)
    half = n * part
    for w in range(TP):
        for s in range(n):
            at = (s * TP + w) * part
            out_ref[w, :, s * part : (s + 1) * part] = gate_ref[:, at : at + part]
            out_ref[w, :, half + s * part : half + (s + 1) * part] = up_ref[:, at : at + part]


def ff_columns(gate, up):
    rows, width = gate.shape
    return pl.pallas_call(
        functools.partial(ff_kernel, lax.axis_size("seq")),
        out_shape=jax.ShapeDtypeStruct((TP, rows, 2 * width // TP), bf16),
        compiler_params=pltpu.CompilerParams(vmem_limit_bytes=24 * 2**20),
        cost_estimate=pl.CostEstimate(flops=rows * width * 8, bytes_accessed=rows * width * 8, transcendentals=0),
    )(gate, up)


class Weights:
    def __init__(self, shards, layer):
        self.shards = [s[layer] for s in shards]
        self.buffers = {}
        self.flip = bool(layer % 2)

    def slot(self, name, shape):
        n = lax.axis_size("seq")
        if name not in self.buffers:
            self.buffers[name] = jnp.zeros((n,) + shape, bf16)

    def put(self, name, block, at, column=0):
        self.buffers[name] = lax.dynamic_update_slice(self.buffers[name], block[None], (at, 0, column))

    def prepare_first(self):
        (mix_gain, proj_gelu, proj_stream, conv_taps, lru_gates, decay_param, _, mlp_gain, _, _, _) = self.shards
        rp = proj_gelu.shape[0]
        gr = lru_gates.shape[0] // TP
        small = jnp.concatenate([mix_gain, mlp_gain, conv_taps.reshape(-1), decay_param])
        top = jnp.pad(small, (0, (rp - gr) * HEAD_W - small.shape[0])).reshape(rp - gr, HEAD_W)
        extra = jnp.concatenate([top, jnp.zeros((gr, HEAD_W), bf16)])
        pieces = jnp.concatenate(
            [head_columns(proj_gelu), head_columns(proj_stream), jnp.broadcast_to(extra, (TP, rp, HEAD_W))], axis=2
        )
        got = jnp.stack(wt_exchange(pieces))
        gates = to_heads(lru_gates).reshape(TP, gr, HEAD_W)
        width = got.shape[2] - HEAD_W
        self.first_block = lax.dynamic_update_slice(got, gates, (0, rp - gr, width)).reshape(TP * rp, width + HEAD_W)
        return self.first_block

    def prepare_out(self):
        self.out_block = to_heads(self.shards[6])

    def prepare_wide(self):
        proj_gate, proj_up = self.shards[8], self.shards[9]
        wide = jnp.stack(wt_exchange(ff_columns(proj_gate, proj_up)))
        self.wide_block = wide.reshape(TP * proj_gate.shape[0], -1)

    def first_job(self):
        self.slot("first", self.first_block.shape)
        return GatherJob(self.first_block, self.flip, lambda block, at: self.put("first", block, at))

    def out_job(self):
        self.slot("out", self.out_block.shape)
        return GatherJob(self.out_block, not self.flip, lambda block, at: self.put("out", block, at))

    def gather_down(self):
        self.down = lax.all_gather(self.shards[10], "seq", tiled=True)

    def gather_wide(self):
        self.wide = lax.all_gather(self.wide_block, "seq", tiled=True)

    def open_first(self, sizes):
        rp, gr, cp, fb = sizes
        first = self.buffers["first"]
        w = lax.axis_index("wt")
        n = first.shape[0]
        depth = n * TP * rp
        width = first.shape[2] - HEAD_W
        flat = first.reshape(depth, width + HEAD_W)
        extra = flat[:, width:].reshape(n * TP, rp, HEAD_W)
        small = extra[:, : rp - gr].reshape(n * TP, -1)
        at = 2 * rp

        def own_heads(v):
            v = v.reshape(v.shape[0], -1, TP, HEAD_W)
            return lax.dynamic_index_in_dim(v, w, 2, keepdims=False).reshape(v.shape[0], -1).astype(f32)

        self.taps = own_heads(small[:, at : at + CONV * cp].reshape(n * TP, CONV, cp).transpose(1, 0, 2).reshape(CONV, -1))
        decay = own_heads(small[:, at + CONV * cp : at + (CONV + 1) * cp].reshape(1, -1))
        gates = extra[:, rp - gr :].reshape(2, -1, HEAD_W, HEAD_W).transpose(1, 2, 0, 3)
        self.gates = gates.reshape(-1, HEAD_W, 2 * HEAD_W)
        self.mix_gain = small[:, :rp].reshape(-1).astype(f32)
        self.mlp_gain = small[:, rp : 2 * rp].reshape(-1).astype(f32)
        self.decay, self.slope = -DECAY * jax.nn.softplus(decay), -DECAY * jax.nn.sigmoid(decay)
        self.gelu, self.stream = flat[:, : width // 2], flat[:, width // 2 : width]


def forward_block(x, normed, keep, streams, wts, pump, following):
    width = x.shape[1]
    if normed is None:
        normed = tp_gather(rms_norm(x, wts.mix_gain).astype(bf16))
    tokens = normed.shape[0] // streams
    last = normed.reshape(streams, tokens, width)[:, tokens - REACH :].transpose(1, 0, 2)
    halo_in = shift_seq(last.reshape(REACH * streams, width), 1)
    stream = dot(normed, wts.stream, bf16)
    halo = dot(halo_in, wts.stream, bf16).astype(f32)
    a, driven, conv, ends = mix(streams, stream, halo, keep, wts.taps, wts.decay, wts.gates)
    branch = dot(normed, wts.gelu)
    start = carry_in(ends[0], ends[1], 1)
    h, merged = states(streams, a, driven, start, branch)
    wts.out = wts.buffers["out"].reshape(-1, width)
    if following is not None:
        pump.add(following.first_job(), following.out_job())
        merged = pump.step(merged)
    mixed = tp_scatter(lambda rows: dot(rows, wts.out, bf16), merged)
    mixed, wts.wide = tie(mixed, wts.wide)
    mixed = pump.step(mixed)
    x1 = x + mixed
    mlp_in = tp_gather(rms_norm(x1, wts.mlp_gain).astype(bf16))
    mlp_in = pump.step(mlp_in)
    wide = pump.step(dot(mlp_in, wts.wide))
    half = wide.shape[1] // 2
    product = (gelu(wide[:, :half]) * wide[:, half:]).astype(bf16)
    kept = dict(
        x=x, normed=normed, stream=stream, branch=branch, halo=halo, a=a, conv=conv, whole=ends[0], start=start, h=h,
        merged=merged, x1=x1, mlp_in=mlp_in, wide=wide, product=product,
    )
    return kept


def block_end(kept, wts):
    product = kept["product"]
    width = kept["x1"].shape[1]
    return kept["x1"] + tp_scatter(lambda rows: dot(rows, wts.down, bf16), product)


def mlp_back(gx, g_down, wts, kept, results, rp, pump, above):
    width = gx.shape[1]
    n = lax.axis_size("seq")
    grad_down = dot_tokens(kept["product"], g_down)
    g_down, grad_down = tie(g_down, grad_down)
    d_product = dot_t(g_down, wts.down)
    wide = kept["wide"]
    half = wide.shape[1] // 2
    value, slope = gelu_and_slope(wide[:, :half])
    d_wide = jnp.concatenate([(d_product * wide[:, half:] * slope).astype(bf16), (d_product * value).astype(bf16)], axis=1)
    grad_wide = dot_tokens(kept["mlp_in"], d_wide).reshape(n, -1, 2 * half)
    d_wide, grad_wide, grad_down = tie(d_wide, grad_wide, grad_down)
    if above is not None:
        d_wide, above["wide"] = tie(d_wide, above["wide"])
    d_mlp_in = tp_scatter(lambda rows: dot_t(rows, wts.wide, bf16), pump.step(d_wide))
    results["wide"] = lax.psum_scatter(grad_wide, "seq", scatter_dimension=0)
    if above is not None:
        d_mlp_in, grad_down = tie(d_mlp_in, grad_down)
    results["down"] = lax.psum_scatter(grad_down.reshape(n, -1, width), "seq", scatter_dimension=0).astype(f32)
    dv, d_gain = rms_norm_back(kept["x1"], wts.mlp_gain, d_mlp_in)
    return gx + dv, d_gain


def mixer_back(d_x1, keep, streams, wts, kept, d_mlp_gain, d_mix_gain, sizes, results, pump, end=None):
    rp, gr, cp, fb = sizes
    width = d_x1.shape[1]
    n, w = lax.axis_size("seq"), lax.axis_index("wt")
    g_branch = tp_gather(d_x1.astype(bf16))
    d_merged = dot_t(g_branch, wts.out)
    grad_out = dot_tokens(kept["merged"], g_branch)
    dh, d_branch, ends = states_back(streams, d_merged, kept["branch"], kept["a"], kept["h"])
    if end is not None:
        ends = end(ends)
    ends = pump.hold(ends)
    back = carry_in(kept["whole"], ends, -1)
    back = pump.step(back)
    d_stream, tail, head, d_gates, d_taps, d_decay = mix_back(
        streams, dh, kept["a"], kept["h"], kept["start"], back, kept["conv"], kept["stream"], kept["halo"], keep,
        wts.taps, wts.decay, wts.slope, wts.gates,
    )
    tail = (tail + shift_seq(head, -1)).astype(bf16)
    tokens = d_stream.shape[0] // streams
    d_stream = lax.dynamic_update_slice(
        d_stream.reshape(streams, tokens, -1), tail.reshape(REACH, streams, -1).transpose(1, 0, 2), (0, tokens - REACH, 0)
    ).reshape(d_stream.shape)

    def full(v):
        lines = v.reshape(v.shape[0], -1, 1, HEAD_W)
        return jnp.where(lax.iota(jnp.int32, TP)[None, None, :, None] == w, lines, 0.0).reshape(v.shape[0], n * TP, -1)

    small = jnp.concatenate(
        [
            d_mix_gain.reshape(n * TP, rp), d_mlp_gain.reshape(n * TP, rp),
            full(d_taps).transpose(1, 0, 2).reshape(n * TP, -1), full(d_decay)[0],
        ],
        axis=1,
    ).astype(bf16)
    small = jnp.pad(small, ((0, 0), (0, (rp - gr) * HEAD_W - small.shape[1]))).reshape(n * TP, rp - gr, HEAD_W)
    gates = d_gates.reshape(-1, HEAD_W, 2, HEAD_W).transpose(2, 0, 1, 3).reshape(n * TP, gr, HEAD_W).astype(bf16)
    extra = jnp.concatenate([small, gates], axis=1).reshape(n, TP * rp, HEAD_W)
    grad_gelu = dot_tokens(kept["normed"], d_branch).reshape(n, TP * rp, -1)
    grad_stream = dot_tokens(kept["normed"], d_stream).reshape(n, TP * rp, -1)

    both = ScatterJob(
        jnp.concatenate([grad_gelu, grad_stream, extra], axis=2), False, lambda total: results.update(raw=total)
    )
    if end is None:
        d_stream, results["wide"] = tie(d_stream, results["wide"])
    pump.add(
        both,
        ScatterJob(grad_out.reshape(n, -1, width), True, lambda total: results.update(out=from_heads(total))),
    )
    d_normed = tp_scatter(
        lambda branch, stream: (dot_t(branch, wts.gelu) + dot_t(stream, wts.stream)).astype(bf16), d_branch, pump.step(d_stream)
    )
    if end is None:
        d_normed = pump.step(d_normed)
    dv, d_gain = rms_norm_back(kept["x"], wts.mix_gain, d_normed)
    return d_x1 + dv, d_gain, both


def finish_both(raw, results, above, sizes):
    rp, gr, cp, fb = sizes
    width = raw.shape[1] - HEAD_W
    results["gates"] = from_heads(raw.reshape(TP, rp, -1)[:, rp - gr :, width:].reshape(TP * gr, HEAD_W))
    pieces = jnp.stack(wt_exchange(raw.astype(bf16).reshape(TP, rp, -1)))
    results["gelu"], results["stream"] = head_columns_back(pieces)
    sums = jnp.sum(pieces[:, : rp - gr, width:].astype(f32), axis=0).reshape(-1)
    above["mix_gain"], results["mlp_gain"] = sums[:rp], sums[rp : 2 * rp]
    results["taps"] = sums[2 * rp : 2 * rp + CONV * cp].reshape(CONV, cp)
    results["decay"] = sums[2 * rp + CONV * cp : 2 * rp + (CONV + 1) * cp]


def per_device(block_in, start_flags, out_grad, *shards):
    layers = shards[0].shape[0]
    micro, _, tokens, width = block_in.shape
    streams = micro * TP
    sizes = (shards[1].shape[1], shards[4].shape[1] // TP, shards[5].shape[1], shards[10].shape[1])
    rp = sizes[0]

    weights = [Weights(shards, layer) for layer in range(layers)]
    zero, pump = weights[0], Pump()
    zero.prepare_first()
    zero.prepare_out()
    pump.add(zero.first_job(), zero.out_job())
    rest = [w.shards for w in weights]
    block_in, start_flags, out_grad, rest = pump.step((block_in, start_flags, out_grad, rest))
    for w, shards_then in zip(weights, rest):
        w.shards = shards_then
    flags = tp_gather(start_flags[:, 0].astype(f32))
    x_in = block_in[:, 0].reshape(micro * tokens, width)
    grad = out_grad[:, 0].reshape(micro * tokens, width)
    x_all = tp_gather(x_in)
    keep = 1.0 - flags.T
    behind = 1.0 - shift_seq(flags[:, tokens - REACH :].T, 1)
    keep = jnp.concatenate([behind, keep, jnp.ones((REACH, streams), f32)]).reshape(-1, 1)
    keep = jnp.broadcast_to(keep, (keep.shape[0], HEAD_W))

    x = x_in.astype(f32)
    kept = []
    zero.prepare_wide()
    for _ in range(3):
        zero.wide_block = pump.step(zero.wide_block)
    zero.wide_block, x_all, rest = pump.step((zero.wide_block, x_all, [w.shards for w in weights]))
    pump.finish()
    zero.gather_wide()
    for w, shards_then in zip(weights, rest):
        w.shards = shards_then
    zero.gather_down()
    for wts in weights[1:]:
        wts.prepare_first()
        wts.prepare_out()
        wts.prepare_wide()
        wts.gather_wide()
        wts.gather_down()
    for layer in range(layers):
        wts = weights[layer]
        wts.open_first(sizes)
        normed = rms_norm(x_all.astype(f32), wts.mix_gain).astype(bf16) if layer == 0 else None
        following = weights[layer + 1] if layer < layers - 1 else None
        saved = forward_block(x, normed, keep, streams, wts, pump, following)
        if layer < layers - 1:
            x = pump.step(block_end(saved, wts))
            pump.finish()
        kept.append(saved)
        if layer == 0:
            grad_then, saved["wide"] = tie(grad, saved["wide"])
            g_down = tp_gather(grad_then)

    gx = grad.astype(f32)
    d_mix = jnp.zeros((width,), f32)
    results = [dict() for _ in range(layers)]
    spare, outcome, jobs = {}, [], []

    def last(ends):
        ends, kept[-1]["product"] = tie(ends, kept[-1]["product"])
        outcome.append(block_end(kept[-1], weights[-1]))
        return ends

    for layer in reversed(range(layers)):
        if layer != layers - 1:
            g_down = tp_gather(gx.astype(bf16))
            g_down, results[layer + 1]["down"] = tie(g_down, results[layer + 1]["down"])
        d_x1, d_mlp = mlp_back(
            gx, g_down, weights[layer], kept[layer], results[layer], rp, pump, results[layer + 1] if layer < layers - 1 else None
        )
        gx, d_mix, both = mixer_back(
            d_x1, keep, streams, weights[layer], kept[layer], d_mlp, d_mix, sizes, results[layer], pump, last if layer == layers - 1 else None
        )
        jobs.append(both)
    pump.complete(jobs[:-1])
    held = [found.pop("raw") for found in results[1:]]
    wide = [found["wide"] for found in results[1:]]
    held, wide = pump.step(pump.step((held, wide)))
    for layer in range(1, layers):
        results[layer]["wide"] = wide[layer - 1]
    pump.finish()
    for layer in reversed(range(layers)):
        raw = held[layer - 1] if layer else results[0].pop("raw")
        finish_both(raw, results[layer], results[layer + 1] if layer < layers - 1 else spare, sizes)
    for found in results:
        pieces = wt_exchange(found.pop("wide").reshape(TP, rp, -1))
        found["gate"], found["up"] = ff_columns_back(jnp.stack(pieces))
    results[0]["mix_gain"] = vector_scatter(d_mix.reshape(-1, TP, rp))
    shape = (micro, 1, tokens, width)
    names = ("mix_gain", "gelu", "stream", "taps", "gates", "decay", "out", "mlp_gain", "gate", "up", "down")
    stacked = [jnp.stack([results[layer][k] for layer in range(layers)]) for k in names]
    return (outcome[0].astype(bf16).reshape(shape), gx.astype(bf16).reshape(shape), *stacked)


def solution(mesh):
    both = ("seq", "wt")
    tokens = P(None, "wt", "seq", None)
    vector, matrix = P(None, both), P(None, both, None)
    weights = (vector, matrix, matrix, P(None, None, both), matrix, vector, matrix, vector, matrix, matrix, matrix)
    return jax.shard_map(
        per_device,
        mesh=mesh,
        in_specs=(tokens, P(None, "wt", "seq"), tokens, *weights),
        out_specs=(tokens, tokens, *weights),
        check_vma=False,
    )
```

```python
import functools

import jax
import jax.numpy as jnp
from jax import lax
from jax.experimental import pallas as pl
from jax.experimental.pallas import tpu as pltpu
from jax.sharding import PartitionSpec as P

f32 = jnp.float32
bf16 = jnp.bfloat16
HEAD_W = 128
CONV = 4
REACH = CONV - 1
TP = 4
EPS = 1e-06
DECAY = 8.0
GELU_C = 0.7978845608
GELU_K = 0.044715


def dot(left, right, out=f32):
    return lax.dot_general(left, right, (((1,), (0,)), ((), ())), preferred_element_type=f32).astype(out)


def dot_t(left, right, out=f32):
    return lax.dot_general(left, right, (((1,), (1,)), ((), ())), preferred_element_type=f32).astype(out)


def dot_tokens(left, right, out=bf16):
    return lax.dot_general(left, right, (((0,), (0,)), ((), ())), preferred_element_type=f32).astype(out)


def sigmoid(v):
    return 1.0 / (1.0 + jnp.exp(-v))


def gelu(v):
    return 0.5 * v * (1.0 + jnp.tanh(GELU_C * (v + GELU_K * v * v * v)))


def gelu_and_slope(v):
    square = v * v
    t = jnp.tanh(GELU_C * v * (1.0 + GELU_K * square))
    value = 0.5 * v * (1.0 + t)
    slope = 0.5 * (1.0 + t) + 0.5 * v * (1.0 - t * t) * GELU_C * (1.0 + 3.0 * GELU_K * square)
    return value, slope


def minus_expm1(y, e):
    series = -y * (1.0 + y * (1 / 2) * (1.0 + y * (1 / 3) * (1.0 + y * (1 / 4) * (1.0 + y * (1 / 5) * (1.0 + y * (1 / 6))))))
    return jnp.where(y > -0.25, series, 1.0 - e)


def rms_norm(v, gain):
    return v * lax.rsqrt(jnp.mean(v * v, axis=-1, keepdims=True) + EPS) * gain


def rms_norm_back(v, gain, dy):
    r = lax.rsqrt(jnp.mean(v * v, axis=-1, keepdims=True) + EPS)
    dgain = jnp.sum(dy * v * r, axis=0)
    dyg = dy * gain
    dv = r * dyg - v * (r * r * r) * jnp.mean(dyg * v, axis=-1, keepdims=True)
    return dv, dgain


def swap(x, k):
    return lax.ppermute(x, "wt", [(i, i ^ k) for i in range(TP)])


def tp_gather(x):
    far = swap(x, 2)
    near = swap(x, 1)
    diagonal = swap(far, 1)
    return jnp.concatenate([x, near, far, diagonal], axis=0)


def tp_scatter(part):
    far = (part[2].astype(f32) + swap(part[3], 1).astype(f32)).astype(bf16)
    across = swap(far, 2)
    near = swap(part[1], 1)
    return part[0].astype(f32) + near.astype(f32) + across.astype(f32)


def wt_exchange(pieces):
    w = lax.axis_index("wt")
    pick = lambda stack, j: lax.dynamic_index_in_dim(stack, j, 0, keepdims=False)
    got = [pick(pieces, w)] + [swap(pick(pieces, w ^ k), k) for k in range(1, TP)]
    stack = jnp.stack(got)
    return [pick(stack, w ^ j) for j in range(TP)]


def ring_tables():
    n = lax.axis_size("seq")
    order = [0, 1, 3, 5, 7, 6, 4, 2] if n == 8 else list(range(n))
    right = [(order[i], order[(i + 1) % n]) for i in range(n)]
    left = [(b, a) for a, b in right]
    s = lax.axis_index("seq")
    if n == 8:
        position = jnp.where(s % 2 == 1, s // 2 + 1, (8 - s // 2) % 8)
        owner = lambda p: jnp.where(p == 0, 0, jnp.where(p <= 4, 2 * p - 1, 16 - 2 * p))
    else:
        position, owner = s, lambda p: p
    device = lambda offset: owner(lax.rem(position + offset + n, n))
    return n, right, left, device


class GatherJob:
    def __init__(self, block, flip, place):
        self.n, right, left, self.device = ring_tables()
        self.routes = (left, right) if flip else (right, left)
        self.sign = -1 if flip else 1
        self.a = self.b = block
        self.hop, self.place = 0, place
        self.place(block, self.device(0))
        self.done = False

    def start(self):
        self.hop += 1
        flight = [lax.ppermute(self.a, "seq", self.routes[0])]
        if self.hop <= self.n - 1 - self.n // 2:
            flight.append(lax.ppermute(self.b, "seq", self.routes[1]))
        return flight

    def bytes(self):
        return self.a.size * 2

    def receive(self, flight):
        self.a = flight[0]
        self.place(self.a, self.device(-self.sign * self.hop))
        if len(flight) > 1:
            self.b = flight[1]
            self.place(self.b, self.device(self.sign * self.hop))
        self.done = self.hop == self.n // 2


class ScatterJob:
    def __init__(self, stack, flip, finish):
        self.n, right, left, self.device = ring_tables()
        self.routes = (left, right) if flip else (right, left)
        self.sign = -1 if flip else 1
        self.stack, self.finish = stack, finish
        self.far, self.near = self.n // 2, self.n - 1 - self.n // 2
        self.a, self.b = self.chunk(self.far), self.chunk(-self.near)
        self.hop, self.done = 0, False

    def chunk(self, k):
        return lax.dynamic_index_in_dim(self.stack, self.device(self.sign * k), 0, keepdims=False)

    def bytes(self):
        return self.a.size * 2

    def start(self):
        self.hop += 1
        flight = [lax.ppermute(self.a, "seq", self.routes[0])]
        if self.hop <= self.near:
            flight.append(lax.ppermute(self.b, "seq", self.routes[1]))
        return flight

    def receive(self, flight):
        add = lambda x, y: (x.astype(f32) + y.astype(f32)).astype(bf16)
        self.a = flight[0]
        if self.hop < self.far:
            self.a = add(self.a, self.chunk(self.far - self.hop))
        if len(flight) > 1:
            self.b = flight[1]
            if self.hop < self.near:
                self.b = add(self.b, self.chunk(self.hop - self.near))
        if self.hop == self.far:
            self.done = True
            self.finish(self.chunk(0).astype(f32) + self.a.astype(f32) + self.b.astype(f32))


def tie(*values):
    return lax.optimization_barrier(values)


def run(job):
    while not job.done:
        job.receive(job.start())


class Pump:
    def __init__(self):
        self.waiting, self.active = [], []

    def add(self, *jobs):
        self.waiting += jobs

    def hold(self, value):
        flights = [flight for _, flight in self.active]
        if flights:
            value, flights = lax.optimization_barrier((value, flights))
        for (job, _), flight in zip(self.active, flights):
            job.receive(flight)
            if not job.done:
                self.waiting.append(job)
        self.active = []
        return value

    def step(self, value):
        flights = [flight for _, flight in self.active]
        heads = [(job.a, job.b) for job in self.waiting]
        if flights or heads:
            value, flights, heads = lax.optimization_barrier((value, flights, heads))
        moved = []
        for (job, _), flight in zip(self.active, flights):
            job.receive(flight)
            if not job.done:
                moved.append(job)
        for job, (a, b) in zip(self.waiting, heads):
            job.a, job.b = a, b
            moved.append(job)
        self.waiting = []
        self.active = [(job, job.start()) for job in moved]
        return value

    def complete(self, jobs):
        for job, flight in self.active:
            if job in jobs:
                job.receive(flight)
        self.active = [(job, flight) for job, flight in self.active if job not in jobs]
        self.waiting = [job for job in self.waiting if job not in jobs]
        for job in jobs:
            run(job)

    def finish(self):
        for job, flight in self.active:
            job.receive(flight)
            run(job)
        for job in self.waiting:
            run(job)
        self.active, self.waiting = [], []


def shift_seq(x, distance):
    n = lax.axis_size("seq")
    return lax.ppermute(x, "seq", [(i, i + distance) for i in range(n) if 0 <= i + distance < n])


def carry_in(decay, state, direction):
    n = lax.axis_size("seq")
    width = decay.shape[-1]
    inclusive = jnp.concatenate([decay, state], axis=-1)

    def then(near, far):
        return jnp.concatenate(
            [near[:, :width] * far[:, :width], near[:, width:] + near[:, :width] * far[:, width:]], axis=-1
        )

    reach, covered, total = 1, 0, None
    while covered < n - 1:
        first = shift_seq(inclusive, direction * reach)
        second = shift_seq(inclusive, direction * 2 * reach) if covered + reach < n - 1 else None
        both = first if second is None else then(first, second)
        total = both if total is None else then(total, both)
        covered += 2 * reach if second is not None else reach
        inclusive = then(inclusive, both)
        reach *= 3
    return total[:, width:]


def head_route(rows):
    n = lax.axis_size("seq")
    per = HEAD_W // rows
    route = []
    for s in range(n):
        base = s // per * per
        for w in range(TP):
            b = TP * (s - base) + w
            route.append((s * TP + w, (base + b % per) * TP + b // per))
    return route


def to_heads(x):
    route = head_route(x.shape[0])
    return x if all(a == b for a, b in route) else lax.ppermute(x, ("seq", "wt"), route)


def from_heads(x):
    route = head_route(x.shape[0])
    return x if all(a == b for a, b in route) else lax.ppermute(x, ("seq", "wt"), [(b, a) for a, b in route])


def vector_scatter(v):
    w, s = lax.axis_index("wt"), lax.axis_index("seq")
    pick = lambda x, j, ax: lax.dynamic_index_in_dim(x, j, ax, keepdims=False)
    n, _, k = v.shape
    v = v.reshape(n, 2, 2, k)
    hi, lo = w >> 1, w & 1
    v = pick(v, hi, 1) + swap(pick(v, 1 - hi, 1), 2)
    v = pick(v, lo, 1) + swap(pick(v, 1 - lo, 1), 1)
    half = n // 2
    while half:
        v = v.reshape(2, half, k)
        bit = (s // half) % 2
        other = lax.ppermute(pick(v, 1 - bit, 0), "seq", [(i, i ^ half) for i in range(n)])
        v = pick(v, bit, 0) + other
        half //= 2
    return v.reshape(k)


def lay_stream(buf, src, streams, tokens, lead):
    for b in range(streams):
        buf[pl.ds(lead + b, tokens, stride=streams), :] = src[pl.ds(b * tokens, tokens), :].astype(f32)


def gate_values(pre_rows, decay_row, keep):
    sr = sigmoid(pre_rows[:, :HEAD_W])
    si = sigmoid(pre_rows[:, HEAD_W:])
    log_a = decay_row * sr
    raw = jnp.exp(log_a)
    e2 = raw * raw
    msq = keep * minus_expm1(2.0 * log_a, e2) + (1.0 - keep)
    return sr, si, raw, e2, jnp.sqrt(msq)


def mix_kernel(
    streams, tokens, stream_ref, halo_ref, keep_ref, taps_ref, decay_ref, gates_ref,
    a_ref, d_ref, conv_ref, ends_ref, buf, pre,
):
    lead = REACH * streams
    rows = streams * tokens
    step = 128
    buf[pl.ds(0, lead), :] = halo_ref[...]
    lay_stream(buf, stream_ref, streams, tokens, lead)
    taps = [taps_ref[pl.ds(k, 1), :] for k in range(CONV)]

    def conv_step(i, _):
        r = pl.multiple_of(i * step, step)
        total = taps[0] * buf[pl.ds(r + lead, step), :]
        valid = None
        for k in range(1, CONV):
            keep = keep_ref[pl.ds(r + lead - (k - 1) * streams, step), :]
            valid = keep if valid is None else valid * keep
            total = total + taps[k] * buf[pl.ds(r + lead - k * streams, step), :] * valid
        conv_ref[pl.ds(r, step), :] = total.astype(bf16)
        return 0

    lax.fori_loop(0, rows // step, conv_step, 0)
    pre[...] = jnp.dot(conv_ref[...], gates_ref[0], preferred_element_type=f32)

    def gate_step(i, _):
        r = pl.multiple_of(i * step, step)
        keep = keep_ref[pl.ds(r + lead, step), :]
        _, si, raw, _, m = gate_values(pre[pl.ds(r, step), :], decay_ref[...], keep)
        a_ref[pl.ds(r, step), :] = raw * keep
        d_ref[pl.ds(r, step), :] = m * si * conv_ref[pl.ds(r, step), :].astype(f32)
        return 0

    lax.fori_loop(0, rows // step, gate_step, 0)

    def scan_step(t, carry):
        total, h = carry
        r = pl.multiple_of(t * streams, streams)
        a = a_ref[pl.ds(r, streams), :]
        return total * a, a * h + d_ref[pl.ds(r, streams), :]

    total, h = lax.fori_loop(
        0, tokens, scan_step, (jnp.ones((streams, HEAD_W), f32), jnp.zeros((streams, HEAD_W), f32)), unroll=8
    )
    ends_ref[0] = total
    ends_ref[1] = h


def state_kernel(streams, tokens, a_ref, d_ref, start_ref, branch_ref, h_ref, merged_ref):
    def scan_step(t, h):
        r = pl.multiple_of(t * streams, streams)
        h = a_ref[pl.ds(r, streams), :] * h + d_ref[pl.ds(r, streams), :]
        h_ref[pl.ds(r, streams), :] = h
        return h

    lax.fori_loop(0, tokens, scan_step, start_ref[...], unroll=8)
    for b in range(streams):
        at = pl.ds(b * tokens, tokens)
        h = h_ref[pl.ds(b, tokens, stride=streams), :]
        merged_ref[at, :] = (h * gelu(branch_ref[at, :])).astype(bf16)


def state_back_kernel(streams, tokens, dm_ref, branch_ref, a_ref, h_ref, dh_ref, db_ref, ends_ref):
    for b in range(streams):
        at = pl.ds(b * tokens, tokens)
        dm = dm_ref[at, :]
        value, slope = gelu_and_slope(branch_ref[at, :])
        h = h_ref[pl.ds(b, tokens, stride=streams), :]
        dh_ref[pl.ds(b, tokens, stride=streams), :] = dm * value
        db_ref[at, :] = (dm * h * slope).astype(bf16)

    def scan_step(i, g):
        r = pl.multiple_of((tokens - 1 - i) * streams, streams)
        return a_ref[pl.ds(r, streams), :] * (dh_ref[pl.ds(r, streams), :] + g)

    ends_ref[...] = lax.fori_loop(0, tokens, scan_step, jnp.zeros((streams, HEAD_W), f32), unroll=8)


def mix_back_kernel(
    streams, tokens, dh_ref, a_ref, h_ref, start_ref, back_ref, conv_ref, stream_ref, halo_ref, keep_ref, taps_ref,
    decay_ref, slope_ref, gates_ref,
    ds_ref, tail_ref, head_ref, dgates_ref, dtaps_ref, ddecay_ref,
    buf, pre, back, dpre, dconv,
):
    lead = REACH * streams
    rows = streams * tokens
    step = 128
    buf[pl.ds(0, lead), :] = halo_ref[...]
    lay_stream(buf, stream_ref, streams, tokens, lead)
    pre[...] = jnp.dot(conv_ref[...], gates_ref[0], preferred_element_type=f32)

    def scan_step(i, g):
        r = pl.multiple_of((tokens - 1 - i) * streams, streams)
        total = dh_ref[pl.ds(r, streams), :] + g
        back[pl.ds(r, streams), :] = total
        return a_ref[pl.ds(r, streams), :] * total

    lax.fori_loop(0, tokens, scan_step, back_ref[...], unroll=8)
    dconv[pl.ds(rows, lead), :] = jnp.zeros((lead, HEAD_W), f32)

    def gate_step(i, acc):
        r = pl.multiple_of(i * step, step)
        keep = keep_ref[pl.ds(r + lead, step), :]
        decay = decay_ref[...]
        sr, si, raw, e2, m = gate_values(pre[pl.ds(r, step), :], decay, keep)
        g = back[pl.ds(r, step), :]
        conv = conv_ref[pl.ds(r, step), :].astype(f32)
        before = h_ref[pl.ds(jnp.maximum(r - streams, 0), step), :]
        shifted = jnp.concatenate([start_ref[...], before[: step - streams]], axis=0)
        previous = jnp.where(i == 0, shifted, before)
        gsi = g * si
        gm = gsi * m
        dconv[pl.ds(r, step), :] = gm
        d_input = gm * conv * (1.0 - si)
        d_log = g * previous * raw * keep - gsi * conv * keep * e2 / m
        by_rate = d_log * sr
        d_rate = by_rate * decay * (1.0 - sr)
        dpre[pl.ds(r, step), :] = jnp.concatenate([d_rate.astype(bf16), d_input.astype(bf16)], axis=1)
        return acc + jnp.sum(by_rate.reshape(step // 8, 8, HEAD_W), axis=0)

    acc = lax.fori_loop(0, rows // step, gate_step, jnp.zeros((8, HEAD_W), f32))
    ddecay_ref[...] = jnp.sum(acc, axis=0, keepdims=True) * slope_ref[...]
    dgates_ref[0] = lax.dot_general(conv_ref[...], dpre[...], (((0,), (0,)), ((), ())), preferred_element_type=f32)
    pre[:, :HEAD_W] = lax.dot_general(dpre[...], gates_ref[0], (((1,), (1,)), ((), ())), preferred_element_type=f32)
    taps = [taps_ref[pl.ds(k, 1), :] for k in range(CONV)]

    def add_step(i, accs):
        r = pl.multiple_of(i * step, step)
        dc = dconv[pl.ds(r, step), :] + pre[pl.ds(r, step), :HEAD_W]
        dconv[pl.ds(r, step), :] = dc
        out, valid = [], None
        for k in range(CONV):
            term = dc * buf[pl.ds(r + lead - k * streams, step), :]
            if k:
                keep = keep_ref[pl.ds(r + lead - (k - 1) * streams, step), :]
                valid = keep if valid is None else valid * keep
                term = term * valid
            out.append(accs[k] + jnp.sum(term.reshape(step // 8, 8, HEAD_W), axis=0))
        return tuple(out)

    accs = lax.fori_loop(0, rows // step, add_step, tuple(jnp.zeros((8, HEAD_W), f32) for _ in range(CONV)))
    for k in range(CONV):
        dtaps_ref[pl.ds(k, 1), :] = jnp.sum(accs[k], axis=0, keepdims=True)

    def stream_rows(r, count):
        total = taps[0] * dconv[pl.ds(r, count), :]
        valid = None
        for k in range(1, CONV):
            keep = keep_ref[pl.ds(r + lead + k * streams, count), :]
            valid = keep if valid is None else valid * keep
            total = total + taps[k] * dconv[pl.ds(r + k * streams, count), :] * valid
        return total

    def stream_step(i, _):
        r = pl.multiple_of(i * step, step)
        buf[pl.ds(r, step), :] = stream_rows(r, step)
        return 0

    lax.fori_loop(0, rows // step, stream_step, 0)
    tail_ref[...] = buf[pl.ds(rows - lead, lead), :]
    for b in range(streams):
        ds_ref[pl.ds(b * tokens, tokens), :] = buf[pl.ds(b, tokens, stride=streams), :].astype(bf16)
    for j in range(REACH):
        total = None
        valid = None
        for k in range(1, CONV):
            at = j + k - REACH
            keep = keep_ref[pl.ds((j + k) * streams, streams), :]
            valid = keep if valid is None else valid * keep
            if at >= 0:
                term = taps[k] * dconv[pl.ds(at * streams, streams), :] * valid
                total = term if total is None else total + term
        head_ref[pl.ds(j * streams, streams), :] = total


def by_head(rows):
    return pl.BlockSpec((rows, HEAD_W), lambda h: (0, h))


def whole(rows):
    return pl.BlockSpec((rows, HEAD_W), lambda h: (0, 0))


def params():
    return pltpu.CompilerParams(vmem_limit_bytes=40 * 2**20, dimension_semantics=("arbitrary",))


def mix(streams, stream, halo, keep, taps, decay, gates):
    rows, width = stream.shape
    tokens, heads, lead = rows // streams, width // HEAD_W, REACH * streams
    two = pl.BlockSpec((2, streams, HEAD_W), lambda h: (0, 0, h))
    shape = jax.ShapeDtypeStruct
    return pl.pallas_call(
        functools.partial(mix_kernel, streams, tokens),
        grid=(heads,),
        in_specs=[
            by_head(rows), by_head(lead), whole(keep.shape[0]), by_head(CONV), by_head(1),
            pl.BlockSpec((1, HEAD_W, 2 * HEAD_W), lambda h: (h, 0, 0)),
        ],
        out_specs=[by_head(rows), by_head(rows), by_head(rows), two],
        out_shape=[
            shape((rows, width), f32), shape((rows, width), f32), shape((rows, width), bf16), shape((2, streams, width), f32),
        ],
        scratch_shapes=[pltpu.VMEM((rows + lead, HEAD_W), f32), pltpu.VMEM((rows, 2 * HEAD_W), f32)],
        compiler_params=params(),
        cost_estimate=pl.CostEstimate(flops=rows * width * 600, bytes_accessed=rows * width * 12, transcendentals=rows * width * 6),
    )(stream, halo, keep, taps, decay, gates)


def states(streams, a, driven, start, branch):
    rows, width = a.shape
    tokens, heads = rows // streams, width // HEAD_W
    shape = jax.ShapeDtypeStruct
    return pl.pallas_call(
        functools.partial(state_kernel, streams, tokens),
        grid=(heads,),
        in_specs=[by_head(rows), by_head(rows), by_head(streams), by_head(rows)],
        out_specs=[by_head(rows), by_head(rows)],
        out_shape=[shape((rows, width), f32), shape((rows, width), bf16)],
        compiler_params=params(),
        cost_estimate=pl.CostEstimate(flops=rows * width * 30, bytes_accessed=rows * width * 18, transcendentals=rows * width),
    )(a, driven, start, branch)


def states_back(streams, d_merged, branch, a, h):
    rows, width = a.shape
    tokens, heads = rows // streams, width // HEAD_W
    shape = jax.ShapeDtypeStruct
    return pl.pallas_call(
        functools.partial(state_back_kernel, streams, tokens),
        grid=(heads,),
        in_specs=[by_head(rows)] * 4,
        out_specs=[by_head(rows), by_head(rows), by_head(streams)],
        out_shape=[shape((rows, width), f32), shape((rows, width), bf16), shape((streams, width), f32)],
        compiler_params=params(),
        cost_estimate=pl.CostEstimate(flops=rows * width * 40, bytes_accessed=rows * width * 22, transcendentals=rows * width),
    )(d_merged, branch, a, h)


def mix_back(streams, dh, a, h, start, back, conv, stream, halo, keep, taps, decay, slope, gates):
    rows, width = a.shape
    tokens, heads, lead = rows // streams, width // HEAD_W, REACH * streams
    shape = jax.ShapeDtypeStruct
    gate_spec = pl.BlockSpec((1, HEAD_W, 2 * HEAD_W), lambda h: (h, 0, 0))
    return pl.pallas_call(
        functools.partial(mix_back_kernel, streams, tokens),
        grid=(heads,),
        in_specs=[
            by_head(rows), by_head(rows), by_head(rows), by_head(streams), by_head(streams), by_head(rows), by_head(rows),
            by_head(lead), whole(keep.shape[0]), by_head(CONV), by_head(1), by_head(1), gate_spec,
        ],
        out_specs=[by_head(rows), by_head(lead), by_head(lead), gate_spec, by_head(CONV), by_head(1)],
        out_shape=[
            shape((rows, width), bf16), shape((lead, width), f32), shape((lead, width), f32),
            shape((heads, HEAD_W, 2 * HEAD_W), f32), shape((CONV, width), f32), shape((1, width), f32),
        ],
        scratch_shapes=[
            pltpu.VMEM((rows + lead, HEAD_W), f32), pltpu.VMEM((rows, 2 * HEAD_W), f32), pltpu.VMEM((rows, HEAD_W), f32),
            pltpu.VMEM((rows, 2 * HEAD_W), bf16), pltpu.VMEM((rows + lead, HEAD_W), f32),
        ],
        compiler_params=params(),
        cost_estimate=pl.CostEstimate(flops=rows * width * 1200, bytes_accessed=rows * width * 22, transcendentals=rows * width * 6),
    )(dh, a, h, start, back, conv, stream, halo, keep, taps, decay, slope, gates)


def head_columns(block):
    rows, width = block.shape
    groups = width // (TP * HEAD_W)
    return block.reshape(rows, groups, TP, HEAD_W).transpose(2, 0, 1, 3).reshape(TP, rows, width // TP)


def head_back_kernel(groups, pieces_ref, gelu_ref, stream_ref):
    half = groups * HEAD_W
    for w in range(TP):
        for g in range(groups):
            to = (g * TP + w) * HEAD_W
            gelu_ref[:, to : to + HEAD_W] = pieces_ref[w, :, g * HEAD_W : (g + 1) * HEAD_W].astype(f32)
            stream_ref[:, to : to + HEAD_W] = pieces_ref[w, :, half + g * HEAD_W : half + (g + 1) * HEAD_W].astype(f32)


def head_columns_back(pieces):
    _, rows, width = pieces.shape
    groups = (width - HEAD_W) // (2 * HEAD_W)
    out = jax.ShapeDtypeStruct((rows, TP * groups * HEAD_W), f32)
    return pl.pallas_call(
        functools.partial(head_back_kernel, groups), out_shape=[out, out],
        compiler_params=pltpu.CompilerParams(vmem_limit_bytes=24 * 2**20),
        cost_estimate=pl.CostEstimate(flops=rows * width * 8, bytes_accessed=rows * width * 40, transcendentals=0),
    )(pieces)


def ff_back_kernel(n, pieces_ref, gate_ref, up_ref):
    part = gate_ref.shape[1] // (n * TP)
    half = n * part
    for w in range(TP):
        for s in range(n):
            to = (s * TP + w) * part
            gate_ref[:, to : to + part] = pieces_ref[w, :, s * part : (s + 1) * part].astype(f32)
            up_ref[:, to : to + part] = pieces_ref[w, :, half + s * part : half + (s + 1) * part].astype(f32)


def ff_columns_back(pieces):
    n = lax.axis_size("seq")
    _, rows, width = pieces.shape
    out = jax.ShapeDtypeStruct((rows, TP * width // 2), f32)
    return pl.pallas_call(
        functools.partial(ff_back_kernel, n), out_shape=[out, out],
        compiler_params=pltpu.CompilerParams(vmem_limit_bytes=24 * 2**20),
        cost_estimate=pl.CostEstimate(flops=rows * width * 8, bytes_accessed=rows * width * 40, transcendentals=0),
    )(pieces)


def ff_kernel(n, gate_ref, up_ref, out_ref):
    part = gate_ref.shape[1] // (n * TP)
    half = n * part
    for w in range(TP):
        for s in range(n):
            at = (s * TP + w) * part
            out_ref[w, :, s * part : (s + 1) * part] = gate_ref[:, at : at + part]
            out_ref[w, :, half + s * part : half + (s + 1) * part] = up_ref[:, at : at + part]


def ff_columns(gate, up):
    rows, width = gate.shape
    return pl.pallas_call(
        functools.partial(ff_kernel, lax.axis_size("seq")),
        out_shape=jax.ShapeDtypeStruct((TP, rows, 2 * width // TP), bf16),
        compiler_params=pltpu.CompilerParams(vmem_limit_bytes=24 * 2**20),
        cost_estimate=pl.CostEstimate(flops=rows * width * 8, bytes_accessed=rows * width * 8, transcendentals=0),
    )(gate, up)


class Weights:
    def __init__(self, shards, layer):
        self.shards = [s[layer] for s in shards]
        self.buffers = {}
        self.flip = bool(layer % 2)

    def slot(self, name, shape):
        n = lax.axis_size("seq")
        if name not in self.buffers:
            self.buffers[name] = jnp.zeros((n,) + shape, bf16)

    def put(self, name, block, at, column=0):
        self.buffers[name] = lax.dynamic_update_slice(self.buffers[name], block[None], (at, 0, column))

    def prepare_first(self):
        (mix_gain, proj_gelu, proj_stream, conv_taps, lru_gates, decay_param, _, mlp_gain, _, _, _) = self.shards
        rp = proj_gelu.shape[0]
        gr = lru_gates.shape[0] // TP
        small = jnp.concatenate([mix_gain, mlp_gain, conv_taps.reshape(-1), decay_param])
        top = jnp.pad(small, (0, (rp - gr) * HEAD_W - small.shape[0])).reshape(rp - gr, HEAD_W)
        extra = jnp.concatenate([top, jnp.zeros((gr, HEAD_W), bf16)])
        pieces = jnp.concatenate(
            [head_columns(proj_gelu), head_columns(proj_stream), jnp.broadcast_to(extra, (TP, rp, HEAD_W))], axis=2
        )
        got = jnp.stack(wt_exchange(pieces))
        gates = to_heads(lru_gates).reshape(TP, gr, HEAD_W)
        width = got.shape[2] - HEAD_W
        self.first_block = lax.dynamic_update_slice(got, gates, (0, rp - gr, width)).reshape(TP * rp, width + HEAD_W)
        return self.first_block

    def prepare_out(self):
        self.out_block = to_heads(self.shards[6])

    def prepare_wide(self):
        proj_gate, proj_up = self.shards[8], self.shards[9]
        wide = jnp.stack(wt_exchange(ff_columns(proj_gate, proj_up)))
        self.wide_block = wide.reshape(TP * proj_gate.shape[0], -1)

    def first_job(self):
        self.slot("first", self.first_block.shape)
        return GatherJob(self.first_block, self.flip, lambda block, at: self.put("first", block, at))

    def out_job(self):
        self.slot("out", self.out_block.shape)
        return GatherJob(self.out_block, not self.flip, lambda block, at: self.put("out", block, at))

    def gather_down(self):
        self.down = lax.all_gather(self.shards[10], "seq", tiled=True)

    def gather_wide(self):
        self.wide = lax.all_gather(self.wide_block, "seq", tiled=True)

    def open_first(self, sizes):
        rp, gr, cp, fb = sizes
        first = self.buffers["first"]
        w = lax.axis_index("wt")
        n = first.shape[0]
        depth = n * TP * rp
        width = first.shape[2] - HEAD_W
        flat = first.reshape(depth, width + HEAD_W)
        extra = flat[:, width:].reshape(n * TP, rp, HEAD_W)
        small = extra[:, : rp - gr].reshape(n * TP, -1)
        at = 2 * rp

        def own_heads(v):
            v = v.reshape(v.shape[0], -1, TP, HEAD_W)
            return lax.dynamic_index_in_dim(v, w, 2, keepdims=False).reshape(v.shape[0], -1).astype(f32)

        self.taps = own_heads(small[:, at : at + CONV * cp].reshape(n * TP, CONV, cp).transpose(1, 0, 2).reshape(CONV, -1))
        decay = own_heads(small[:, at + CONV * cp : at + (CONV + 1) * cp].reshape(1, -1))
        gates = extra[:, rp - gr :].reshape(2, -1, HEAD_W, HEAD_W).transpose(1, 2, 0, 3)
        self.gates = gates.reshape(-1, HEAD_W, 2 * HEAD_W)
        self.mix_gain = small[:, :rp].reshape(-1).astype(f32)
        self.mlp_gain = small[:, rp : 2 * rp].reshape(-1).astype(f32)
        self.decay, self.slope = -DECAY * jax.nn.softplus(decay), -DECAY * jax.nn.sigmoid(decay)
        self.gelu, self.stream = flat[:, : width // 2], flat[:, width // 2 : width]


def forward_block(x, normed, keep, streams, wts, pump, following):
    width = x.shape[1]
    if normed is None:
        normed = tp_gather(rms_norm(x, wts.mix_gain).astype(bf16))
    tokens = normed.shape[0] // streams
    last = normed.reshape(streams, tokens, width)[:, tokens - REACH :].transpose(1, 0, 2)
    halo_in = shift_seq(last.reshape(REACH * streams, width), 1)
    stream = dot(normed, wts.stream, bf16)
    halo = dot(halo_in, wts.stream, bf16).astype(f32)
    a, driven, conv, ends = mix(streams, stream, halo, keep, wts.taps, wts.decay, wts.gates)
    branch = dot(normed, wts.gelu)
    start = carry_in(ends[0], ends[1], 1)
    h, merged = states(streams, a, driven, start, branch)
    wts.out = wts.buffers["out"].reshape(-1, width)
    if following is not None:
        pump.add(following.first_job(), following.out_job())
        merged = pump.step(merged)
    mixed = tp_scatter(dot(merged, wts.out, bf16).reshape(TP, -1, width))
    mixed, wts.wide = tie(mixed, wts.wide)
    mixed = pump.step(mixed)
    x1 = x + mixed
    mlp_in = tp_gather(rms_norm(x1, wts.mlp_gain).astype(bf16))
    mlp_in = pump.step(mlp_in)
    wide = pump.step(dot(mlp_in, wts.wide))
    half = wide.shape[1] // 2
    product = (gelu(wide[:, :half]) * wide[:, half:]).astype(bf16)
    kept = dict(
        x=x, normed=normed, stream=stream, branch=branch, halo=halo, a=a, conv=conv, whole=ends[0], start=start, h=h,
        merged=merged, x1=x1, mlp_in=mlp_in, wide=wide, product=product,
    )
    return kept


def block_end(kept, wts):
    product = kept["product"]
    width = kept["x1"].shape[1]
    return kept["x1"] + tp_scatter(dot(product, wts.down, bf16).reshape(TP, -1, width))


def mlp_back(gx, g_down, wts, kept, results, rp, pump, above):
    width = gx.shape[1]
    n = lax.axis_size("seq")
    grad_down = dot_tokens(kept["product"], g_down)
    g_down, grad_down = tie(g_down, grad_down)
    d_product = dot_t(g_down, wts.down)
    wide = kept["wide"]
    half = wide.shape[1] // 2
    value, slope = gelu_and_slope(wide[:, :half])
    d_wide = jnp.concatenate([(d_product * wide[:, half:] * slope).astype(bf16), (d_product * value).astype(bf16)], axis=1)
    grad_wide = dot_tokens(kept["mlp_in"], d_wide).reshape(n, -1, 2 * half)
    d_wide, grad_wide, grad_down = tie(d_wide, grad_wide, grad_down)
    if above is not None:
        d_wide, above["wide"] = tie(d_wide, above["wide"])
    part = dot_t(d_wide, wts.wide, bf16).reshape(TP, -1, width)
    d_mlp_in = tp_scatter(pump.step(part))
    results["wide"] = lax.psum_scatter(grad_wide, "seq", scatter_dimension=0)
    if above is not None:
        d_mlp_in, grad_down = tie(d_mlp_in, grad_down)
    results["down"] = lax.psum_scatter(grad_down.reshape(n, -1, width), "seq", scatter_dimension=0).astype(f32)
    dv, d_gain = rms_norm_back(kept["x1"], wts.mlp_gain, d_mlp_in)
    return gx + dv, d_gain


def mixer_back(d_x1, keep, streams, wts, kept, d_mlp_gain, d_mix_gain, sizes, results, pump, end=None):
    rp, gr, cp, fb = sizes
    width = d_x1.shape[1]
    n, w = lax.axis_size("seq"), lax.axis_index("wt")
    g_branch = tp_gather(d_x1.astype(bf16))
    d_merged = dot_t(g_branch, wts.out)
    grad_out = dot_tokens(kept["merged"], g_branch)
    dh, d_branch, ends = states_back(streams, d_merged, kept["branch"], kept["a"], kept["h"])
    if end is not None:
        ends = end(ends)
    ends = pump.hold(ends)
    back = carry_in(kept["whole"], ends, -1)
    pump.add(ScatterJob(grad_out.reshape(n, -1, width), True, lambda total: results.update(out=from_heads(total))))
    back = pump.step(back)
    d_stream, tail, head, d_gates, d_taps, d_decay = mix_back(
        streams, dh, kept["a"], kept["h"], kept["start"], back, kept["conv"], kept["stream"], kept["halo"], keep,
        wts.taps, wts.decay, wts.slope, wts.gates,
    )
    tail = (tail + shift_seq(head, -1)).astype(bf16)
    tokens = d_stream.shape[0] // streams
    d_stream = lax.dynamic_update_slice(
        d_stream.reshape(streams, tokens, -1), tail.reshape(REACH, streams, -1).transpose(1, 0, 2), (0, tokens - REACH, 0)
    ).reshape(d_stream.shape)
    part = (dot_t(d_branch, wts.gelu) + dot_t(d_stream, wts.stream)).astype(bf16).reshape(TP, -1, width)

    def full(v):
        lines = v.reshape(v.shape[0], -1, 1, HEAD_W)
        return jnp.where(lax.iota(jnp.int32, TP)[None, None, :, None] == w, lines, 0.0).reshape(v.shape[0], n * TP, -1)

    small = jnp.concatenate(
        [
            d_mix_gain.reshape(n * TP, rp), d_mlp_gain.reshape(n * TP, rp),
            full(d_taps).transpose(1, 0, 2).reshape(n * TP, -1), full(d_decay)[0],
        ],
        axis=1,
    ).astype(bf16)
    small = jnp.pad(small, ((0, 0), (0, (rp - gr) * HEAD_W - small.shape[1]))).reshape(n * TP, rp - gr, HEAD_W)
    gates = d_gates.reshape(-1, HEAD_W, 2, HEAD_W).transpose(2, 0, 1, 3).reshape(n * TP, gr, HEAD_W).astype(bf16)
    extra = jnp.concatenate([small, gates], axis=1).reshape(n, TP * rp, HEAD_W)
    grad_gelu = dot_tokens(kept["normed"], d_branch).reshape(n, TP * rp, -1)
    grad_stream = dot_tokens(kept["normed"], d_stream).reshape(n, TP * rp, -1)

    both = ScatterJob(
        jnp.concatenate([grad_gelu, grad_stream, extra], axis=2), False, lambda total: results.update(raw=total)
    )
    if end is None:
        part, results["wide"] = tie(part, results["wide"])
    pump.add(
        both,
    )
    d_normed = tp_scatter(pump.step(part))
    if end is None:
        d_normed = pump.step(d_normed)
    dv, d_gain = rms_norm_back(kept["x"], wts.mix_gain, d_normed)
    return d_x1 + dv, d_gain, both


def finish_both(raw, results, above, sizes):
    rp, gr, cp, fb = sizes
    width = raw.shape[1] - HEAD_W
    results["gates"] = from_heads(raw.reshape(TP, rp, -1)[:, rp - gr :, width:].reshape(TP * gr, HEAD_W))
    pieces = jnp.stack(wt_exchange(raw.astype(bf16).reshape(TP, rp, -1)))
    results["gelu"], results["stream"] = head_columns_back(pieces)
    sums = jnp.sum(pieces[:, : rp - gr, width:].astype(f32), axis=0).reshape(-1)
    above["mix_gain"], results["mlp_gain"] = sums[:rp], sums[rp : 2 * rp]
    results["taps"] = sums[2 * rp : 2 * rp + CONV * cp].reshape(CONV, cp)
    results["decay"] = sums[2 * rp + CONV * cp : 2 * rp + (CONV + 1) * cp]


def per_device(block_in, start_flags, out_grad, *shards):
    layers = shards[0].shape[0]
    micro, _, tokens, width = block_in.shape
    streams = micro * TP
    sizes = (shards[1].shape[1], shards[4].shape[1] // TP, shards[5].shape[1], shards[10].shape[1])
    rp = sizes[0]

    weights = [Weights(shards, layer) for layer in range(layers)]
    zero, pump = weights[0], Pump()
    zero.prepare_first()
    zero.prepare_out()
    pump.add(zero.first_job(), zero.out_job())
    rest = [w.shards for w in weights]
    block_in, start_flags, out_grad, rest = pump.step((block_in, start_flags, out_grad, rest))
    for w, shards_then in zip(weights, rest):
        w.shards = shards_then
    flags = tp_gather(start_flags[:, 0].astype(f32))
    x_in = block_in[:, 0].reshape(micro * tokens, width)
    grad = out_grad[:, 0].reshape(micro * tokens, width)
    x_all = tp_gather(x_in)
    keep = 1.0 - flags.T
    behind = 1.0 - shift_seq(flags[:, tokens - REACH :].T, 1)
    keep = jnp.concatenate([behind, keep, jnp.ones((REACH, streams), f32)]).reshape(-1, 1)
    keep = jnp.broadcast_to(keep, (keep.shape[0], HEAD_W))

    x = x_in.astype(f32)
    kept = []
    zero.prepare_wide()
    for _ in range(3):
        zero.wide_block = pump.step(zero.wide_block)
    zero.wide_block, x_all, rest = pump.step((zero.wide_block, x_all, [w.shards for w in weights]))
    pump.finish()
    zero.gather_wide()
    for w, shards_then in zip(weights, rest):
        w.shards = shards_then
    zero.gather_down()
    for wts in weights[1:]:
        wts.prepare_first()
        wts.prepare_out()
        wts.prepare_wide()
        wts.gather_wide()
        wts.gather_down()
    for layer in range(layers):
        wts = weights[layer]
        wts.open_first(sizes)
        normed = rms_norm(x_all.astype(f32), wts.mix_gain).astype(bf16) if layer == 0 else None
        following = weights[layer + 1] if layer < layers - 1 else None
        saved = forward_block(x, normed, keep, streams, wts, pump, following)
        if layer < layers - 1:
            x = pump.step(block_end(saved, wts))
            pump.finish()
        kept.append(saved)
        if layer == 0:
            grad_then, saved["wide"] = tie(grad, saved["wide"])
            g_down = tp_gather(grad_then)

    gx = grad.astype(f32)
    d_mix = jnp.zeros((width,), f32)
    results = [dict() for _ in range(layers)]
    spare, outcome, jobs = {}, [], []

    def last(ends):
        ends, kept[-1]["product"] = tie(ends, kept[-1]["product"])
        outcome.append(block_end(kept[-1], weights[-1]))
        return ends

    for layer in reversed(range(layers)):
        if layer != layers - 1:
            g_down = tp_gather(gx.astype(bf16))
            g_down, results[layer + 1]["down"] = tie(g_down, results[layer + 1]["down"])
        d_x1, d_mlp = mlp_back(
            gx, g_down, weights[layer], kept[layer], results[layer], rp, pump, results[layer + 1] if layer < layers - 1 else None
        )
        gx, d_mix, both = mixer_back(
            d_x1, keep, streams, weights[layer], kept[layer], d_mlp, d_mix, sizes, results[layer], pump, last if layer == layers - 1 else None
        )
        jobs.append(both)
    pump.complete(jobs[:-1])
    held = [found.pop("raw") for found in results[1:]]
    held, wide = pump.step((held, [found["wide"] for found in results]))
    for found, total in zip(results, wide):
        found["wide"] = total
    held = pump.step(held)
    pump.finish()
    for layer in reversed(range(layers)):
        raw = held[layer - 1] if layer else results[0].pop("raw")
        finish_both(raw, results[layer], results[layer + 1] if layer < layers - 1 else spare, sizes)
    for found in results:
        pieces = wt_exchange(found.pop("wide").reshape(TP, rp, -1))
        found["gate"], found["up"] = ff_columns_back(jnp.stack(pieces))
    results[0]["mix_gain"] = vector_scatter(d_mix.reshape(-1, TP, rp))
    shape = (micro, 1, tokens, width)
    names = ("mix_gain", "gelu", "stream", "taps", "gates", "decay", "out", "mlp_gain", "gate", "up", "down")
    stacked = [jnp.stack([results[layer][k] for layer in range(layers)]) for k in names]
    return (outcome[0].astype(bf16).reshape(shape), gx.astype(bf16).reshape(shape), *stacked)


def solution(mesh):
    both = ("seq", "wt")
    tokens = P(None, "wt", "seq", None)
    vector, matrix = P(None, both), P(None, both, None)
    weights = (vector, matrix, matrix, P(None, None, both), matrix, vector, matrix, vector, matrix, matrix, matrix)
    return jax.shard_map(
        per_device,
        mesh=mesh,
        in_specs=(tokens, P(None, "wt", "seq"), tokens, *weights),
        out_specs=(tokens, tokens, *weights),
        check_vma=False,
    )
```

```python
import functools

import jax
import jax.numpy as jnp
from jax import lax
from jax.experimental import pallas as pl
from jax.experimental.pallas import tpu as pltpu
from jax.sharding import PartitionSpec as P

f32 = jnp.float32
bf16 = jnp.bfloat16
HEAD_W = 128
CONV = 4
REACH = CONV - 1
TP = 4
EPS = 1e-06
DECAY = 8.0
GELU_C = 0.7978845608
GELU_K = 0.044715


def dot(left, right, out=f32):
    return lax.dot_general(left, right, (((1,), (0,)), ((), ())), preferred_element_type=f32).astype(out)


def dot_t(left, right, out=f32):
    return lax.dot_general(left, right, (((1,), (1,)), ((), ())), preferred_element_type=f32).astype(out)


def dot_tokens(left, right, out=bf16):
    return lax.dot_general(left, right, (((0,), (0,)), ((), ())), preferred_element_type=f32).astype(out)


def sigmoid(v):
    return 1.0 / (1.0 + jnp.exp(-v))


def gelu(v):
    return 0.5 * v * (1.0 + jnp.tanh(GELU_C * (v + GELU_K * v * v * v)))


def gelu_and_slope(v):
    square = v * v
    t = jnp.tanh(GELU_C * v * (1.0 + GELU_K * square))
    value = 0.5 * v * (1.0 + t)
    slope = 0.5 * (1.0 + t) + 0.5 * v * (1.0 - t * t) * GELU_C * (1.0 + 3.0 * GELU_K * square)
    return value, slope


def minus_expm1(y, e):
    series = -y * (1.0 + y * (1 / 2) * (1.0 + y * (1 / 3) * (1.0 + y * (1 / 4) * (1.0 + y * (1 / 5) * (1.0 + y * (1 / 6))))))
    return jnp.where(y > -0.25, series, 1.0 - e)


def rms_norm(v, gain):
    return v * lax.rsqrt(jnp.mean(v * v, axis=-1, keepdims=True) + EPS) * gain


def rms_norm_back(v, gain, dy):
    r = lax.rsqrt(jnp.mean(v * v, axis=-1, keepdims=True) + EPS)
    dgain = jnp.sum(dy * v * r, axis=0)
    dyg = dy * gain
    dv = r * dyg - v * (r * r * r) * jnp.mean(dyg * v, axis=-1, keepdims=True)
    return dv, dgain


def swap(x, k):
    return lax.ppermute(x, "wt", [(i, i ^ k) for i in range(TP)])


def tp_gather(x):
    far = swap(x, 2)
    near = swap(x, 1)
    diagonal = swap(far, 1)
    return jnp.concatenate([x, near, far, diagonal], axis=0)


def tp_scatter(part):
    far = (part[2].astype(f32) + swap(part[3], 1).astype(f32)).astype(bf16)
    across = swap(far, 2)
    near = swap(part[1], 1)
    return part[0].astype(f32) + near.astype(f32) + across.astype(f32)


def wt_exchange(pieces):
    w = lax.axis_index("wt")
    pick = lambda stack, j: lax.dynamic_index_in_dim(stack, j, 0, keepdims=False)
    got = [pick(pieces, w)] + [swap(pick(pieces, w ^ k), k) for k in range(1, TP)]
    stack = jnp.stack(got)
    return [pick(stack, w ^ j) for j in range(TP)]


def ring_tables():
    n = lax.axis_size("seq")
    order = [0, 1, 3, 5, 7, 6, 4, 2] if n == 8 else list(range(n))
    right = [(order[i], order[(i + 1) % n]) for i in range(n)]
    left = [(b, a) for a, b in right]
    s = lax.axis_index("seq")
    if n == 8:
        position = jnp.where(s % 2 == 1, s // 2 + 1, (8 - s // 2) % 8)
        owner = lambda p: jnp.where(p == 0, 0, jnp.where(p <= 4, 2 * p - 1, 16 - 2 * p))
    else:
        position, owner = s, lambda p: p
    device = lambda offset: owner(lax.rem(position + offset + n, n))
    return n, right, left, device


class GatherJob:
    def __init__(self, block, flip, place):
        self.n, right, left, self.device = ring_tables()
        self.routes = (left, right) if flip else (right, left)
        self.sign = -1 if flip else 1
        self.a = self.b = block
        self.hop, self.place = 0, place
        self.place(block, self.device(0))
        self.done = False

    def start(self):
        self.hop += 1
        flight = [lax.ppermute(self.a, "seq", self.routes[0])]
        if self.hop <= self.n - 1 - self.n // 2:
            flight.append(lax.ppermute(self.b, "seq", self.routes[1]))
        return flight

    def bytes(self):
        return self.a.size * 2

    def receive(self, flight):
        self.a = flight[0]
        self.place(self.a, self.device(-self.sign * self.hop))
        if len(flight) > 1:
            self.b = flight[1]
            self.place(self.b, self.device(self.sign * self.hop))
        self.done = self.hop == self.n // 2


class ScatterJob:
    def __init__(self, stack, flip, finish):
        self.n, right, left, self.device = ring_tables()
        self.routes = (left, right) if flip else (right, left)
        self.sign = -1 if flip else 1
        self.stack, self.finish = stack, finish
        self.far, self.near = self.n // 2, self.n - 1 - self.n // 2
        self.a, self.b = self.chunk(self.far), self.chunk(-self.near)
        self.hop, self.done = 0, False

    def chunk(self, k):
        return lax.dynamic_index_in_dim(self.stack, self.device(self.sign * k), 0, keepdims=False)

    def bytes(self):
        return self.a.size * 2

    def start(self):
        self.hop += 1
        flight = [lax.ppermute(self.a, "seq", self.routes[0])]
        if self.hop <= self.near:
            flight.append(lax.ppermute(self.b, "seq", self.routes[1]))
        return flight

    def receive(self, flight):
        add = lambda x, y: (x.astype(f32) + y.astype(f32)).astype(bf16)
        self.a = flight[0]
        if self.hop < self.far:
            self.a = add(self.a, self.chunk(self.far - self.hop))
        if len(flight) > 1:
            self.b = flight[1]
            if self.hop < self.near:
                self.b = add(self.b, self.chunk(self.hop - self.near))
        if self.hop == self.far:
            self.done = True
            self.finish(self.chunk(0).astype(f32) + self.a.astype(f32) + self.b.astype(f32))


def tie(*values):
    return lax.optimization_barrier(values)


def run(job):
    while not job.done:
        job.receive(job.start())


class Pump:
    def __init__(self):
        self.waiting, self.active = [], []

    def add(self, *jobs):
        self.waiting += jobs

    def hold(self, value):
        flights = [flight for _, flight in self.active]
        if flights:
            value, flights = lax.optimization_barrier((value, flights))
        for (job, _), flight in zip(self.active, flights):
            job.receive(flight)
            if not job.done:
                self.waiting.append(job)
        self.active = []
        return value

    def step(self, value):
        flights = [flight for _, flight in self.active]
        heads = [(job.a, job.b) for job in self.waiting]
        if flights or heads:
            value, flights, heads = lax.optimization_barrier((value, flights, heads))
        moved = []
        for (job, _), flight in zip(self.active, flights):
            job.receive(flight)
            if not job.done:
                moved.append(job)
        for job, (a, b) in zip(self.waiting, heads):
            job.a, job.b = a, b
            moved.append(job)
        self.waiting = []
        self.active = [(job, job.start()) for job in moved]
        return value

    def complete(self, jobs):
        for job, flight in self.active:
            if job in jobs:
                job.receive(flight)
        self.active = [(job, flight) for job, flight in self.active if job not in jobs]
        self.waiting = [job for job in self.waiting if job not in jobs]
        for job in jobs:
            run(job)

    def finish(self):
        for job, flight in self.active:
            job.receive(flight)
            run(job)
        for job in self.waiting:
            run(job)
        self.active, self.waiting = [], []


def shift_seq(x, distance):
    n = lax.axis_size("seq")
    return lax.ppermute(x, "seq", [(i, i + distance) for i in range(n) if 0 <= i + distance < n])


def carry_in(decay, state, direction):
    n = lax.axis_size("seq")
    width = decay.shape[-1]
    inclusive = jnp.concatenate([decay, state], axis=-1)

    def then(near, far):
        return jnp.concatenate(
            [near[:, :width] * far[:, :width], near[:, width:] + near[:, :width] * far[:, width:]], axis=-1
        )

    reach, covered, total = 1, 0, None
    while covered < n - 1:
        first = shift_seq(inclusive, direction * reach)
        second = shift_seq(inclusive, direction * 2 * reach) if covered + reach < n - 1 else None
        both = first if second is None else then(first, second)
        total = both if total is None else then(total, both)
        covered += 2 * reach if second is not None else reach
        inclusive = then(inclusive, both)
        reach *= 3
    return total[:, width:]


def head_route(rows):
    n = lax.axis_size("seq")
    per = HEAD_W // rows
    route = []
    for s in range(n):
        base = s // per * per
        for w in range(TP):
            b = TP * (s - base) + w
            route.append((s * TP + w, (base + b % per) * TP + b // per))
    return route


def to_heads(x):
    route = head_route(x.shape[0])
    return x if all(a == b for a, b in route) else lax.ppermute(x, ("seq", "wt"), route)


def from_heads(x):
    route = head_route(x.shape[0])
    return x if all(a == b for a, b in route) else lax.ppermute(x, ("seq", "wt"), [(b, a) for a, b in route])


def vector_scatter(v):
    w, s = lax.axis_index("wt"), lax.axis_index("seq")
    pick = lambda x, j, ax: lax.dynamic_index_in_dim(x, j, ax, keepdims=False)
    n, _, k = v.shape
    v = v.reshape(n, 2, 2, k)
    hi, lo = w >> 1, w & 1
    v = pick(v, hi, 1) + swap(pick(v, 1 - hi, 1), 2)
    v = pick(v, lo, 1) + swap(pick(v, 1 - lo, 1), 1)
    half = n // 2
    while half:
        v = v.reshape(2, half, k)
        bit = (s // half) % 2
        other = lax.ppermute(pick(v, 1 - bit, 0), "seq", [(i, i ^ half) for i in range(n)])
        v = pick(v, bit, 0) + other
        half //= 2
    return v.reshape(k)


def lay_stream(buf, src, streams, tokens, lead):
    for b in range(streams):
        buf[pl.ds(lead + b, tokens, stride=streams), :] = src[pl.ds(b * tokens, tokens), :].astype(f32)


def gate_values(pre_rows, decay_row, keep):
    sr = sigmoid(pre_rows[:, :HEAD_W])
    si = sigmoid(pre_rows[:, HEAD_W:])
    log_a = decay_row * sr
    raw = jnp.exp(log_a)
    e2 = raw * raw
    msq = keep * minus_expm1(2.0 * log_a, e2) + (1.0 - keep)
    return sr, si, raw, e2, jnp.sqrt(msq)


def mix_kernel(
    streams, tokens, stream_ref, halo_ref, keep_ref, taps_ref, decay_ref, gates_ref,
    a_ref, d_ref, conv_ref, ends_ref, buf, pre,
):
    lead = REACH * streams
    rows = streams * tokens
    step = 128
    buf[pl.ds(0, lead), :] = halo_ref[...]
    lay_stream(buf, stream_ref, streams, tokens, lead)
    taps = [taps_ref[pl.ds(k, 1), :] for k in range(CONV)]

    def conv_step(i, _):
        r = pl.multiple_of(i * step, step)
        total = taps[0] * buf[pl.ds(r + lead, step), :]
        valid = None
        for k in range(1, CONV):
            keep = keep_ref[pl.ds(r + lead - (k - 1) * streams, step), :]
            valid = keep if valid is None else valid * keep
            total = total + taps[k] * buf[pl.ds(r + lead - k * streams, step), :] * valid
        conv_ref[pl.ds(r, step), :] = total.astype(bf16)
        return 0

    lax.fori_loop(0, rows // step, conv_step, 0)
    pre[...] = jnp.dot(conv_ref[...], gates_ref[0], preferred_element_type=f32)

    def gate_step(i, _):
        r = pl.multiple_of(i * step, step)
        keep = keep_ref[pl.ds(r + lead, step), :]
        _, si, raw, _, m = gate_values(pre[pl.ds(r, step), :], decay_ref[...], keep)
        a_ref[pl.ds(r, step), :] = raw * keep
        d_ref[pl.ds(r, step), :] = m * si * conv_ref[pl.ds(r, step), :].astype(f32)
        return 0

    lax.fori_loop(0, rows // step, gate_step, 0)

    def scan_step(t, carry):
        total, h = carry
        r = pl.multiple_of(t * streams, streams)
        a = a_ref[pl.ds(r, streams), :]
        return total * a, a * h + d_ref[pl.ds(r, streams), :]

    total, h = lax.fori_loop(
        0, tokens, scan_step, (jnp.ones((streams, HEAD_W), f32), jnp.zeros((streams, HEAD_W), f32)), unroll=8
    )
    ends_ref[0] = total
    ends_ref[1] = h


def state_kernel(streams, tokens, a_ref, d_ref, start_ref, branch_ref, h_ref, merged_ref):
    def scan_step(t, h):
        r = pl.multiple_of(t * streams, streams)
        h = a_ref[pl.ds(r, streams), :] * h + d_ref[pl.ds(r, streams), :]
        h_ref[pl.ds(r, streams), :] = h
        return h

    lax.fori_loop(0, tokens, scan_step, start_ref[...], unroll=8)
    for b in range(streams):
        at = pl.ds(b * tokens, tokens)
        h = h_ref[pl.ds(b, tokens, stride=streams), :]
        merged_ref[at, :] = (h * gelu(branch_ref[at, :])).astype(bf16)


def state_back_kernel(streams, tokens, dm_ref, branch_ref, a_ref, h_ref, dh_ref, db_ref, ends_ref):
    for b in range(streams):
        at = pl.ds(b * tokens, tokens)
        dm = dm_ref[at, :]
        value, slope = gelu_and_slope(branch_ref[at, :])
        h = h_ref[pl.ds(b, tokens, stride=streams), :]
        dh_ref[pl.ds(b, tokens, stride=streams), :] = dm * value
        db_ref[at, :] = (dm * h * slope).astype(bf16)

    def scan_step(i, g):
        r = pl.multiple_of((tokens - 1 - i) * streams, streams)
        return a_ref[pl.ds(r, streams), :] * (dh_ref[pl.ds(r, streams), :] + g)

    ends_ref[...] = lax.fori_loop(0, tokens, scan_step, jnp.zeros((streams, HEAD_W), f32), unroll=8)


def mix_back_kernel(
    streams, tokens, dh_ref, a_ref, h_ref, start_ref, back_ref, conv_ref, stream_ref, halo_ref, keep_ref, taps_ref,
    decay_ref, slope_ref, gates_ref,
    ds_ref, tail_ref, head_ref, dgates_ref, dtaps_ref, ddecay_ref,
    buf, pre, back, dpre, dconv,
):
    lead = REACH * streams
    rows = streams * tokens
    step = 128
    buf[pl.ds(0, lead), :] = halo_ref[...]
    lay_stream(buf, stream_ref, streams, tokens, lead)
    pre[...] = jnp.dot(conv_ref[...], gates_ref[0], preferred_element_type=f32)

    def scan_step(i, g):
        r = pl.multiple_of((tokens - 1 - i) * streams, streams)
        total = dh_ref[pl.ds(r, streams), :] + g
        back[pl.ds(r, streams), :] = total
        return a_ref[pl.ds(r, streams), :] * total

    lax.fori_loop(0, tokens, scan_step, back_ref[...], unroll=8)
    dconv[pl.ds(rows, lead), :] = jnp.zeros((lead, HEAD_W), f32)

    def gate_step(i, acc):
        r = pl.multiple_of(i * step, step)
        keep = keep_ref[pl.ds(r + lead, step), :]
        decay = decay_ref[...]
        sr, si, raw, e2, m = gate_values(pre[pl.ds(r, step), :], decay, keep)
        g = back[pl.ds(r, step), :]
        conv = conv_ref[pl.ds(r, step), :].astype(f32)
        before = h_ref[pl.ds(jnp.maximum(r - streams, 0), step), :]
        shifted = jnp.concatenate([start_ref[...], before[: step - streams]], axis=0)
        previous = jnp.where(i == 0, shifted, before)
        gsi = g * si
        gm = gsi * m
        dconv[pl.ds(r, step), :] = gm
        d_input = gm * conv * (1.0 - si)
        d_log = g * previous * raw * keep - gsi * conv * keep * e2 / m
        by_rate = d_log * sr
        d_rate = by_rate * decay * (1.0 - sr)
        dpre[pl.ds(r, step), :] = jnp.concatenate([d_rate.astype(bf16), d_input.astype(bf16)], axis=1)
        return acc + jnp.sum(by_rate.reshape(step // 8, 8, HEAD_W), axis=0)

    acc = lax.fori_loop(0, rows // step, gate_step, jnp.zeros((8, HEAD_W), f32))
    ddecay_ref[...] = jnp.sum(acc, axis=0, keepdims=True) * slope_ref[...]
    dgates_ref[0] = lax.dot_general(conv_ref[...], dpre[...], (((0,), (0,)), ((), ())), preferred_element_type=f32)
    pre[:, :HEAD_W] = lax.dot_general(dpre[...], gates_ref[0], (((1,), (1,)), ((), ())), preferred_element_type=f32)
    taps = [taps_ref[pl.ds(k, 1), :] for k in range(CONV)]

    def add_step(i, accs):
        r = pl.multiple_of(i * step, step)
        dc = dconv[pl.ds(r, step), :] + pre[pl.ds(r, step), :HEAD_W]
        dconv[pl.ds(r, step), :] = dc
        out, valid = [], None
        for k in range(CONV):
            term = dc * buf[pl.ds(r + lead - k * streams, step), :]
            if k:
                keep = keep_ref[pl.ds(r + lead - (k - 1) * streams, step), :]
                valid = keep if valid is None else valid * keep
                term = term * valid
            out.append(accs[k] + jnp.sum(term.reshape(step // 8, 8, HEAD_W), axis=0))
        return tuple(out)

    accs = lax.fori_loop(0, rows // step, add_step, tuple(jnp.zeros((8, HEAD_W), f32) for _ in range(CONV)))
    for k in range(CONV):
        dtaps_ref[pl.ds(k, 1), :] = jnp.sum(accs[k], axis=0, keepdims=True)

    def stream_rows(r, count):
        total = taps[0] * dconv[pl.ds(r, count), :]
        valid = None
        for k in range(1, CONV):
            keep = keep_ref[pl.ds(r + lead + k * streams, count), :]
            valid = keep if valid is None else valid * keep
            total = total + taps[k] * dconv[pl.ds(r + k * streams, count), :] * valid
        return total

    def stream_step(i, _):
        r = pl.multiple_of(i * step, step)
        buf[pl.ds(r, step), :] = stream_rows(r, step)
        return 0

    lax.fori_loop(0, rows // step, stream_step, 0)
    tail_ref[...] = buf[pl.ds(rows - lead, lead), :]
    for b in range(streams):
        ds_ref[pl.ds(b * tokens, tokens), :] = buf[pl.ds(b, tokens, stride=streams), :].astype(bf16)
    for j in range(REACH):
        total = None
        valid = None
        for k in range(1, CONV):
            at = j + k - REACH
            keep = keep_ref[pl.ds((j + k) * streams, streams), :]
            valid = keep if valid is None else valid * keep
            if at >= 0:
                term = taps[k] * dconv[pl.ds(at * streams, streams), :] * valid
                total = term if total is None else total + term
        head_ref[pl.ds(j * streams, streams), :] = total


def by_head(rows):
    return pl.BlockSpec((rows, HEAD_W), lambda h: (0, h))


def whole(rows):
    return pl.BlockSpec((rows, HEAD_W), lambda h: (0, 0))


def params():
    return pltpu.CompilerParams(vmem_limit_bytes=40 * 2**20, dimension_semantics=("arbitrary",))


def mix(streams, stream, halo, keep, taps, decay, gates):
    rows, width = stream.shape
    tokens, heads, lead = rows // streams, width // HEAD_W, REACH * streams
    two = pl.BlockSpec((2, streams, HEAD_W), lambda h: (0, 0, h))
    shape = jax.ShapeDtypeStruct
    return pl.pallas_call(
        functools.partial(mix_kernel, streams, tokens),
        grid=(heads,),
        in_specs=[
            by_head(rows), by_head(lead), whole(keep.shape[0]), by_head(CONV), by_head(1),
            pl.BlockSpec((1, HEAD_W, 2 * HEAD_W), lambda h: (h, 0, 0)),
        ],
        out_specs=[by_head(rows), by_head(rows), by_head(rows), two],
        out_shape=[
            shape((rows, width), f32), shape((rows, width), f32), shape((rows, width), bf16), shape((2, streams, width), f32),
        ],
        scratch_shapes=[pltpu.VMEM((rows + lead, HEAD_W), f32), pltpu.VMEM((rows, 2 * HEAD_W), f32)],
        compiler_params=params(),
        cost_estimate=pl.CostEstimate(flops=rows * width * 600, bytes_accessed=rows * width * 12, transcendentals=rows * width * 6),
    )(stream, halo, keep, taps, decay, gates)


def states(streams, a, driven, start, branch):
    rows, width = a.shape
    tokens, heads = rows // streams, width // HEAD_W
    shape = jax.ShapeDtypeStruct
    return pl.pallas_call(
        functools.partial(state_kernel, streams, tokens),
        grid=(heads,),
        in_specs=[by_head(rows), by_head(rows), by_head(streams), by_head(rows)],
        out_specs=[by_head(rows), by_head(rows)],
        out_shape=[shape((rows, width), f32), shape((rows, width), bf16)],
        compiler_params=params(),
        cost_estimate=pl.CostEstimate(flops=rows * width * 30, bytes_accessed=rows * width * 18, transcendentals=rows * width),
    )(a, driven, start, branch)


def states_back(streams, d_merged, branch, a, h):
    rows, width = a.shape
    tokens, heads = rows // streams, width // HEAD_W
    shape = jax.ShapeDtypeStruct
    return pl.pallas_call(
        functools.partial(state_back_kernel, streams, tokens),
        grid=(heads,),
        in_specs=[by_head(rows)] * 4,
        out_specs=[by_head(rows), by_head(rows), by_head(streams)],
        out_shape=[shape((rows, width), f32), shape((rows, width), bf16), shape((streams, width), f32)],
        compiler_params=params(),
        cost_estimate=pl.CostEstimate(flops=rows * width * 40, bytes_accessed=rows * width * 22, transcendentals=rows * width),
    )(d_merged, branch, a, h)


def mix_back(streams, dh, a, h, start, back, conv, stream, halo, keep, taps, decay, slope, gates):
    rows, width = a.shape
    tokens, heads, lead = rows // streams, width // HEAD_W, REACH * streams
    shape = jax.ShapeDtypeStruct
    gate_spec = pl.BlockSpec((1, HEAD_W, 2 * HEAD_W), lambda h: (h, 0, 0))
    return pl.pallas_call(
        functools.partial(mix_back_kernel, streams, tokens),
        grid=(heads,),
        in_specs=[
            by_head(rows), by_head(rows), by_head(rows), by_head(streams), by_head(streams), by_head(rows), by_head(rows),
            by_head(lead), whole(keep.shape[0]), by_head(CONV), by_head(1), by_head(1), gate_spec,
        ],
        out_specs=[by_head(rows), by_head(lead), by_head(lead), gate_spec, by_head(CONV), by_head(1)],
        out_shape=[
            shape((rows, width), bf16), shape((lead, width), f32), shape((lead, width), f32),
            shape((heads, HEAD_W, 2 * HEAD_W), f32), shape((CONV, width), f32), shape((1, width), f32),
        ],
        scratch_shapes=[
            pltpu.VMEM((rows + lead, HEAD_W), f32), pltpu.VMEM((rows, 2 * HEAD_W), f32), pltpu.VMEM((rows, HEAD_W), f32),
            pltpu.VMEM((rows, 2 * HEAD_W), bf16), pltpu.VMEM((rows + lead, HEAD_W), f32),
        ],
        compiler_params=params(),
        cost_estimate=pl.CostEstimate(flops=rows * width * 1200, bytes_accessed=rows * width * 22, transcendentals=rows * width * 6),
    )(dh, a, h, start, back, conv, stream, halo, keep, taps, decay, slope, gates)


def head_columns(block):
    rows, width = block.shape
    groups = width // (TP * HEAD_W)
    return block.reshape(rows, groups, TP, HEAD_W).transpose(2, 0, 1, 3).reshape(TP, rows, width // TP)


def head_back_kernel(groups, pieces_ref, gelu_ref, stream_ref):
    half = groups * HEAD_W
    for w in range(TP):
        for g in range(groups):
            to = (g * TP + w) * HEAD_W
            gelu_ref[:, to : to + HEAD_W] = pieces_ref[w, :, g * HEAD_W : (g + 1) * HEAD_W].astype(f32)
            stream_ref[:, to : to + HEAD_W] = pieces_ref[w, :, half + g * HEAD_W : half + (g + 1) * HEAD_W].astype(f32)


def head_columns_back(pieces):
    _, rows, width = pieces.shape
    groups = (width - HEAD_W) // (2 * HEAD_W)
    out = jax.ShapeDtypeStruct((rows, TP * groups * HEAD_W), f32)
    return pl.pallas_call(
        functools.partial(head_back_kernel, groups), out_shape=[out, out],
        compiler_params=pltpu.CompilerParams(vmem_limit_bytes=24 * 2**20),
        cost_estimate=pl.CostEstimate(flops=rows * width * 8, bytes_accessed=rows * width * 40, transcendentals=0),
    )(pieces)


def ff_back_kernel(n, pieces_ref, gate_ref, up_ref):
    part = gate_ref.shape[1] // (n * TP)
    half = n * part
    for w in range(TP):
        for s in range(n):
            to = (s * TP + w) * part
            gate_ref[:, to : to + part] = pieces_ref[w, :, s * part : (s + 1) * part].astype(f32)
            up_ref[:, to : to + part] = pieces_ref[w, :, half + s * part : half + (s + 1) * part].astype(f32)


def ff_columns_back(pieces):
    n = lax.axis_size("seq")
    _, rows, width = pieces.shape
    out = jax.ShapeDtypeStruct((rows, TP * width // 2), f32)
    return pl.pallas_call(
        functools.partial(ff_back_kernel, n), out_shape=[out, out],
        compiler_params=pltpu.CompilerParams(vmem_limit_bytes=24 * 2**20),
        cost_estimate=pl.CostEstimate(flops=rows * width * 8, bytes_accessed=rows * width * 40, transcendentals=0),
    )(pieces)


def ff_kernel(n, gate_ref, up_ref, out_ref):
    part = gate_ref.shape[1] // (n * TP)
    half = n * part
    for w in range(TP):
        for s in range(n):
            at = (s * TP + w) * part
            out_ref[w, :, s * part : (s + 1) * part] = gate_ref[:, at : at + part]
            out_ref[w, :, half + s * part : half + (s + 1) * part] = up_ref[:, at : at + part]


def ff_columns(gate, up):
    rows, width = gate.shape
    return pl.pallas_call(
        functools.partial(ff_kernel, lax.axis_size("seq")),
        out_shape=jax.ShapeDtypeStruct((TP, rows, 2 * width // TP), bf16),
        compiler_params=pltpu.CompilerParams(vmem_limit_bytes=24 * 2**20),
        cost_estimate=pl.CostEstimate(flops=rows * width * 8, bytes_accessed=rows * width * 8, transcendentals=0),
    )(gate, up)


class Weights:
    def __init__(self, shards, layer):
        self.shards = [s[layer] for s in shards]
        self.buffers = {}
        self.flip = bool(layer % 2)

    def slot(self, name, shape):
        n = lax.axis_size("seq")
        if name not in self.buffers:
            self.buffers[name] = jnp.zeros((n,) + shape, bf16)

    def put(self, name, block, at, column=0):
        self.buffers[name] = lax.dynamic_update_slice(self.buffers[name], block[None], (at, 0, column))

    def prepare_first(self):
        (mix_gain, proj_gelu, proj_stream, conv_taps, lru_gates, decay_param, _, mlp_gain, _, _, _) = self.shards
        rp = proj_gelu.shape[0]
        gr = lru_gates.shape[0] // TP
        small = jnp.concatenate([mix_gain, mlp_gain, conv_taps.reshape(-1), decay_param])
        top = jnp.pad(small, (0, (rp - gr) * HEAD_W - small.shape[0])).reshape(rp - gr, HEAD_W)
        extra = jnp.concatenate([top, jnp.zeros((gr, HEAD_W), bf16)])
        pieces = jnp.concatenate(
            [head_columns(proj_gelu), head_columns(proj_stream), jnp.broadcast_to(extra, (TP, rp, HEAD_W))], axis=2
        )
        got = jnp.stack(wt_exchange(pieces))
        gates = to_heads(lru_gates).reshape(TP, gr, HEAD_W)
        width = got.shape[2] - HEAD_W
        self.first_block = lax.dynamic_update_slice(got, gates, (0, rp - gr, width)).reshape(TP * rp, width + HEAD_W)
        return self.first_block

    def prepare_out(self):
        self.out_block = to_heads(self.shards[6])

    def prepare_wide(self):
        proj_gate, proj_up = self.shards[8], self.shards[9]
        wide = jnp.stack(wt_exchange(ff_columns(proj_gate, proj_up)))
        self.wide_block = wide.reshape(TP * proj_gate.shape[0], -1)

    def first_job(self):
        self.slot("first", self.first_block.shape)
        return GatherJob(self.first_block, self.flip, lambda block, at: self.put("first", block, at))

    def out_job(self):
        self.slot("out", self.out_block.shape)
        return GatherJob(self.out_block, not self.flip, lambda block, at: self.put("out", block, at))

    def gather_down(self):
        self.down = lax.all_gather(self.shards[10], "seq", tiled=True)

    def gather_wide(self):
        self.wide = lax.all_gather(self.wide_block, "seq", tiled=True)

    def open_first(self, sizes):
        rp, gr, cp, fb = sizes
        first = self.buffers["first"]
        w = lax.axis_index("wt")
        n = first.shape[0]
        depth = n * TP * rp
        width = first.shape[2] - HEAD_W
        flat = first.reshape(depth, width + HEAD_W)
        extra = flat[:, width:].reshape(n * TP, rp, HEAD_W)
        small = extra[:, : rp - gr].reshape(n * TP, -1)
        at = 2 * rp

        def own_heads(v):
            v = v.reshape(v.shape[0], -1, TP, HEAD_W)
            return lax.dynamic_index_in_dim(v, w, 2, keepdims=False).reshape(v.shape[0], -1).astype(f32)

        self.taps = own_heads(small[:, at : at + CONV * cp].reshape(n * TP, CONV, cp).transpose(1, 0, 2).reshape(CONV, -1))
        decay = own_heads(small[:, at + CONV * cp : at + (CONV + 1) * cp].reshape(1, -1))
        gates = extra[:, rp - gr :].reshape(2, -1, HEAD_W, HEAD_W).transpose(1, 2, 0, 3)
        self.gates = gates.reshape(-1, HEAD_W, 2 * HEAD_W)
        self.mix_gain = small[:, :rp].reshape(-1).astype(f32)
        self.mlp_gain = small[:, rp : 2 * rp].reshape(-1).astype(f32)
        self.decay, self.slope = -DECAY * jax.nn.softplus(decay), -DECAY * jax.nn.sigmoid(decay)
        self.gelu, self.stream = flat[:, : width // 2], flat[:, width // 2 : width]


def forward_block(x, normed, keep, streams, wts, pump, following):
    width = x.shape[1]
    if normed is None:
        normed = tp_gather(rms_norm(x, wts.mix_gain).astype(bf16))
    tokens = normed.shape[0] // streams
    last = normed.reshape(streams, tokens, width)[:, tokens - REACH :].transpose(1, 0, 2)
    halo_in = shift_seq(last.reshape(REACH * streams, width), 1)
    stream = dot(normed, wts.stream, bf16)
    halo = dot(halo_in, wts.stream, bf16).astype(f32)
    a, driven, conv, ends = mix(streams, stream, halo, keep, wts.taps, wts.decay, wts.gates)
    branch = dot(normed, wts.gelu)
    start = carry_in(ends[0], ends[1], 1)
    h, merged = states(streams, a, driven, start, branch)
    wts.out = wts.buffers["out"].reshape(-1, width)
    if following is not None:
        pump.add(following.first_job(), following.out_job())
        merged = pump.step(merged)
    mixed = tp_scatter(dot(merged, wts.out, bf16).reshape(TP, -1, width))
    mixed, wts.wide = tie(mixed, wts.wide)
    mixed = pump.step(mixed)
    x1 = x + mixed
    mlp_in = tp_gather(rms_norm(x1, wts.mlp_gain).astype(bf16))
    mlp_in = pump.step(mlp_in)
    wide = pump.step(dot(mlp_in, wts.wide))
    half = wide.shape[1] // 2
    product = (gelu(wide[:, :half]) * wide[:, half:]).astype(bf16)
    kept = dict(
        x=x, normed=normed, stream=stream, branch=branch, halo=halo, a=a, conv=conv, whole=ends[0], start=start, h=h,
        merged=merged, x1=x1, mlp_in=mlp_in, wide=wide, product=product,
    )
    return kept


def block_end(kept, wts):
    product = kept["product"]
    width = kept["x1"].shape[1]
    return kept["x1"] + tp_scatter(dot(product, wts.down, bf16).reshape(TP, -1, width))


def mlp_back(gx, g_down, wts, kept, results, rp, pump, above):
    width = gx.shape[1]
    n = lax.axis_size("seq")
    grad_down = dot_tokens(kept["product"], g_down)
    g_down, grad_down = tie(g_down, grad_down)
    d_product = dot_t(g_down, wts.down)
    wide = kept["wide"]
    half = wide.shape[1] // 2
    value, slope = gelu_and_slope(wide[:, :half])
    d_wide = jnp.concatenate([(d_product * wide[:, half:] * slope).astype(bf16), (d_product * value).astype(bf16)], axis=1)
    grad_wide = dot_tokens(kept["mlp_in"], d_wide).reshape(n, -1, 2 * half)
    d_wide, grad_wide, grad_down = tie(d_wide, grad_wide, grad_down)
    if above is not None:
        d_wide, above["wide"] = tie(d_wide, above["wide"])
    part = dot_t(d_wide, wts.wide, bf16).reshape(TP, -1, width)
    d_mlp_in = tp_scatter(pump.step(part))
    results["wide"] = lax.psum_scatter(grad_wide, "seq", scatter_dimension=0)
    if above is not None:
        d_mlp_in, grad_down = tie(d_mlp_in, grad_down)
    results["down"] = lax.psum_scatter(grad_down.reshape(n, -1, width), "seq", scatter_dimension=0).astype(f32)
    dv, d_gain = rms_norm_back(kept["x1"], wts.mlp_gain, d_mlp_in)
    return gx + dv, d_gain


def mixer_back(d_x1, keep, streams, wts, kept, d_mlp_gain, d_mix_gain, sizes, results, pump, end=None):
    rp, gr, cp, fb = sizes
    width = d_x1.shape[1]
    n, w = lax.axis_size("seq"), lax.axis_index("wt")
    g_branch = tp_gather(d_x1.astype(bf16))
    d_merged = dot_t(g_branch, wts.out)
    grad_out = dot_tokens(kept["merged"], g_branch)
    dh, d_branch, ends = states_back(streams, d_merged, kept["branch"], kept["a"], kept["h"])
    if end is not None:
        ends = end[0](ends)
    ends = pump.hold(ends)
    back = carry_in(kept["whole"], ends, -1)
    back = pump.step(back)
    d_stream, tail, head, d_gates, d_taps, d_decay = mix_back(
        streams, dh, kept["a"], kept["h"], kept["start"], back, kept["conv"], kept["stream"], kept["halo"], keep,
        wts.taps, wts.decay, wts.slope, wts.gates,
    )
    if end is not None:
        d_stream = end[1](d_stream)
    tail = (tail + shift_seq(head, -1)).astype(bf16)
    tokens = d_stream.shape[0] // streams
    d_stream = lax.dynamic_update_slice(
        d_stream.reshape(streams, tokens, -1), tail.reshape(REACH, streams, -1).transpose(1, 0, 2), (0, tokens - REACH, 0)
    ).reshape(d_stream.shape)
    part = (dot_t(d_branch, wts.gelu) + dot_t(d_stream, wts.stream)).astype(bf16).reshape(TP, -1, width)

    def full(v):
        lines = v.reshape(v.shape[0], -1, 1, HEAD_W)
        return jnp.where(lax.iota(jnp.int32, TP)[None, None, :, None] == w, lines, 0.0).reshape(v.shape[0], n * TP, -1)

    small = jnp.concatenate(
        [
            d_mix_gain.reshape(n * TP, rp), d_mlp_gain.reshape(n * TP, rp),
            full(d_taps).transpose(1, 0, 2).reshape(n * TP, -1), full(d_decay)[0],
        ],
        axis=1,
    ).astype(bf16)
    small = jnp.pad(small, ((0, 0), (0, (rp - gr) * HEAD_W - small.shape[1]))).reshape(n * TP, rp - gr, HEAD_W)
    gates = d_gates.reshape(-1, HEAD_W, 2, HEAD_W).transpose(2, 0, 1, 3).reshape(n * TP, gr, HEAD_W).astype(bf16)
    extra = jnp.concatenate([small, gates], axis=1).reshape(n, TP * rp, HEAD_W)
    grad_gelu = dot_tokens(kept["normed"], d_branch).reshape(n, TP * rp, -1)
    grad_stream = dot_tokens(kept["normed"], d_stream).reshape(n, TP * rp, -1)

    both = ScatterJob(
        jnp.concatenate([grad_gelu, grad_stream, extra], axis=2), False, lambda total: results.update(raw=total)
    )
    if end is None:
        part, results["wide"] = tie(part, results["wide"])
    pump.add(
        both,
        ScatterJob(grad_out.reshape(n, -1, width), True, lambda total: results.update(out=from_heads(total))),
    )
    d_normed = tp_scatter(pump.step(part))
    if end is None:
        d_normed = pump.step(d_normed)
    dv, d_gain = rms_norm_back(kept["x"], wts.mix_gain, d_normed)
    return d_x1 + dv, d_gain, both


def finish_both(raw, results, above, sizes):
    rp, gr, cp, fb = sizes
    width = raw.shape[1] - HEAD_W
    results["gates"] = from_heads(raw.reshape(TP, rp, -1)[:, rp - gr :, width:].reshape(TP * gr, HEAD_W))
    pieces = jnp.stack(wt_exchange(raw.astype(bf16).reshape(TP, rp, -1)))
    results["gelu"], results["stream"] = head_columns_back(pieces)
    sums = jnp.sum(pieces[:, : rp - gr, width:].astype(f32), axis=0).reshape(-1)
    above["mix_gain"], results["mlp_gain"] = sums[:rp], sums[rp : 2 * rp]
    results["taps"] = sums[2 * rp : 2 * rp + CONV * cp].reshape(CONV, cp)
    results["decay"] = sums[2 * rp + CONV * cp : 2 * rp + (CONV + 1) * cp]


def per_device(block_in, start_flags, out_grad, *shards):
    layers = shards[0].shape[0]
    micro, _, tokens, width = block_in.shape
    streams = micro * TP
    sizes = (shards[1].shape[1], shards[4].shape[1] // TP, shards[5].shape[1], shards[10].shape[1])
    rp = sizes[0]

    weights = [Weights(shards, layer) for layer in range(layers)]
    zero, pump = weights[0], Pump()
    zero.prepare_first()
    zero.prepare_out()
    pump.add(zero.first_job(), zero.out_job())
    rest = [w.shards for w in weights]
    block_in, start_flags, out_grad, rest = pump.step((block_in, start_flags, out_grad, rest))
    for w, shards_then in zip(weights, rest):
        w.shards = shards_then
    flags = tp_gather(start_flags[:, 0].astype(f32))
    x_in = block_in[:, 0].reshape(micro * tokens, width)
    grad = out_grad[:, 0].reshape(micro * tokens, width)
    x_all = tp_gather(x_in)
    keep = 1.0 - flags.T
    behind = 1.0 - shift_seq(flags[:, tokens - REACH :].T, 1)
    keep = jnp.concatenate([behind, keep, jnp.ones((REACH, streams), f32)]).reshape(-1, 1)
    keep = jnp.broadcast_to(keep, (keep.shape[0], HEAD_W))

    x = x_in.astype(f32)
    kept = []
    zero.prepare_wide()
    for _ in range(3):
        zero.wide_block = pump.step(zero.wide_block)
    zero.wide_block, x_all, rest = pump.step((zero.wide_block, x_all, [w.shards for w in weights]))
    pump.finish()
    zero.gather_wide()
    for w, shards_then in zip(weights, rest):
        w.shards = shards_then
    zero.gather_down()
    for wts in weights[1:]:
        wts.prepare_first()
        wts.prepare_out()
        wts.prepare_wide()
        wts.gather_wide()
        wts.gather_down()
    for layer in range(layers):
        wts = weights[layer]
        wts.open_first(sizes)
        normed = rms_norm(x_all.astype(f32), wts.mix_gain).astype(bf16) if layer == 0 else None
        following = weights[layer + 1] if layer < layers - 1 else None
        saved = forward_block(x, normed, keep, streams, wts, pump, following)
        if layer < layers - 1:
            x = pump.step(block_end(saved, wts))
            pump.finish()
        kept.append(saved)
        if layer == 0:
            grad_then, saved["wide"] = tie(grad, saved["wide"])
            g_down = tp_gather(grad_then)

    gx = grad.astype(f32)
    d_mix = jnp.zeros((width,), f32)
    results = [dict() for _ in range(layers)]
    spare, outcome, jobs = {}, [], []

    def last(ends):
        ends, kept[-1]["product"] = tie(ends, kept[-1]["product"])
        outcome.append(block_end(kept[-1], weights[-1]))
        return ends

    def settle(d_stream):
        d_stream, outcome[0] = tie(d_stream, outcome[0])
        return d_stream

    for layer in reversed(range(layers)):
        if layer != layers - 1:
            g_down = tp_gather(gx.astype(bf16))
            g_down, results[layer + 1]["down"] = tie(g_down, results[layer + 1]["down"])
        d_x1, d_mlp = mlp_back(
            gx, g_down, weights[layer], kept[layer], results[layer], rp, pump, results[layer + 1] if layer < layers - 1 else None
        )
        gx, d_mix, both = mixer_back(
            d_x1, keep, streams, weights[layer], kept[layer], d_mlp, d_mix, sizes, results[layer], pump, (last, settle) if layer == layers - 1 else None
        )
        jobs.append(both)
    pump.complete(jobs[:-1])
    held = [found.pop("raw") for found in results[1:]]
    wide = [found["wide"] for found in results[1:]]
    held, wide = pump.step(pump.step((held, wide)))
    for layer in range(1, layers):
        results[layer]["wide"] = wide[layer - 1]
    pump.finish()
    for layer in reversed(range(layers)):
        raw = held[layer - 1] if layer else results[0].pop("raw")
        finish_both(raw, results[layer], results[layer + 1] if layer < layers - 1 else spare, sizes)
    for found in results:
        pieces = wt_exchange(found.pop("wide").reshape(TP, rp, -1))
        found["gate"], found["up"] = ff_columns_back(jnp.stack(pieces))
    results[0]["mix_gain"] = vector_scatter(d_mix.reshape(-1, TP, rp))
    shape = (micro, 1, tokens, width)
    names = ("mix_gain", "gelu", "stream", "taps", "gates", "decay", "out", "mlp_gain", "gate", "up", "down")
    stacked = [jnp.stack([results[layer][k] for layer in range(layers)]) for k in names]
    return (outcome[0].astype(bf16).reshape(shape), gx.astype(bf16).reshape(shape), *stacked)


def solution(mesh):
    both = ("seq", "wt")
    tokens = P(None, "wt", "seq", None)
    vector, matrix = P(None, both), P(None, both, None)
    weights = (vector, matrix, matrix, P(None, None, both), matrix, vector, matrix, vector, matrix, matrix, matrix)
    return jax.shard_map(
        per_device,
        mesh=mesh,
        in_specs=(tokens, P(None, "wt", "seq"), tokens, *weights),
        out_specs=(tokens, tokens, *weights),
        check_vma=False,
    )
```
